128 devices in a mesh: batch: 16 (over x, z), seq: 8 (over y, core).
Axes of the slice: x: 4, y: 4, z: 4, core: 2. Of those that a mesh axis runs over, the one named last changes fastest.
Arguments:
- inputs: bfloat16 [16, 1024, 2048], P('batch', 'seq'), may hold values from -6 to 6
- positions: int32 [16, 1024], P('batch', 'seq'), may hold values from 0 to 1023, as said below
- w_qkv: bfloat16 [2048, 6144], P(('batch', 'seq')), may hold values from -0.1875 to 0.1875
- b_qkv: bfloat16 [6144], P(('batch', 'seq')), may hold values from -3 to 3
- w_out: bfloat16 [2048, 2048], P(('batch', 'seq')), may hold values from -0.5 to 0.5
- b_out: bfloat16 [2048], P(('batch', 'seq')), may hold values from -2 to 2
- w_up: bfloat16 [2048, 8192], P(('batch', 'seq')), may hold values from -0.125 to 0.125
- b_up: bfloat16 [8192], P(('batch', 'seq')), may hold values from -3 to 3
- w_down: bfloat16 [8192, 2048], P(('batch', 'seq')), may hold values from -0.0625 to 0.0625
- b_down: bfloat16 [2048], P(('batch', 'seq')), may hold values from -2 to 2
- gain_attn: bfloat16 [2048], P(('batch', 'seq')), may hold values from 0.099609375 to 1.8984375
- shift_attn: bfloat16 [2048], P(('batch', 'seq')), may hold values from -3 to 3
- gain_mlp: bfloat16 [2048], P(('batch', 'seq')), may hold values from 0.099609375 to 1.8984375
- shift_mlp: bfloat16 [2048], P(('batch', 'seq')), may hold values from -3 to 3
- grad_out: bfloat16 [16, 1024, 2048], P('batch', 'seq'), may hold values from -6 to 6
Outputs:
- layer_out: bfloat16 [16, 1024, 2048], P('batch', 'seq')
- grad_in: bfloat16 [16, 1024, 2048], P('batch', 'seq')
- grad_w_qkv: float32 [2048, 6144], P(('batch', 'seq'))
- grad_b_qkv: float32 [6144], P(('batch', 'seq'))
- grad_w_out: float32 [2048, 2048], P(('batch', 'seq'))
- grad_b_out: float32 [2048], P(('batch', 'seq'))
- grad_w_up: float32 [2048, 8192], P(('batch', 'seq'))
- grad_b_up: float32 [8192], P(('batch', 'seq'))
- grad_w_down: float32 [8192, 2048], P(('batch', 'seq'))
- grad_b_down: float32 [2048], P(('batch', 'seq'))
- grad_gain_attn: float32 [2048], P(('batch', 'seq'))
- grad_shift_attn: float32 [2048], P(('batch', 'seq'))
- grad_gain_mlp: float32 [2048], P(('batch', 'seq'))
- grad_shift_mlp: float32 [2048], P(('batch', 'seq'))
The draws below stay inside these ranges and needn't reach their ends.
Inputs may be any that keep to these rules, and one draw needn't show every extreme that they name: `positions`: in each sequence the first position is 0 and each later one is either 0 (a new document) or one more than the one before; some sequence has no restart.
All inputs are finite; a program needn't handle non-finite values.
Results may differ from the reference program's by a relative error of at most 0.015.
Values may be sent and summed in bfloat16 or wider, within the bound.
A program may use at most 512 MiB of HBM per device.

```python
import jax
import jax.numpy as jnp
from jax import lax

D = 2048
H = 16
HD = 128
ROT = 32
FF = 8192
SEQ_LEN = 1024
SEQUENCES = 16


def draw_positions(key, part):
    key = jax.random.fold_in(key, 7)
    reset_marks = jax.random.randint(key, (SEQUENCES, SEQ_LEN), 0, SEQ_LEN)
    position_idx = jnp.arange(SEQ_LEN, dtype=jnp.int32)[None, :]
    starts = jnp.where((reset_marks < 4) | (position_idx == 0), position_idx, 0)
    begins = lax.cummax(starts, axis=1)
    chosen = jax.random.randint(jax.random.fold_in(key, 1), (), 0, SEQUENCES)
    whole_row = jnp.arange(SEQUENCES, dtype=jnp.int32)[:, None] == chosen
    return jnp.where(whole_row, position_idx, position_idx - begins).astype(jnp.int32)


def spiked(values, rng, source, target, parts, factor):
    def block_of(dim):
        return (jnp.arange(values.shape[dim]) // (values.shape[dim] // parts)).reshape((-1,) + (1,) * (values.ndim - 1 - dim))

    near = jax.random.permutation(rng, parts)[block_of(target)]
    second = (block_of(target) + parts // 2) % parts
    return jnp.where((block_of(source) == near) | (block_of(source) == second), factor * values, values)


def levels(stream_key, shape, split, smallest, top_value):
    def one(position, blocks):
        steps = jax.random.uniform(jax.random.fold_in(jax.random.fold_in(stream_key, 6), position), (blocks,), jnp.float32, smallest / len(split), top_value / len(split))
        return jnp.repeat(jnp.exp(steps), shape[position] // blocks).reshape((-1,) + (1,) * (len(shape) - position - 1))

    gain = one(*split[0])
    for cut in split[1:]:
        gain = gain * one(*cut)
    return gain


def bell_draw(own_key, dims, scale, reach, split=(), kind=jnp.bfloat16):
    array = scale * jax.random.normal(own_key, dims, jnp.float32)
    if split:
        array = array * levels(own_key, dims, split, -0.22, 0.18)
    return jnp.clip(array, -reach, reach).astype(kind)


def heavy_noise(key, dims, spread, bound, split, heavy, held_as=jnp.bfloat16):
    values = spread * jax.random.normal(key, dims, jnp.float32)
    if split:
        values = values * levels(key, dims, split, -0.22, 0.18)
    return jnp.clip(spiked(values, jax.random.fold_in(key, 3), *heavy), -bound, bound).astype(held_as)


def setup_inputs(seed: int = 0) -> dict:
    key_list = jax.random.split(jax.random.key(seed), 16)
    inputs = bell_draw(key_list[0], (SEQUENCES, SEQ_LEN, D), 1.0, 6.0, ((0, 16), (1, 8)))
    positions = draw_positions(jax.random.fold_in(key_list[15], 71), 0)
    w_qkv = bell_draw(key_list[2], (D, 3 * D), (D // 2) ** -0.5, 0.1875, ((0, 128),))
    b_qkv = bell_draw(key_list[3], (3 * D,), 0.5, 3.0, ((0, 128),))
    w_out = bell_draw(key_list[4], (D, D), (D // 16) ** -0.5, 0.5, ((0, 128),))
    b_out = bell_draw(key_list[5], (D,), 0.3, 2.0, ((0, 128),))
    w_up = bell_draw(key_list[6], (D, FF), D ** -0.5, 0.125, ((0, 128),))
    b_up = bell_draw(key_list[7], (FF,), 0.5, 3.0, ((0, 128),))
    w_down = bell_draw(key_list[8], (FF, D), FF ** -0.5, 0.0625, ((0, 128),))
    b_down = bell_draw(key_list[9], (D,), 0.3, 2.0, ((0, 128),))
    gain_attn = jnp.clip(1.0 + 0.18 * jax.random.normal(key_list[10], (D,), jnp.float32), 0.099609375, 1.8984375).astype(jnp.bfloat16)
    shift_attn = bell_draw(key_list[11], (D,), 0.5, 3.0, ((0, 128),))
    gain_mlp = jnp.clip(1.0 + 0.18 * jax.random.normal(key_list[12], (D,), jnp.float32), 0.099609375, 1.8984375).astype(jnp.bfloat16)
    shift_mlp = bell_draw(key_list[13], (D,), 0.5, 3.0, ((0, 128),))
    grad_out = heavy_noise(key_list[14], (SEQUENCES, SEQ_LEN, D), 1.0, 6.0, ((0, 16), (1, 8)), (0, 2, 16, 2.0))
    return dict(inputs=inputs, positions=positions, w_qkv=w_qkv, b_qkv=b_qkv, w_out=w_out, b_out=b_out, w_up=w_up, b_up=b_up, w_down=w_down, b_down=b_down, gain_attn=gain_attn, shift_attn=shift_attn, gain_mlp=gain_mlp, shift_mlp=shift_mlp, grad_out=grad_out)


EPS = 1e-05
HIGH = lax.Precision.HIGHEST

@jax.custom_vjp
def low(v):
    return lax.optimization_barrier(v.astype(jnp.bfloat16)).astype(jnp.float32)

@jax.custom_vjp
def low_back(v):
    return v

def low_keep(v):
    return (low(v), None)

def low_pass(kept, grad):
    return (grad,)

def back_keep(v):
    return (v, None)

def back_low(kept, grad):
    return (low(grad),)
low.defvjp(low_keep, low_pass)
low_back.defvjp(back_keep, back_low)

def matmul_high(left, right):
    return jnp.dot(left, right, precision=HIGH)

def layer_norm(tensor, gain_vec, shift_vec):
    average = lax.optimization_barrier(jnp.mean(tensor, -1, keepdims=True))
    centred = tensor - average
    inverse = lax.rsqrt(lax.optimization_barrier(jnp.mean(centred * centred, -1, keepdims=True)) + EPS)
    return centred * inverse * gain_vec + shift_vec

def tables(positions):
    half_rot = ROT // 2
    exponent = jnp.arange(half_rot).astype(jnp.float32) / half_rot
    frequency = jnp.power(10000.0, -exponent)
    angles = positions.astype(jnp.float32)[..., None] * frequency
    return (jnp.cos(angles)[..., None, :], jnp.sin(angles)[..., None, :])

def rotate(tensor, cos_tab, sine_tab):
    half_rot = ROT // 2
    first_half = tensor[..., :half_rot]
    second_half = tensor[..., half_rot:ROT]
    return jnp.concatenate([first_half * cos_tab - second_half * sine_tab, second_half * cos_tab + first_half * sine_tab, tensor[..., ROT:]], -1)

def one_sequence(seq_x, seq_pos, w_qkv, b_qkv, w_out, b_out, w_up, b_up, w_down, b_down, gain_attn, shift_attn, gain_mlp, shift_mlp):
    length = seq_x.shape[0]
    first_in = low(layer_norm(seq_x, gain_attn, shift_attn))
    second_in = low(layer_norm(seq_x, gain_mlp, shift_mlp))
    qkv = low_back(matmul_high(first_in, w_qkv)) + b_qkv
    qkv = qkv.reshape(length, 3, H, HD)
    cos_tab, sine_tab = tables(seq_pos)
    queries = low(rotate(qkv[:, 0], cos_tab, sine_tab) * HD ** (-0.5))
    all_keys = low(rotate(qkv[:, 1], cos_tab, sine_tab))
    all_values = low(qkv[:, 2])
    scores = low_back(jnp.einsum('qhd,khd->hqk', queries, all_keys, precision=HIGH))
    token_idx = jnp.arange(length)
    visible = token_idx[:, None] >= token_idx[None, :]
    scores = jnp.where(visible[None], scores, -1e+30)
    peak_score = lax.optimization_barrier(jnp.max(scores, -1, keepdims=True))
    exponent = jnp.exp(scores - peak_score)
    probs = exponent / lax.optimization_barrier(jnp.sum(exponent, -1, keepdims=True))
    mixture = jnp.einsum('hqk,khd->qhd', low(probs), all_values, precision=HIGH)
    mixture = low(low_back(mixture)).reshape(length, D)
    attended = matmul_high(mixture, w_out) + b_out
    hidden = low_back(matmul_high(second_in, w_up)) + b_up
    active_low = low(jax.nn.gelu(hidden, approximate=False))
    fed_forward = matmul_high(active_low, w_down) + b_down
    return seq_x + attended + fed_forward

def reference(inputs, positions, w_qkv, b_qkv, w_out, b_out, w_up, b_up, w_down, b_down, gain_attn, shift_attn, gain_mlp, shift_mlp, grad_out):
    floats = [a.astype(jnp.float32) for a in (inputs, w_qkv, b_qkv, w_out, b_out, w_up, b_up, w_down, b_down, gain_attn, shift_attn, gain_mlp, shift_mlp)]
    checked = jax.checkpoint(one_sequence)

    def forward(xf, *params):

        def per_step(carried, entries):
            seq_x, seq_pos = entries
            return (carried, checked(seq_x, seq_pos, *params))
        _, result = lax.scan(per_step, jnp.zeros((), jnp.float32), (xf, positions))
        return result
    layer_out, pullback = jax.vjp(forward, *floats)
    grads = pullback(grad_out.astype(jnp.float32))
    return (layer_out.astype(jnp.bfloat16), grads[0].astype(jnp.bfloat16), grads[1], grads[2], grads[3], grads[4], grads[5], grads[6], grads[7], grads[8], grads[9], grads[10], grads[11], grads[12])
```

```python
from functools import partial

import jax
import jax.numpy as jnp
from jax import lax
from jax.sharding import PartitionSpec as P

H = 16
HD = 128
ROT = 32
EPS = 1e-05
F32 = jnp.float32
BF16 = jnp.bfloat16


def tables(positions):
    half_rot = ROT // 2
    exponent = jnp.arange(half_rot).astype(F32) / half_rot
    frequency = jnp.power(10000.0, -exponent)
    angles = positions.astype(F32)[..., None] * frequency
    return (jnp.cos(angles)[..., None, :], jnp.sin(angles)[..., None, :])


def rotate(tensor, cos_tab, sine_tab):
    half_rot = ROT // 2
    first_half = tensor[..., :half_rot]
    second_half = tensor[..., half_rot:ROT]
    return jnp.concatenate(
        [
            first_half * cos_tab - second_half * sine_tab,
            second_half * cos_tab + first_half * sine_tab,
            tensor[..., ROT:],
        ],
        -1,
    )


def over_rows(left, right):
    return lax.dot_general(
        left, right, (((0,), (0,)), ((), ())), preferred_element_type=F32
    )


def against(left, right):
    return lax.dot_general(
        left, right, (((1,), (1,)), ((), ())), preferred_element_type=F32
    )


def plain(left, right):
    return jnp.dot(left, right, preferred_element_type=F32)


def norm_stats(rows):
    average = jnp.mean(rows, -1, keepdims=True)
    centred = rows - average
    inverse = lax.rsqrt(jnp.mean(centred * centred, -1, keepdims=True) + EPS)
    return centred * inverse, inverse


def shards(
    inputs,
    positions,
    w_qkv,
    b_qkv,
    w_out,
    b_out,
    w_up,
    b_up,
    w_down,
    b_down,
    gain_attn,
    shift_attn,
    gain_mlp,
    shift_mlp,
    grad_out,
):
    _, block_len, width = inputs.shape
    groups = lax.axis_size("batch")
    parts = lax.axis_size("seq")
    every = ("batch", "seq")
    me = lax.axis_index("seq")
    heads = H // parts
    length = block_len * parts
    scaling = HD ** (-0.5)

    x_local = inputs[0]
    g_local = grad_out[0]
    x_rows = lax.all_gather(x_local, "seq", axis=0, tiled=True)
    g_rows = lax.all_gather(g_local, "seq", axis=0, tiled=True)
    pos_rows = lax.all_gather(positions[0], "seq", axis=0, tiled=True)

    small = jnp.concatenate(
        [b_out, b_down, gain_attn, shift_attn, gain_mlp, shift_mlp, b_qkv]
    )
    small = lax.all_gather(small, every, axis=0, tiled=False).astype(F32)
    rows16 = b_out.shape[0]
    b_out_f, b_down_f, gain_a, shift_a, gain_m, shift_m = [
        small[:, i * rows16 : (i + 1) * rows16].reshape(-1) for i in range(6)
    ]
    b_qkv_f = small[:, 6 * rows16 :].reshape(3, parts, heads * HD)
    b_qkv_f = lax.dynamic_index_in_dim(b_qkv_f, me, 1, keepdims=False).reshape(-1)
    b_up_f = lax.all_gather(b_up, "batch", axis=0, tiled=True).astype(F32)

    unit = b_up.shape[0]
    w_up_t = w_up.reshape(-1, groups, parts, unit)
    w_up_t = lax.all_to_all(w_up_t, "seq", split_axis=2, concat_axis=0, tiled=True)
    w_up_t = w_up_t.reshape(-1, groups * unit)
    w_up_f = lax.all_gather(w_up_t, "batch", axis=0, tiled=True)
    w_down_f = lax.all_gather(w_down, "batch", axis=0, tiled=True)
    w_qkv_t = w_qkv.reshape(-1, 3, parts, heads * HD)
    w_qkv_t = lax.all_to_all(w_qkv_t, "seq", split_axis=2, concat_axis=0, tiled=True)
    w_qkv_t = w_qkv_t.reshape(-1, 3 * heads * HD)
    w_qkv_f = lax.all_gather(w_qkv_t, "batch", axis=0, tiled=True)
    there = [
        (b * parts + s, ((b % heads) * parts + s) * parts + b // heads)
        for b in range(groups)
        for s in range(parts)
    ]
    w_out_t = lax.ppermute(w_out, every, there)
    w_out_f = lax.all_gather(w_out_t, "batch", axis=0, tiled=True)

    normed, _ = norm_stats(x_rows.astype(F32))
    first_in = (normed * gain_a + shift_a).astype(BF16)
    second_in = (normed * gain_m + shift_m).astype(BF16)

    hidden = plain(second_in, w_up_f) + b_up_f
    active, gelu_pull = jax.vjp(partial(jax.nn.gelu, approximate=False), hidden)
    active_low = active.astype(BF16)
    grad_active = against(g_rows, w_down_f)
    (grad_hidden,) = gelu_pull(grad_active)
    grad_b_up = jnp.sum(grad_hidden, 0)
    grad_hidden_low = grad_hidden.astype(BF16)
    grad_w_down = over_rows(active_low, g_rows).astype(BF16)
    grad_w_down = lax.psum_scatter(grad_w_down, "batch", scatter_dimension=0, tiled=True)
    grad_w_up = over_rows(second_in, grad_hidden_low).astype(BF16)
    grad_w_up = lax.psum_scatter(grad_w_up, "batch", scatter_dimension=0, tiled=True)
    fed_forward = plain(active_low, w_down_f)
    grad_second = against(grad_hidden_low, w_up_f)

    qkv = (plain(first_in, w_qkv_f) + b_qkv_f).reshape(length, 3, heads, HD)
    cos_tab, sine_tab = tables(pos_rows)
    queries = (rotate(qkv[:, 0], cos_tab, sine_tab) * scaling).astype(BF16)
    keys = rotate(qkv[:, 1], cos_tab, sine_tab).astype(BF16)
    values = qkv[:, 2].astype(BF16)
    token = jnp.arange(length)
    visible = token[:, None] >= token[None, :]
    scores = jnp.einsum("qhd,khd->hqk", queries, keys, preferred_element_type=F32)
    scores = jnp.where(visible, scores, -1e30)
    exponent = jnp.exp(scores - jnp.max(scores, -1, keepdims=True))
    probs = exponent / jnp.sum(exponent, -1, keepdims=True)
    probs_low = probs.astype(BF16)
    mixture = jnp.einsum("hqk,khd->qhd", probs_low, values, preferred_element_type=F32)
    mixture = mixture.reshape(length, -1).astype(BF16)
    grad_w_out = over_rows(mixture, g_rows).astype(BF16)
    grad_w_out = lax.psum_scatter(grad_w_out, "batch", scatter_dimension=0, tiled=True)
    attended = plain(mixture, w_out_f)
    grad_mixture = against(g_rows, w_out_f).astype(BF16).reshape(length, heads, HD)
    grad_probs = jnp.einsum("qhd,khd->hqk", grad_mixture, values, preferred_element_type=F32)
    row_delta = jnp.sum(probs * grad_probs, -1, keepdims=True)
    grad_scores = (probs * (grad_probs - row_delta)).astype(BF16)
    grad_query = (
        jnp.einsum("hqk,khd->qhd", grad_scores, keys, preferred_element_type=F32) * scaling
    )
    grad_key = jnp.einsum("hqk,qhd->khd", grad_scores, queries, preferred_element_type=F32)
    grad_value = jnp.einsum("hqk,qhd->khd", probs_low, grad_mixture, preferred_element_type=F32)
    grad_qkv = jnp.stack(
        [
            rotate(grad_query, cos_tab, -sine_tab),
            rotate(grad_key, cos_tab, -sine_tab),
            grad_value,
        ],
        1,
    ).reshape(length, -1)
    grad_b_qkv = jnp.sum(grad_qkv, 0)
    grad_qkv_low = grad_qkv.astype(BF16)
    grad_w_qkv = over_rows(first_in, grad_qkv_low).astype(BF16)
    grad_w_qkv = lax.psum_scatter(grad_w_qkv, "batch", scatter_dimension=0, tiled=True)
    grad_first = against(grad_qkv_low, w_qkv_f)

    summed = (attended + fed_forward).astype(BF16)
    summed = lax.psum_scatter(summed, "seq", scatter_dimension=0, tiled=True)
    x_f = x_local.astype(F32)
    layer_out = (x_f + summed.astype(F32) + (b_out_f + b_down_f)).astype(BF16)

    back = (grad_first * gain_a + grad_second * gain_m).astype(BF16)
    back = lax.psum_scatter(back, "seq", scatter_dimension=0, tiled=True).astype(F32)
    n_local, r_local = norm_stats(x_f)
    back = r_local * (
        back
        - jnp.mean(back, -1, keepdims=True)
        - n_local * jnp.mean(back * n_local, -1, keepdims=True)
    )
    g_f = g_local.astype(F32)
    grad_in = (g_f + back).astype(BF16)

    grad_w_up = grad_w_up.reshape(parts, -1, groups, 1, unit)
    grad_w_up = lax.all_to_all(grad_w_up, "seq", split_axis=0, concat_axis=3, tiled=True)
    grad_w_up = grad_w_up.reshape(w_up.shape).astype(F32)
    grad_w_qkv = grad_w_qkv.reshape(parts, -1, 3, 1, heads * HD)
    grad_w_qkv = lax.all_to_all(grad_w_qkv, "seq", split_axis=0, concat_axis=3, tiled=True)
    grad_w_qkv = grad_w_qkv.reshape(w_qkv.shape).astype(F32)
    grad_w_out = lax.ppermute(grad_w_out, every, [(d, s) for s, d in there]).astype(F32)

    spread_qkv = jnp.zeros((3, parts, heads * HD), F32)
    spread_qkv = lax.dynamic_update_index_in_dim(
        spread_qkv, grad_b_qkv.reshape(3, 1, -1), me, 1
    )
    spread_up = jnp.zeros((groups, parts, unit), F32)
    spread_up = lax.dynamic_update_index_in_dim(
        spread_up, grad_b_up.reshape(groups, 1, unit), me, 1
    )
    count = groups * parts
    packed = [
        jnp.sum(g_f, 0),
        jnp.sum(grad_first * normed, 0),
        jnp.sum(grad_first, 0),
        jnp.sum(grad_second * normed, 0),
        jnp.sum(grad_second, 0),
        spread_qkv,
        spread_up,
    ]
    packed = jnp.concatenate([p.reshape(count, -1) for p in packed], 1)
    packed = lax.psum_scatter(packed, every, scatter_dimension=0, tiled=True).reshape(-1)
    pieces = [packed[i * rows16 : (i + 1) * rows16] for i in range(5)]
    out_b_qkv = packed[5 * rows16 : 5 * rows16 + b_qkv.shape[0]]
    out_b_up = packed[5 * rows16 + b_qkv.shape[0] :]
    return (
        layer_out[None],
        grad_in[None],
        grad_w_qkv,
        out_b_qkv,
        grad_w_out,
        pieces[0],
        grad_w_up,
        out_b_up,
        grad_w_down.astype(F32),
        pieces[0],
        pieces[1],
        pieces[2],
        pieces[3],
        pieces[4],
    )


def solution(mesh):
    both = ("batch", "seq")
    rows = P("batch", "seq", None)
    matrix = P(both, None)
    vector = P(both)
    return jax.shard_map(
        shards,
        mesh=mesh,
        in_specs=(
            rows,
            P("batch", "seq"),
            matrix,
            vector,
            matrix,
            vector,
            matrix,
            vector,
            matrix,
            vector,
            vector,
            vector,
            vector,
            vector,
            rows,
        ),
        out_specs=(
            rows,
            rows,
            matrix,
            vector,
            matrix,
            vector,
            matrix,
            vector,
            matrix,
            vector,
            vector,
            vector,
            vector,
            vector,
        ),
        check_vma=False,
    )
```

```python
import functools

import jax
import jax.numpy as jnp
from jax import lax
from jax.experimental import pallas as pl
from jax.experimental.pallas import tpu as pltpu
from jax.sharding import PartitionSpec as P

H = 16
HD = 128
ROT = 32
EPS = 1e-05
F32 = jnp.float32
BF16 = jnp.bfloat16
MESH = pl.DeviceIdType.MESH
STEPS = (1, -1, 2)
SEQ_PEERS = [(dy, dc) for dc in (1, 0) for dy in (0, 1, -1, 2) if (dy, dc) != (0, 0)]


def place():
    b = lax.axis_index("batch")
    s = lax.axis_index("seq")
    return b // 4, b % 4, s // 2, s % 2


def shifted(x=0, z=0, y=0, c=0):
    px, pz, py, pc = place()
    px = lax.rem(px + x + 4, 4)
    pz = lax.rem(pz + z + 4, 4)
    py = lax.rem(py + y + 4, 4)
    pc = lax.rem(pc + c, 2)
    return (px * 4 + pz, py * 2 + pc)


def moved(pos, step):
    return lax.rem(pos + step + 4, 4)


class Copies:
    def __init__(self, send, recv):
        self.send, self.recv, self.count, self.made = send, recv, 0, []

    def make(self, src, dst, device):
        k = self.count
        self.count += 1
        return pltpu.make_async_remote_copy(
            src_ref=src,
            dst_ref=dst,
            send_sem=self.send.at[k],
            recv_sem=self.recv.at[k],
            device_id=device,
            device_id_type=MESH,
        )

    def start(self, src, dst, device):
        copy = self.make(src, dst, device)
        copy.start()
        self.made.append(copy)
        return copy

    def drain(self):
        for copy in self.made:
            copy.wait_send()


class Locals:
    def __init__(self, sems):
        self.sems, self.count = sems, 0

    def start(self, src, dst):
        copy = pltpu.make_async_copy(src, dst, self.sems.at[self.count])
        self.count += 1
        copy.start()
        return copy


def greet(extra=None):
    barrier = pltpu.get_barrier_semaphore()
    peers = [dict(x=d) for d in STEPS] + [dict(z=d) for d in STEPS]
    peers += [dict(y=dy, c=dc) for dy, dc in SEQ_PEERS]
    for p in peers:
        pl.semaphore_signal(barrier, inc=1, device_id=shifted(**p), device_id_type=MESH)
    count = len(peers)
    if extra is not None:
        differs, source = extra

        @pl.when(differs)
        def _():
            pl.semaphore_signal(barrier, inc=1, device_id=source, device_id_type=MESH)

        count = jnp.where(differs, count + 1, count)
    pl.semaphore_wait(barrier, count)


def group(buf, first, at, half=None, rows=None):
    span = pl.ds(0, 4) if half is None else pl.ds(2 * half, 2)
    index = (span, at) if first == "x" else (at, span)
    if rows is not None:
        index += (pl.ds(*rows),)
    return buf.at[index]


class Gather:
    def __init__(self, copies, buf, first, rows=None):
        self.copies, self.buf, self.first, self.rows = copies, buf, first, rows
        self.other = "z" if first == "x" else "x"
        x, z, _, _ = place()
        self.at = z if first == "x" else x
        self.own = buf.at[x, z] if rows is None else buf.at[x, z, pl.ds(*rows)]

    def part(self, step, half=None):
        return group(self.buf, self.first, moved(self.at, step), half, self.rows)

    def one(self, src=None):
        src = self.own if src is None else src
        self.sent = [self.copies.start(src, self.own, shifted(**{self.first: d})) for d in STEPS]

    def two(self):
        for c in self.sent:
            c.wait_recv()
        mine = self.part(0)
        self.sent = [self.copies.start(mine, mine, shifted(**{self.other: d})) for d in (1, -1)]

    def three(self):
        sent = []
        for c, d, half in zip(self.sent, (1, -1), (0, 1)):
            c.wait_recv()
            passed = self.part(-d, half)
            sent.append(self.copies.start(passed, passed, shifted(**{self.other: d})))
        self.sent = sent

    def done(self):
        for c in self.sent:
            c.wait_recv()


def out_route(groups=16, parts=8, heads=2):
    b = lax.axis_index("batch")
    s = lax.axis_index("seq")
    to = ((b % heads) * parts + s, b // heads)
    source = (s * heads + b // parts, b % parts)
    differs = jnp.logical_or(to[0] != b, to[1] != s)
    return to, source, differs


def gather_kernel(x_ref, g_ref, small_ref, up_ref, qkv_ref, down_ref, out_ref,
                  X, G, SM, UP, QK, DN, WO, send, recv):
    copies = Copies(send, recv)
    x, z, y, c = place()
    s = y * 2 + c
    to, source, differs = out_route()
    greet((differs, source))

    def across(src, dst):
        dst[...] = src[s]
        return [
            copies.start(src.at[moved(y, dy) * 2 + lax.rem(c + dc, 2)], dst, shifted(y=dy, c=dc))
            for dy, dc in SEQ_PEERS
        ]

    SM[x, z, s] = small_ref[...]
    sm = [copies.start(small_ref, SM.at[x, z, s], shifted(y=dy, c=dc)) for dy, dc in SEQ_PEERS]
    up = across(up_ref, UP.at[x, z, pl.ds(s * 16, 16)])
    down = Gather(copies, DN, "x")
    down.one(down_ref)
    DN[x, z] = down_ref[...]
    def seq_one(src, dst):
        dst[s] = src[...]
        return [copies.start(src, dst.at[s], shifted(y=d)) for d in (1, -1)] + [
            copies.start(src, dst.at[s], shifted(c=1))
        ]

    xs = seq_one(x_ref, X)
    qk = across(qkv_ref, QK.at[x, z, pl.ds(s * 16, 16)])
    out_copy = copies.make(out_ref, WO.at[to[0] // 4, to[0] % 4], to)

    @pl.when(differs)
    def _():
        out_copy.start()

    @pl.when(jnp.logical_not(differs))
    def _():
        WO[x, z] = out_ref[...]

    gs = seq_one(g_ref, G)

    for cp in sm:
        cp.wait_recv()
    small = Gather(copies, SM, "z")
    small.one()
    for cp in up:
        cp.wait_recv()
    upg = Gather(copies, UP, "z")
    upg.one()
    small.two()
    down.two()

    def seq_two(sent, dst):
        more = []
        for cp, d in zip(sent[:2], (1, -1)):
            cp.wait_recv()
            got = dst.at[moved(y, -d) * 2 + c]
            more.append(copies.start(got, got, shifted(c=1)))
        up_way = c == 0
        got = dst.at[jnp.where(up_way, moved(y, -1), moved(y, 1)) * 2 + c]
        py = jnp.where(up_way, moved(y, 1), moved(y, -1))
        b = lax.axis_index("batch")
        fwd = copies.start(got, got, (b, py * 2 + c))
        sent[2].wait_recv()
        return more, fwd

    xs2, xf = seq_two(xs, X)
    small.three()
    for cp in qk:
        cp.wait_recv()
    qa = Gather(copies, QK, "x", (0, 64))
    qb = Gather(copies, QK, "z", (64, 64))
    qa.one()
    qb.one()

    @pl.when(differs)
    def _():
        out_copy.wait_recv()
        out_copy.wait_send()

    wo = Gather(copies, WO, "x")
    wo.one()
    gs2, gf = seq_two(gs, G)
    upg.two()

    def seq_three(more, fwd, dst):
        fwd.wait_recv()
        got = dst.at[moved(y, 2) * 2 + c]
        last = copies.start(got, got, shifted(c=1))
        return more + [last]

    xs3 = seq_three(xs2, xf, X)
    down.three()
    qa.two()
    qb.two()
    wo.two()
    upg.three()
    gs3 = seq_three(gs2, gf, G)
    small.done()
    for cp in xs3 + gs3:
        cp.wait_recv()
    qa.three()
    qb.three()
    wo.three()
    for gth in (down, upg, qa, qb, wo):
        gth.done()
    copies.drain()


def gather(x, g, small, up, qkv, down, out):
    vm = pl.BlockSpec(memory_space=pltpu.VMEM)
    shapes = [
        ((8,) + x.shape, BF16), ((8,) + g.shape, BF16), ((4, 4, 8) + small.shape, small.dtype),
        ((4, 4, 128, up.shape[-1]), BF16), ((4, 4, 128, qkv.shape[-1]), BF16),
        ((4, 4) + down.shape, BF16), ((4, 4) + out.shape, BF16),
    ]
    return pl.pallas_call(
        gather_kernel,
        out_shape=[jax.ShapeDtypeStruct(*s) for s in shapes],
        in_specs=[vm] * 7,
        out_specs=[vm] * 7,
        scratch_shapes=[pltpu.SemaphoreType.DMA((96,)), pltpu.SemaphoreType.DMA((96,))],
        compiler_params=pltpu.CompilerParams(
            collective_id=1, has_side_effects=True, vmem_limit_bytes=60 * 2**20
        ),
    )(x, g, small, up, qkv, down, out)


class Scatter:
    def __init__(self, copies, local, buf, first, own, land, last, rows=None):
        self.copies, self.buf, self.first, self.rows = copies, buf, first, rows
        self.own, self.land, self.last = own, land, last
        self.other = "z" if first == "x" else "x"
        x, z, _, _ = place()
        self.at, self.mine = (z, x) if first == "x" else (x, z)
        self.local = local

    def one(self):
        self.sent = [
            self.copies.start(
                group(self.buf, self.first, moved(self.at, d), None, self.rows),
                self.land.at[k],
                shifted(**{self.other: d}),
            )
            for k, d in enumerate(STEPS)
        ]
        self.kept = self.local.start(group(self.buf, self.first, self.at, None, self.rows), self.own)

    def two(self):
        self.kept.wait()
        for c in self.sent:
            c.wait_recv()
        own, land = self.own, self.land
        rows = own.shape[1]
        step = min(rows, 16)

        def add(t, _):
            i = t // (rows // step)
            r = pl.ds(pl.multiple_of(t % (rows // step) * step, step), step)
            total = own[i, r].astype(F32) + land[0, i, r].astype(F32)
            total += land[1, i, r].astype(F32) + land[2, i, r].astype(F32)
            own[i, r] = total.astype(own.dtype)
            return 0

        lax.fori_loop(0, 4 * (rows // step), add, 0)
        self.sent = [
            self.copies.start(
                own.at[moved(self.mine, d)], self.last.at[k], shifted(**{self.first: d})
            )
            for k, d in enumerate(STEPS)
        ]

    def three(self, put):
        for c in self.sent:
            c.wait_recv()
        own, last = self.own, self.last
        rows = own.shape[1]
        step = min(rows, 16)

        def add(t, _):
            at = pl.multiple_of(t * step, step)
            r = pl.ds(at, step)
            total = own[self.mine, r].astype(F32) + last[0, r].astype(F32)
            total += last[1, r].astype(F32) + last[2, r].astype(F32)
            put(at, step, total)
            return 0

        lax.fori_loop(0, rows // step, add, 0)


class SeqScatter:
    def __init__(self, copies, local, buf, own, pair, last):
        self.copies, self.local, self.buf = copies, local, buf
        self.own, self.pair, self.last = own, pair, last

    def one(self):
        _, _, _, c = place()
        self.sent = self.copies.start(self.buf.at[:, 1 - c], self.pair, shifted(c=1))
        self.kept = self.local.start(self.buf.at[:, c], self.own)

    def two(self):
        _, _, y, _ = place()
        self.kept.wait()
        self.sent.wait_recv()
        own, pair = self.own, self.pair

        def add(t, _):
            r = pl.ds(pl.multiple_of(t % 8 * 16, 16), 16)
            i = t // 8
            own[i, r] = (own[i, r].astype(F32) + pair[i, r].astype(F32)).astype(BF16)
            return 0

        lax.fori_loop(0, 32, add, 0)
        self.sent = [
            self.copies.start(own.at[moved(y, d)], self.last.at[k], shifted(y=d))
            for k, d in enumerate(STEPS)
        ]

    def three(self, put):
        _, _, y, _ = place()
        for c in self.sent:
            c.wait_recv()
        own, last = self.own, self.last

        def add(t, _):
            at = pl.multiple_of(t * 16, 16)
            r = pl.ds(at, 16)
            total = own[y, r].astype(F32) + last[0, r].astype(F32)
            total += last[1, r].astype(F32) + last[2, r].astype(F32)
            put(at, 16, total)
            return 0

        lax.fori_loop(0, 8, add, 0)


def scatter_kernel(P, Q, GD, GU, GQ, GO, V1, V2,
                   sp, sq, gd, gu, gq, go, sv,
                   p_own, p_pair, p_last, q_own, q_pair, q_last,
                   d_own, d_land, d_last, u_own, u_land, u_last,
                   a_own, a_land, a_last, b_own, b_land, b_last,
                   o_own, o_land, o_last, v_land, C, c_own, c_land, c_last,
                   gu_part, gq_part, go_part,
                   send, recv, loc):
    copies, local = Copies(send, recv), Locals(loc)
    x, z, y, c = place()
    s = y * 2 + c
    to, source, differs = out_route()
    greet((differs, to))
    fp = SeqScatter(copies, local, P, p_own, p_pair, p_last)
    fq = SeqScatter(copies, local, Q, q_own, q_pair, q_last)
    sd = Scatter(copies, local, GD, "x", d_own, d_land, d_last)
    su = Scatter(copies, local, GU, "z", u_own, u_land, u_last)
    sa = Scatter(copies, local, GQ, "x", a_own, a_land, a_last, (0, 64))
    sb = Scatter(copies, local, GQ, "z", b_own, b_land, b_last, (64, 64))
    so = Scatter(copies, local, GO, "x", o_own, o_land, o_last)
    sc = Scatter(copies, local, C, "z", c_own, c_land, c_last)
    vs = [
        copies.start(V1.at[moved(y, dy) * 2 + lax.rem(c + dc, 2)], v_land.at[k], shifted(y=dy, c=dc))
        for k, (dy, dc) in enumerate(SEQ_PEERS)
    ]
    fp.one()
    su.one()
    sd.one()
    fq.one()
    sa.one()
    sb.one()
    so.one()
    fp.two()
    fq.two()
    for cp in vs:
        cp.wait_recv()
    w = V1[s]
    for k in range(7):
        w = w + v_land[k]
    for i in range(4):
        for j in range(4):
            r = i * 4 + j
            C[i, j, 0:1, :] = w[r : r + 1]
            C[i, j, 1:2, :] = V2[r : r + 1, :]
    sc.one()
    su.two()
    sd.two()
    sa.two()
    sb.two()
    so.two()
    sc.two()

    def store(ref):
        def put(at, n, total):
            ref[pl.ds(at, n)] = total.astype(ref.dtype)

        return put

    su.three(store(gu_part))

    def back(part, out):
        out[s] = part[pl.ds(pl.multiple_of(s * 16, 16), 16)]
        made = []
        for dy, dc in SEQ_PEERS:
            peer = moved(y, dy) * 2 + lax.rem(c + dc, 2)
            made.append(
                copies.start(
                    part.at[pl.ds(pl.multiple_of(peer * 16, 16), 16)], out.at[s], shifted(y=dy, c=dc)
                )
            )
        return made

    backs = back(gu_part, gu)
    sd.three(store(gd))
    fp.three(store(sp))
    fq.three(store(sq))
    sa.three(store(gq_part))
    sb.three(lambda at, n, total: store(gq_part)(at + 64, n, total))
    backs += back(gq_part, gq)
    so.three(store(go_part))
    out_copy = copies.make(go_part, go, source)

    @pl.when(differs)
    def _():
        out_copy.start()

    @pl.when(jnp.logical_not(differs))
    def _():
        go[...] = go_part[...]

    sc.three(store(sv))

    @pl.when(differs)
    def _():
        out_copy.wait()

    for cp in backs:
        cp.wait_recv()
    copies.drain()


def scatter(P, Q, GD, GU, GQ, GO, V1, V2):
    any_ = pl.BlockSpec(memory_space=pl.ANY)
    vm = pl.BlockSpec(memory_space=pltpu.VMEM)
    n_d, n_u, n_q, n_o = GD.shape[3], GU.shape[3], GQ.shape[3], GO.shape[3]
    S = pltpu.VMEM

    def set_of(rows, cols, kind=BF16):
        return [S((4, rows, cols), kind), S((3, 4, rows, cols), kind), S((3, rows, cols), kind)]

    seq = [S((4, 128, 2048), BF16), S((4, 128, 2048), BF16), S((3, 128, 2048), BF16)]
    return pl.pallas_call(
        scatter_kernel,
        out_shape=[
            jax.ShapeDtypeStruct((128, 2048), F32), jax.ShapeDtypeStruct((128, 2048), F32),
            jax.ShapeDtypeStruct((64, n_d), F32), jax.ShapeDtypeStruct((8, 16, n_u), BF16),
            jax.ShapeDtypeStruct((8, 16, n_q), BF16), jax.ShapeDtypeStruct((16, n_o), BF16),
            jax.ShapeDtypeStruct((8, 128), F32),
        ],
        in_specs=[any_] * 6 + [vm] * 2,
        out_specs=[vm] * 7,
        scratch_shapes=seq + seq + set_of(64, n_d) + set_of(128, n_u) + set_of(64, n_q) + set_of(64, n_q)
        + set_of(16, n_o) + [S((7, 16, 128), F32), S((4, 4, 8, 128), F32)] + set_of(8, 128, F32)
        + [S((128, n_u), BF16), S((128, n_q), BF16), S((16, n_o), BF16),
           pltpu.SemaphoreType.DMA((80,)), pltpu.SemaphoreType.DMA((80,)), pltpu.SemaphoreType.DMA((12,))],
        compiler_params=pltpu.CompilerParams(collective_id=2, has_side_effects=True, vmem_limit_bytes=60 * 2**20),
    )(P, Q, GD, GU, GQ, GO, V1, V2)


def tables(positions):
    half_rot = ROT // 2
    exponent = jnp.arange(half_rot).astype(F32) / half_rot
    frequency = jnp.power(10000.0, -exponent)
    angles = positions.astype(F32)[..., None] * frequency
    return (jnp.cos(angles)[..., None, :], jnp.sin(angles)[..., None, :])


def rotate(tensor, cos_tab, sine_tab):
    half_rot = ROT // 2
    first_half = tensor[..., :half_rot]
    second_half = tensor[..., half_rot:ROT]
    return jnp.concatenate(
        [
            first_half * cos_tab - second_half * sine_tab,
            second_half * cos_tab + first_half * sine_tab,
            tensor[..., ROT:],
        ],
        -1,
    )


def over_rows(left, right):
    return lax.dot_general(
        left, right, (((0,), (0,)), ((), ())), preferred_element_type=F32
    )


def against(left, right):
    return lax.dot_general(
        left, right, (((1,), (1,)), ((), ())), preferred_element_type=F32
    )


def plain(left, right):
    return jnp.dot(left, right, preferred_element_type=F32)


def norm_stats(rows):
    average = jnp.mean(rows, -1, keepdims=True)
    centred = rows - average
    inverse = lax.rsqrt(jnp.mean(centred * centred, -1, keepdims=True) + EPS)
    return centred * inverse, inverse


def shards(
    inputs,
    positions,
    w_qkv,
    b_qkv,
    w_out,
    b_out,
    w_up,
    b_up,
    w_down,
    b_down,
    gain_attn,
    shift_attn,
    gain_mlp,
    shift_mlp,
    grad_out,
):
    _, block_len, width = inputs.shape
    groups = lax.axis_size("batch")
    parts = lax.axis_size("seq")
    me = lax.axis_index("seq")
    b_me = lax.axis_index("batch")
    heads = H // parts
    length = block_len * parts
    scaling = HD ** (-0.5)
    x_local = inputs[0]
    g_local = grad_out[0]
    unit = b_up.shape[0]
    cut = b_qkv.shape[0]
    rows16 = b_out.shape[0]

    spot = positions[0]
    small = jnp.concatenate(
        [b_out, b_down, gain_attn, shift_attn, gain_mlp, shift_mlp, b_qkv, b_up]
        + [(spot // 32).astype(BF16), (spot % 32).astype(BF16)]
    )
    filled = small.shape[0]
    small = jnp.pad(small, (0, 2048 - filled)).reshape(16, 128)
    up_cut = w_up.reshape(-1, groups, parts, unit).transpose(2, 0, 1, 3).reshape(parts, -1, groups * unit)
    qkv_cut = w_qkv.reshape(-1, 3, parts, heads * HD).transpose(2, 0, 1, 3).reshape(parts, -1, 3 * heads * HD)
    X, G, SM, UP, QK, DN, WO = gather(x_local, g_local, small, up_cut, qkv_cut, w_down, w_out)
    x_rows = X.reshape(length, width)
    g_rows = G.reshape(length, width)
    w_up_f = UP.reshape(width, -1)
    w_qkv_f = QK.reshape(width, -1)
    w_down_f = DN.reshape(-1, width)
    w_out_f = WO.reshape(-1, width)
    small = SM.reshape(groups, parts, 2048)[:, :, :filled].astype(F32)
    b_out_f, b_down_f, gain_a, shift_a, gain_m, shift_m = [
        small[:, :, i * rows16 : (i + 1) * rows16].reshape(-1) for i in range(6)
    ]
    at = 6 * rows16
    b_qkv_f = small[:, :, at : at + cut].reshape(3, parts, heads * HD)
    b_qkv_f = lax.dynamic_index_in_dim(b_qkv_f, me, 1, keepdims=False).reshape(-1)
    at += cut
    b_up_f = lax.dynamic_index_in_dim(small[:, :, at : at + unit], me, 1, keepdims=False).reshape(-1)
    at += unit
    digits = lax.dynamic_index_in_dim(small[:, :, at:], b_me, 0, keepdims=False)
    pos_rows = (32.0 * digits[:, :block_len] + digits[:, block_len:]).reshape(-1)

    normed, _ = norm_stats(x_rows.astype(F32))
    first_in = (normed * gain_a + shift_a).astype(BF16)
    second_in = (normed * gain_m + shift_m).astype(BF16)

    hidden = plain(second_in, w_up_f) + b_up_f
    active, gelu_pull = jax.vjp(functools.partial(jax.nn.gelu, approximate=False), hidden)
    active_low = active.astype(BF16)
    grad_active = against(g_rows, w_down_f)
    (grad_hidden,) = gelu_pull(grad_active)
    grad_b_up = jnp.sum(grad_hidden, 0)
    grad_hidden_low = grad_hidden.astype(BF16)
    grad_w_down = over_rows(active_low, g_rows).astype(BF16)
    grad_w_up = over_rows(second_in, grad_hidden_low).astype(BF16)
    fed_forward = plain(active_low, w_down_f)
    grad_second = against(grad_hidden_low, w_up_f)

    qkv = (plain(first_in, w_qkv_f) + b_qkv_f).reshape(length, 3, heads, HD)
    cos_tab, sine_tab = tables(pos_rows)
    queries = (rotate(qkv[:, 0], cos_tab, sine_tab) * scaling).astype(BF16)
    keys = rotate(qkv[:, 1], cos_tab, sine_tab).astype(BF16)
    values = qkv[:, 2].astype(BF16)
    token = jnp.arange(length)
    visible = token[:, None] >= token[None, :]
    scores = jnp.einsum("qhd,khd->hqk", queries, keys, preferred_element_type=F32)
    scores = jnp.where(visible, scores, -1e30)
    exponent = jnp.exp(scores - jnp.max(scores, -1, keepdims=True))
    probs = exponent / jnp.sum(exponent, -1, keepdims=True)
    probs_low = probs.astype(BF16)
    mixture = jnp.einsum("hqk,khd->qhd", probs_low, values, preferred_element_type=F32)
    mixture = mixture.reshape(length, -1).astype(BF16)
    grad_w_out = over_rows(mixture, g_rows).astype(BF16)
    attended = plain(mixture, w_out_f)
    grad_mixture = against(g_rows, w_out_f).astype(BF16).reshape(length, heads, HD)
    grad_probs = jnp.einsum("qhd,khd->hqk", grad_mixture, values, preferred_element_type=F32)
    row_delta = jnp.sum(probs * grad_probs, -1, keepdims=True)
    grad_scores = (probs * (grad_probs - row_delta)).astype(BF16)
    grad_query = (
        jnp.einsum("hqk,khd->qhd", grad_scores, keys, preferred_element_type=F32) * scaling
    )
    grad_key = jnp.einsum("hqk,qhd->khd", grad_scores, queries, preferred_element_type=F32)
    grad_value = jnp.einsum("hqk,qhd->khd", probs_low, grad_mixture, preferred_element_type=F32)
    grad_qkv = jnp.stack(
        [
            rotate(grad_query, cos_tab, -sine_tab),
            rotate(grad_key, cos_tab, -sine_tab),
            grad_value,
        ],
        1,
    ).reshape(length, -1)
    grad_b_qkv = jnp.sum(grad_qkv, 0)
    grad_qkv_low = grad_qkv.astype(BF16)
    grad_w_qkv = over_rows(first_in, grad_qkv_low).astype(BF16)
    grad_first = against(grad_qkv_low, w_qkv_f)

    summed = (attended + fed_forward).astype(BF16)
    back = (grad_first * gain_a + grad_second * gain_m).astype(BF16)
    g_f = g_local.astype(F32)
    spread_qkv = jnp.zeros((3, parts, heads * HD), F32)
    spread_qkv = lax.dynamic_update_index_in_dim(
        spread_qkv, grad_b_qkv.reshape(3, 1, -1), me, 1
    )
    packed = [
        jnp.sum(g_f, 0),
        jnp.sum(grad_first * normed, 0),
        jnp.sum(grad_first, 0),
        jnp.sum(grad_second * normed, 0),
        jnp.sum(grad_second, 0),
        spread_qkv,
    ]
    packed = jnp.concatenate([p.reshape(groups, parts, -1) for p in packed], 2)
    packed = jnp.swapaxes(packed, 0, 1)
    ups = jnp.pad(grad_b_up.reshape(groups, unit), ((0, 0), (0, 128 - unit)))
    grid = (4, groups // 4)
    pairs = (parts // 2, 2, block_len, width)
    summed, back, out_w_down, grad_w_up, grad_w_qkv, grad_w_out, sums = scatter(
        summed.reshape(pairs),
        back.reshape(pairs),
        grad_w_down.reshape(grid + w_down.shape),
        grad_w_up.reshape(grid + (-1, groups * unit)),
        grad_w_qkv.reshape(grid + (-1, 3 * heads * HD)),
        grad_w_out.reshape(grid + w_out.shape),
        packed,
        ups,
    )

    x_f = x_local.astype(F32)
    layer_out = (x_f + summed + (b_out_f + b_down_f)).astype(BF16)
    n_local, r_local = norm_stats(x_f)
    back = r_local * (
        back
        - jnp.mean(back, -1, keepdims=True)
        - n_local * jnp.mean(back * n_local, -1, keepdims=True)
    )
    grad_in = (g_f + back).astype(BF16)
    grad_w_up = grad_w_up.reshape(parts, -1, groups, unit).transpose(1, 2, 0, 3).reshape(w_up.shape)
    grad_w_qkv = grad_w_qkv.reshape(parts, -1, 3, heads * HD).transpose(1, 2, 0, 3).reshape(w_qkv.shape)
    pieces = [sums[0, i * rows16 : (i + 1) * rows16] for i in range(5)]
    return (
        layer_out[None],
        grad_in[None],
        grad_w_qkv.astype(F32),
        sums[0, 5 * rows16 :],
        grad_w_out.astype(F32),
        pieces[0],
        grad_w_up.astype(F32),
        sums[1, :unit],
        out_w_down,
        pieces[0],
        pieces[1],
        pieces[2],
        pieces[3],
        pieces[4],
    )


def solution(mesh):
    both = ("batch", "seq")
    rows = P("batch", "seq", None)
    matrix = P(both, None)
    vector = P(both)
    return jax.shard_map(
        shards,
        mesh=mesh,
        in_specs=(
            rows,
            P("batch", "seq"),
            matrix,
            vector,
            matrix,
            vector,
            matrix,
            vector,
            matrix,
            vector,
            vector,
            vector,
            vector,
            vector,
            rows,
        ),
        out_specs=(
            rows,
            rows,
            matrix,
            vector,
            matrix,
            vector,
            matrix,
            vector,
            matrix,
            vector,
            vector,
            vector,
            vector,
            vector,
        ),
        check_vma=False,
    )
```

```python
import jax
import jax.numpy as jnp
from jax import lax
from jax.experimental import pallas as pl
from jax.experimental.pallas import tpu as pltpu
from jax.sharding import PartitionSpec as P

H = 16
HD = 128
ROT = 32
EPS = 1e-05
C = 2048
SCALE = HD ** (-0.5)
F32 = jnp.float32
BF16 = jnp.bfloat16
MESH = pl.DeviceIdType.MESH
STEPS = (1, -1, 2)
SEQ_PEERS = [(dy, dc) for dc in (1, 0) for dy in (0, 1, -1, 2) if (dy, dc) != (0, 0)]


def place():
    b = lax.axis_index("batch")
    s = lax.axis_index("seq")
    return b // 4, b % 4, s // 2, s % 2


def shifted(x=0, z=0, y=0, c=0):
    px, pz, py, pc = place()
    px = lax.rem(px + x + 4, 4)
    pz = lax.rem(pz + z + 4, 4)
    py = lax.rem(py + y + 4, 4)
    pc = lax.rem(pc + c, 2)
    return (px * 4 + pz, py * 2 + pc)


def moved(pos, step):
    return lax.rem(pos + step + 4, 4)


class Copies:
    def __init__(self, send, recv):
        self.send, self.recv, self.count, self.made = send, recv, 0, []

    def make(self, src, dst, device):
        k = self.count
        self.count += 1
        return pltpu.make_async_remote_copy(
            src_ref=src,
            dst_ref=dst,
            send_sem=self.send.at[k],
            recv_sem=self.recv.at[k],
            device_id=device,
            device_id_type=MESH,
        )

    def start(self, src, dst, device):
        copy = self.make(src, dst, device)
        copy.start()
        self.made.append(copy)
        return copy

    def drain(self):
        for copy in self.made:
            copy.wait_send()


class Locals:
    def __init__(self, sems):
        self.sems, self.count = sems, 0

    def start(self, src, dst):
        copy = pltpu.make_async_copy(src, dst, self.sems.at[self.count])
        self.count += 1
        copy.start()
        return copy


def greet(extra=None):
    barrier = pltpu.get_barrier_semaphore()
    peers = [dict(x=d) for d in STEPS] + [dict(z=d) for d in STEPS]
    peers += [dict(y=dy, c=dc) for dy, dc in SEQ_PEERS]
    for p in peers:
        pl.semaphore_signal(barrier, inc=1, device_id=shifted(**p), device_id_type=MESH)
    count = len(peers)
    if extra is not None:
        differs, source = extra

        @pl.when(differs)
        def _():
            pl.semaphore_signal(barrier, inc=1, device_id=source, device_id_type=MESH)

        count = jnp.where(differs, count + 1, count)
    pl.semaphore_wait(barrier, count)


def group(buf, first, at, half=None, rows=None):
    span = pl.ds(0, 4) if half is None else pl.ds(2 * half, 2)
    index = (span, at) if first == "x" else (at, span)
    if rows is not None:
        index += (pl.ds(*rows),)
    return buf.at[index]


class Gather:
    def __init__(self, copies, buf, first, rows=None):
        self.copies, self.buf, self.first, self.rows = copies, buf, first, rows
        self.other = "z" if first == "x" else "x"
        x, z, _, _ = place()
        self.at = z if first == "x" else x
        self.own = buf.at[x, z] if rows is None else buf.at[x, z, pl.ds(*rows)]

    def part(self, step, half=None):
        return group(self.buf, self.first, moved(self.at, step), half, self.rows)

    def one(self, src=None):
        src = self.own if src is None else src
        self.sent = [self.copies.start(src, self.own, shifted(**{self.first: d})) for d in STEPS]

    def two(self):
        for c in self.sent:
            c.wait_recv()
        mine = self.part(0)
        self.sent = [self.copies.start(mine, mine, shifted(**{self.other: d})) for d in (1, -1)]

    def three(self):
        sent = []
        for c, d, half in zip(self.sent, (1, -1), (0, 1)):
            c.wait_recv()
            passed = self.part(-d, half)
            sent.append(self.copies.start(passed, passed, shifted(**{self.other: d})))
        self.sent = sent

    def done(self):
        for c in self.sent:
            c.wait_recv()


def out_route(groups=16, parts=8, heads=2):
    b = lax.axis_index("batch")
    s = lax.axis_index("seq")
    to = ((b % heads) * parts + s, b // heads)
    source = (s * heads + b // parts, b % parts)
    differs = jnp.logical_or(to[0] != b, to[1] != s)
    return to, source, differs


def dot(a, b, ca=1, cb=0):
    return lax.dot_general(a, b, (((ca,), (cb,)), ((), ())), preferred_element_type=F32)


def turn(v, tc, ta, tb):
    return v * tc + pltpu.roll(v, 112, 1) * ta + pltpu.roll(v, 16, 1) * tb


def project(i, F1, QK, bq, TC, TA, TB, Q, K, V):
    r = pl.ds(pl.multiple_of(i * 256, 256), 256)
    w = QK[...].reshape(C, 768)
    full = dot(F1[r], w) + bq[...]
    tc, ta, tb = TC[r], TA[r], TB[r]
    for h in range(2):
        at = h * 128
        q = turn(full[:, at : at + 128], tc, ta, tb) * SCALE
        Q[r, at : at + 128] = q.astype(BF16)
        k = turn(full[:, 256 + at : 384 + at], tc, ta, tb)
        K[r, at : at + 128] = k.astype(BF16)
        V[r, at : at + 128] = full[:, 512 + at : 640 + at].astype(BF16)


def head_pass(h, Q, K, V, GM, MIX, GL, DK, DV, TC, TA, TB, gb):
    cols = pl.ds(h * 128, 128)
    gq_cols, gk_cols, gv_cols = (pl.ds(o + h * 128, 128) for o in (0, 256, 512))
    for i in reversed(range(4)):
        r = pl.ds(i * 256, 256)
        n = (i + 1) * 256
        q, g = Q[r, cols], GM[r, cols]
        k, v = K[0:n, cols], V[0:n, cols]
        s = dot(q, k, 1, 1)
        row = lax.broadcasted_iota(jnp.int32, (256, n), 0) + i * 256
        col = lax.broadcasted_iota(jnp.int32, (256, n), 1)
        s = jnp.where(row >= col, s, -1e30)
        p = jnp.exp(s - jnp.max(s, -1, keepdims=True))
        p = p * (1.0 / jnp.sum(p, -1, keepdims=True))
        p_low = p.astype(BF16)
        MIX[r, cols] = dot(p_low, v).astype(BF16)
        gp = dot(g, v, 1, 1)
        gs = (p * (gp - jnp.sum(p * gp, -1, keepdims=True))).astype(BF16)
        dk, dv = dot(gs, q, 0, 0), dot(p_low, g, 0, 0)
        if i == 3:
            DK[...], DV[...] = dk, dv
        else:
            DK[0:n, :] += dk
            DV[0:n, :] += dv
        gq = dot(gs, k) * SCALE
        gq = turn(gq, TC[r], -TA[r], -TB[r])
        GL[r, gq_cols] = gq.astype(BF16)
        part = jnp.sum(gq, 0, keepdims=True)
        total = part if i == 3 else total + part
    gb[:, gq_cols] = total
    gk = turn(DK[...], TC[...], -TA[...], -TB[...])
    GL[:, gk_cols] = gk.astype(BF16)
    gb[:, gk_cols] = jnp.sum(gk, 0, keepdims=True)
    gv = DV[...]
    GL[:, gv_cols] = gv.astype(BF16)
    gb[:, gv_cols] = jnp.sum(gv, 0, keepdims=True)


def front_kernel(x_ref, g_ref, small_ref, rot_ref, up_ref, qkv_ref, down_ref, out_ref,
                 go, f2o, no, upo, dno, acto, ghlo, gqo, goo, po, so, vec, gsum, gbu, gbq,
                 X, G, SA, RA, SM, UP, QK, DN, WO, F1, F2, NB, ACT, GHL, GQ, GO,
                 Q, K, V, GM, MIX, GL, DK, DV, TC, TA, TB, BQ,
                 send, recv, loc):
    copies, local = Copies(send, recv), Locals(loc)
    x, z, y, c = place()
    s = y * 2 + c
    to, source, differs = out_route()
    greet((differs, source))

    def block(k):
        return pl.ds(pl.multiple_of(k * 128, 128), 128)

    SA[s] = small_ref[...]
    RA[s] = rot_ref[...]
    sm = [copies.start(small_ref, SA.at[s], shifted(y=dy, c=dc)) for dy, dc in SEQ_PEERS]

    def across(src, dst):
        dst[...] = src[s]
        return [
            copies.start(src.at[moved(y, dy) * 2 + lax.rem(c + dc, 2)], dst, shifted(y=dy, c=dc))
            for dy, dc in SEQ_PEERS
        ]

    rows16 = pl.ds(pl.multiple_of(s * 16, 16), 16)
    qk = across(qkv_ref, QK.at[x, z, rows16])
    out_copy = copies.make(out_ref, WO.at[to[0] // 4, to[0] % 4], to)

    @pl.when(differs)
    def _():
        out_copy.start()

    @pl.when(jnp.logical_not(differs))
    def _():
        WO[x, z] = out_ref[...]

    def seq_one(src, dst):
        own = dst.at[block(s)]
        own[...] = src[...]
        return [copies.start(src, own, shifted(y=d)) for d in (1, -1)] + [
            copies.start(src, own, shifted(c=1))
        ]

    def seq_two(sent, dst):
        more = []
        for cp, d in zip(sent[:2], (1, -1)):
            cp.wait_recv()
            got = dst.at[block(moved(y, -d) * 2 + c)]
            more.append(copies.start(got, got, shifted(c=1)))
        up_way = c == 0
        got = dst.at[block(jnp.where(up_way, moved(y, -1), moved(y, 1)) * 2 + c)]
        py = jnp.where(up_way, moved(y, 1), moved(y, -1))
        fwd = copies.start(got, got, (lax.axis_index("batch"), py * 2 + c))
        sent[2].wait_recv()
        return more, fwd

    def seq_three(more, fwd, dst):
        fwd.wait_recv()
        got = dst.at[block(moved(y, 2) * 2 + c)]
        return more + [copies.start(got, got, shifted(c=1))]

    xs = seq_one(x_ref, X)
    ra = [copies.start(rot_ref, RA.at[s], shifted(y=dy, c=dc)) for dy, dc in SEQ_PEERS]
    up = across(up_ref, UP.at[x, z, rows16])
    gs = seq_one(g_ref, G)
    DN[x, z] = down_ref[...]

    for cp in sm:
        cp.wait_recv()
    total = SA[0].astype(F32)
    for k in range(1, 8):
        total += SA[k].astype(F32)
    row = lax.broadcasted_iota(jnp.int32, (16, 128), 0)
    SM[x, z] = jnp.where(row == 9, SA[s].astype(F32), total).astype(BF16)
    small = Gather(copies, SM, "z")
    small.one()

    for cp in qk:
        cp.wait_recv()
    qa = Gather(copies, QK, "x", (0, 64))
    qb = Gather(copies, QK, "z", (64, 64))
    qa.one()
    qb.one()

    @pl.when(differs)
    def _():
        out_copy.wait_recv()
        out_copy.wait_send()

    wo = Gather(copies, WO, "x")
    wo.one()
    small.two()
    qa.two()
    qb.two()
    wo.two()
    down = Gather(copies, DN, "x")
    down.one(down_ref)
    for cp in up:
        cp.wait_recv()
    upg = Gather(copies, UP, "z")
    upg.one()
    small.three()
    xs2, xf = seq_two(xs, X)
    qa.three()
    qb.three()
    wo.three()
    total = jnp.zeros((1, C), F32)
    for k in range(8):
        total += jnp.sum(g_ref[16 * k : 16 * (k + 1)].astype(F32), 0, keepdims=True)
    gsum[...] = total
    small.done()
    for i in range(4):
        for j in range(4):
            b = i * 4 + j
            tile = SM[i, j].astype(F32)
            vec[0:6, b * 128 : (b + 1) * 128] = tile[0:6]
            for k in range(3):
                BQ[3 * b + k : 3 * b + k + 1, :] = tile[6 + k : 7 + k]
            if b % 2 == 0:
                kept = tile[9:10]
            else:
                vec[6:7, b // 2 * 128 : (b // 2 + 1) * 128] = kept + tile[9:10]

    def norm(k):
        def step(t, _):
            r = pl.ds(pl.multiple_of(k * 128 + t * 16, 16), 16)
            v = X[r].astype(F32)
            v = v - jnp.mean(v, -1, keepdims=True)
            n = v * lax.rsqrt(jnp.mean(v * v, -1, keepdims=True) + EPS)
            NB[r] = n.astype(BF16)
            F1[r] = (n * vec[2:3, :] + vec[3:4, :]).astype(BF16)
            F2[r] = (n * vec[4:5, :] + vec[5:6, :]).astype(BF16)
            return 0

        lax.fori_loop(0, 8, step, 0)

    norm(s)
    norm(y * 2 + 1 - c)
    norm(moved(y, -1) * 2 + c)
    norm(moved(y, 1) * 2 + c)
    xs3 = seq_three(xs2, xf, X)
    gs2, gf = seq_two(gs, G)
    xs3[0].wait_recv()
    norm(moved(y, -1) * 2 + 1 - c)
    xs3[1].wait_recv()
    norm(moved(y, 1) * 2 + 1 - c)
    norm(moved(y, 2) * 2 + c)
    xs3[2].wait_recv()
    norm(moved(y, 2) * 2 + 1 - c)
    saves = [local.start(F2, f2o), local.start(NB, no)]
    down.two()
    upg.two()

    for cp in ra:
        cp.wait_recv()
    lane = lax.broadcasted_iota(jnp.int32, (128, 128), 1)
    for k in range(8):
        r = pl.ds(k * 128, 128)
        tile = jnp.concatenate([RA[k], jnp.zeros((96, 128), F32)], 0).T
        TC[r] = jnp.where(lane < 16, tile, jnp.where(lane < 32, pltpu.roll(tile, 16, 1), 1.0))
        TA[r] = jnp.where(lane < 16, -pltpu.roll(tile, 112, 1), 0.0)
        TB[r] = jnp.where((lane >= 16) & (lane < 32), tile, 0.0)
    for gth in (qa, qb):
        gth.done()

    for part in range(3):
        at = pl.multiple_of(part * 16 + s * 2, 2)
        pair = BQ[pl.ds(at, 2), :]
        for k in range(2):
            gbq[:, part * 256 + k * 128 : part * 256 + (k + 1) * 128] = pair[k : k + 1]
    bias = gbq[...]
    vec[9:10, 0:768] = bias

    def first(i, _):
        project(i, F1, QK, vec.at[9:10, 0:768], TC, TA, TB, Q, K, V)
        return 0

    lax.fori_loop(0, 4, first, 0)
    gs3 = seq_three(gs2, gf, G)
    wo.done()
    for cp in gs3:
        cp.wait_recv()
    saves.append(local.start(G, go))

    def mixed(i, _):
        r = pl.ds(pl.multiple_of(i * 256, 256), 256)
        GM[r] = dot(G[r], WO[...].reshape(256, C), 1, 1).astype(BF16)
        return 0

    lax.fori_loop(0, 4, mixed, 0)
    for h in range(2):
        head_pass(h, Q, K, V, GM, MIX, GL, DK, DV, TC, TA, TB, gbq)
    down.three()
    upg.three()

    def grad_out(j, _):
        q = pl.ds(pl.multiple_of(j * 1024, 1024), 1024)
        GO[:, :, :, q] = dot(MIX[...], G[:, q], 0, 0).astype(BF16).reshape(4, 4, 16, 1024)
        return 0

    lax.fori_loop(0, 2, grad_out, 0)
    saves.append(local.start(GO, goo))

    def grad_qkv(i, _):
        r = pl.ds(pl.multiple_of(i * 512, 512), 512)
        GQ[i] = dot(F1[:, r], GL[...], 0, 0).astype(BF16).reshape(4, 128, 768)
        return 0

    lax.fori_loop(0, 4, grad_qkv, 0)
    saves.append(local.start(GQ, gqo))
    for cp in xs + xs2 + [xf, xs3[2]]:
        cp.wait_send()
    copies.made = [cp for cp in copies.made if all(cp is not m for m in xs + xs2 + [xf, xs3[2]])]

    def attend(t, _):
        i, j = t // 2, t % 2
        r = pl.ds(pl.multiple_of(i * 512, 512), 512)
        q = pl.ds(pl.multiple_of(j * 1024, 1024), 1024)
        X[r, q] = dot(MIX[r], WO[:, :, :, q].reshape(256, 1024)).astype(BF16)
        return 0

    lax.fori_loop(0, 4, attend, 0)
    saves.append(local.start(X, po))
    vec[10:12, :] = jnp.zeros((2, C), F32)

    def grad_first(t, _):
        i, j = t // 4, t % 4
        r = pl.ds(pl.multiple_of(i * 256, 256), 256)
        q = pl.ds(pl.multiple_of(j * 512, 512), 512)
        u = dot(GL[r], QK[j].reshape(512, 768), 1, 1)
        vec[10:11, q] += jnp.sum(u * NB[r, q].astype(F32), 0, keepdims=True)
        vec[11:12, q] += jnp.sum(u, 0, keepdims=True)
        F1[r, q] = (u * vec[2:3, q]).astype(BF16)
        return 0

    lax.fori_loop(0, 16, grad_first, 0)
    saves.append(local.start(F1, so))

    gbu[...] = jnp.zeros_like(gbu)
    upg.done()
    saves.append(local.start(UP, upo))
    down.done()
    saves.append(local.start(DN, dno))

    def hidden(t, _):
        i, j = t // 2, t % 2
        r = pl.ds(pl.multiple_of(i * 256, 256), 256)
        q = pl.ds(pl.multiple_of(j * 512, 512), 512)
        h = dot(F2[r], UP[:, :, :, q].reshape(C, 512)) + vec[6:7, q]
        ga = dot(G[r], DN[pl.ds(2 * j, 2)].reshape(512, C), 1, 1)
        cdf = 0.5 + 0.5 * lax.erf(h * (0.5**0.5))
        ACT[r, q] = (h * cdf).astype(BF16)
        gh = ga * (cdf + h * (jnp.exp(h * h * -0.5) * 0.3989422804014327))
        gbu[:, q] += jnp.sum(gh, 0, keepdims=True)
        GHL[r, q] = gh.astype(BF16)
        return 0

    lax.fori_loop(0, 8, hidden, 0)
    saves += [local.start(ACT, acto), local.start(GHL, ghlo)]
    for cp in saves:
        cp.wait()
    copies.drain()


def front(x, g, small, rot, up, qkv, down, out):
    vm = pl.BlockSpec(memory_space=pltpu.VMEM)
    any_ = pl.BlockSpec(memory_space=pl.ANY)
    full = (1024, C)
    n_up, n_qkv = up.shape[-1], qkv.shape[-1]
    up_all, qk_all = (4, 4, 128, n_up), (4, 4, 128, n_qkv)
    dn_all, wo_all = (4, 4) + down.shape, (4, 4) + out.shape
    unit = (1024, n_up)
    held = [full, full, full, up_all, dn_all, unit, unit, qk_all, wo_all, full, full]
    S = pltpu.VMEM
    two = (1024, n_qkv // 3)
    scratch = [
        (full, BF16), (full, BF16), ((8, 16, 128), BF16), ((8, 32, 128), F32), ((4, 4, 16, 128), BF16),
        (up_all, BF16), (qk_all, BF16), (dn_all, BF16), (wo_all, BF16),
        (full, BF16), (full, BF16), (full, BF16), (unit, BF16), (unit, BF16), (qk_all, BF16), (wo_all, BF16),
        (two, BF16), (two, BF16), (two, BF16), (two, BF16), (two, BF16), ((1024, n_qkv), BF16),
        ((1024, HD), F32), ((1024, HD), F32), ((1024, HD), F32), ((1024, HD), F32), ((1024, HD), F32),
        ((48, 128), F32),
    ]
    return pl.pallas_call(
        front_kernel,
        out_shape=[jax.ShapeDtypeStruct(h, BF16) for h in held]
        + [jax.ShapeDtypeStruct(h, F32) for h in ((16, C), (1, C), (1, n_up), (1, n_qkv))],
        in_specs=[vm] * 8,
        out_specs=[any_] * 11 + [vm] * 4,
        scratch_shapes=[S(*h) for h in scratch]
        + [pltpu.SemaphoreType.DMA((96,)), pltpu.SemaphoreType.DMA((96,)), pltpu.SemaphoreType.DMA((12,))],
        compiler_params=pltpu.CompilerParams(
            collective_id=1, has_side_effects=True, vmem_limit_bytes=63 * 2**20
        ),
    )(x, g, small, rot, up, qkv, down, out)


def add_rows(shape, into, parts):
    slabs, rows = shape
    step = min(rows, 16)

    def add(t, _):
        i = t // (rows // step)
        r = pl.ds(pl.multiple_of(t % (rows // step) * step, step), step)
        total = parts[0](i, r).astype(F32)
        for p in parts[1:]:
            total += p(i, r).astype(F32)
        into(i, r, total)
        return 0

    lax.fori_loop(0, slabs * (rows // step), add, 0)


class Scatter:
    def __init__(self, copies, buf, first, relay, land, last, rows=None):
        self.copies, self.buf, self.first, self.rows = copies, buf, first, rows
        self.relay, self.land, self.last = relay, land, last
        self.other = "z" if first == "x" else "x"
        x, z, _, _ = place()
        self.at, self.mine = (z, x) if first == "x" else (x, z)
        self.count = buf.shape[2] if rows is None else rows[1]
        self.base = 0 if rows is None else rows[0]

    def part(self, step, half=None):
        return group(self.buf, self.first, moved(self.at, step), half, self.rows)

    def slab(self, step, i, r):
        at = moved(self.at, step)
        r = pl.ds(self.base + r.start, r.size)
        return (i, at, r) if self.first == "x" else (at, i, r)

    def one(self):
        start, to = self.copies.start, self.other
        self.far = [
            start(self.part(2, k), self.relay.at[k], shifted(**{to: d})) for k, d in enumerate((1, -1))
        ]
        self.near = [
            start(self.part(d, 1 - k), self.land.at[k, pl.ds(2 - 2 * k, 2)], shifted(**{to: d}))
            for k, d in enumerate((1, -1))
        ]

    def mid(self):
        for k, d in enumerate((1, -1)):
            self.far[k].wait_recv()

            def put(i, r, total, k=k, d=d):
                self.buf[self.slab(d, i + 2 * k, r)] = total.astype(self.buf.dtype)

            add_rows(
                (2, self.count),
                put,
                [lambda i, r, k=k, d=d: self.buf[self.slab(d, i + 2 * k, r)],
                 lambda i, r, k=k: self.relay[k, i, r]],
            )
            self.near.append(
                self.copies.start(
                    self.part(d, k), self.land.at[k, pl.ds(2 * k, 2)], shifted(**{self.other: d})
                )
            )

    def two(self):
        for cp in self.near:
            cp.wait_recv()

        def put(i, r, total):
            self.buf[self.slab(0, i, r)] = total.astype(self.buf.dtype)

        add_rows(
            (4, self.count),
            put,
            [lambda i, r: self.buf[self.slab(0, i, r)],
             lambda i, r: self.land[0, i, r], lambda i, r: self.land[1, i, r]],
        )
        x, z, _, _ = place()
        self.sent = []
        for k, d in enumerate(STEPS):
            there = moved(self.mine, d)
            index = (there, self.at) if self.first == "x" else (self.at, there)
            if self.rows is not None:
                index += (pl.ds(*self.rows),)
            self.sent.append(
                self.copies.start(self.buf.at[index], self.last.at[k], shifted(**{self.first: d}))
            )

    def three(self, put):
        for cp in self.sent:
            cp.wait_recv()
        add_rows(
            (1, self.count),
            lambda i, r, total: put(r, total),
            [lambda i, r: self.buf[self.slab(0, self.mine, r)]]
            + [lambda i, r, k=k: self.last[k, r] for k in range(3)],
        )


class SeqScatter:
    def __init__(self, copies, buf, pair, relay, land):
        self.copies, self.buf, self.pair, self.relay, self.land = copies, buf, pair, relay, land
        _, _, self.y, self.c = place()

    def one(self):
        self.sent = self.copies.start(self.buf.at[:, 1 - self.c], self.pair, shifted(c=1))

    def two(self):
        self.sent.wait_recv()
        buf, c = self.buf, self.c

        def put(i, r, total):
            buf[i, c, r] = total.astype(BF16)

        add_rows((4, 128), put, [lambda i, r: buf[i, c, r], lambda i, r: self.pair[i, r]])
        start = self.copies.start
        far = moved(self.y, 2)
        halves = (pl.ds(0, 64), pl.ds(64, 64))
        self.far = [
            start(buf.at[far, c, halves[k]], self.relay.at[k], shifted(y=d)) for k, d in enumerate((1, -1))
        ]
        self.near = [
            start(buf.at[moved(self.y, d), c, halves[1 - k]], self.land.at[k, halves[1 - k]], shifted(y=d))
            for k, d in enumerate((1, -1))
        ]

    def mid(self):
        buf, c = self.buf, self.c
        for k, d in enumerate((1, -1)):
            self.far[k].wait_recv()
            to = moved(self.y, d)

            def rows(r, k=k):
                return pl.ds(64 * k + r.start, r.size)

            def put(i, r, total, rows=rows, to=to):
                buf[to, c, rows(r)] = total.astype(BF16)

            add_rows(
                (1, 64),
                put,
                [lambda i, r, rows=rows, to=to: buf[to, c, rows(r)],
                 lambda i, r, k=k: self.relay[k, r]],
            )
            self.near.append(
                self.copies.start(
                    buf.at[to, c, pl.ds(64 * k, 64)], self.land.at[k, pl.ds(64 * k, 64)], shifted(y=d)
                )
            )

    def three(self, put):
        for cp in self.near:
            cp.wait_recv()
        buf, y, c = self.buf, self.y, self.c
        add_rows(
            (1, 128),
            lambda i, r, total: put(r, total),
            [lambda i, r: buf[y, c, r], lambda i, r: self.land[0, r], lambda i, r: self.land[1, r]],
        )


def back_kernel(g_in, f2_in, n_in, up_in, dn_in, act_in, ghl_in, gq_in, go_in, p_in, s_in,
                vec, g_sum, g_bu, g_bq,
                sp, sq, gd, gu, gq, go, sv,
                A, B, NB, UP, DN, ACT, GHL, GQ, GO, GD, GU,
                p_pair, p_relay, p_land, q_pair, q_relay, q_land,
                d_relay, d_land, d_last, u_relay, u_land, u_last,
                a_relay, a_land, a_last, b_relay, b_land, b_last,
                o_relay, o_land, o_last, BQ, VT, v_land, CT, c_relay, c_land, c_last,
                sums, gu_part, gq_part, go_part,
                send, recv, loc):
    copies, local = Copies(send, recv), Locals(loc)
    x, z, y, c = place()
    s = y * 2 + c
    to, source, differs = out_route()
    loads = {}
    for name, src, dst in (
        ("gq", gq_in, GQ), ("go", go_in, GO), ("act", act_in, ACT), ("g", g_in, A),
        ("ghl", ghl_in, GHL), ("f2", f2_in, B), ("dn", dn_in, DN), ("up", up_in, UP), ("n", n_in, NB),
    ):
        loads[name] = local.start(src, dst)
    greet((differs, to))
    fp = SeqScatter(copies, A, p_pair, p_relay, p_land)
    fq = SeqScatter(copies, B, q_pair, q_relay, q_land)
    sd = Scatter(copies, GD, "x", d_relay, d_land, d_last)
    su = Scatter(copies, GU, "z", u_relay, u_land, u_last)
    sa = Scatter(copies, GQ, "x", a_relay, a_land, a_last, (0, 64))
    sb = Scatter(copies, GQ, "z", b_relay, b_land, b_last, (64, 64))
    so = Scatter(copies, GO, "x", o_relay, o_land, o_last)
    sc = Scatter(copies, CT, "z", c_relay, c_land, c_last)
    loads["gq"].wait()
    sa.one()
    sb.one()
    loads["go"].wait()
    so.one()
    loads["act"].wait()
    loads["g"].wait()

    def grad_down(t, _):
        i, j = t // 2, t % 2
        u = pl.ds(pl.multiple_of(i * 256, 256), 256)
        q = pl.ds(pl.multiple_of(j * 1024, 1024), 1024)
        right = A[:, :, :, q].reshape(1024, 1024)
        GD[i, :, :, q] = dot(ACT[:, u], right, 0, 0).astype(BF16).reshape(4, 64, 1024)
        return 0

    lax.fori_loop(0, 8, grad_down, 0)
    sd.one()
    loads["p"] = local.start(p_in, A)
    loads["ghl"].wait()
    loads["f2"].wait()

    def grad_up(t, _):
        i, j = t // 2, t % 2
        r = pl.ds(pl.multiple_of(i * 512, 512), 512)
        q = pl.ds(pl.multiple_of(j * 512, 512), 512)
        left = B[:, :, :, r].reshape(1024, 512)
        GU[i, :, :, q] = dot(left, GHL[:, q], 0, 0).astype(BF16).reshape(4, 128, 512)
        return 0

    lax.fori_loop(0, 8, grad_up, 0)
    su.one()
    loads["s"] = local.start(s_in, B)
    sa.mid()
    sb.mid()
    so.mid()
    loads["dn"].wait()
    loads["p"].wait()

    def feed(t, _):
        i, j = t // 4, t % 4
        r = pl.ds(pl.multiple_of(i * 512, 512), 512)
        q = pl.ds(pl.multiple_of(j * 512, 512), 512)
        two = pl.ds(2 * i, 2)
        total = dot(ACT[r], DN[:, :, :, q].reshape(1024, 512)) + A[two, :, :, q].reshape(512, 512).astype(F32)
        A[two, :, :, q] = total.astype(BF16).reshape(2, 2, 128, 512)
        return 0

    lax.fori_loop(0, 8, feed, 0)
    fp.one()
    loads["up"].wait()
    loads["n"].wait()
    loads["s"].wait()
    sums[...] = jnp.zeros_like(sums)

    def second(t, _):
        i, j = t // 4, t % 4
        r = pl.ds(pl.multiple_of(i * 256, 256), 256)
        q = pl.ds(pl.multiple_of(j * 512, 512), 512)
        u = dot(GHL[r], UP[j].reshape(512, 1024), 1, 1)
        sums[0:1, q] += jnp.sum(u * NB[r, q].astype(F32), 0, keepdims=True)
        sums[1:2, q] += jnp.sum(u, 0, keepdims=True)
        total = u * vec[4:5, q] + B[i, :, :, q].reshape(256, 512).astype(F32)
        B[i, :, :, q] = total.astype(BF16).reshape(2, 128, 512)
        return 0

    lax.fori_loop(0, 8, second, 0)
    fp.two()
    lax.fori_loop(8, 16, second, 0)
    fq.one()

    BQ[...] = jnp.zeros_like(BQ)
    for part in range(3):
        for k in range(2):
            row = part * 16 + s * 2 + k
            at = part * 256 + k * 128
            BQ[pl.ds(row, 1), :] = g_bq[:, at : at + 128]
    for b in range(16):
        at = b * 128
        VT[b, 0:1, :] = g_sum[:, at : at + 128]
        VT[b, 1:3, :] = vec[10:12, at : at + 128]
        VT[b, 3:5, :] = sums[0:2, at : at + 128]
        VT[b, 5:8, :] = BQ[3 * b : 3 * b + 3, :]
    vs = [
        copies.start(VT, v_land.at[k], shifted(y=dy, c=dc)) for k, (dy, dc) in enumerate(SEQ_PEERS)
    ]
    sa.two()
    sb.two()
    sd.mid()
    su.mid()
    fq.two()
    fp.mid()
    so.two()
    for cp in vs:
        cp.wait_recv()
    for b in range(16):
        total = VT[b]
        for k in range(7):
            total += v_land[k, b]
        CT[b // 4, b % 4, 0:8, :] = total
        CT[b // 4, b % 4, 8:9, :] = g_bu[:, b // 2 * 128 : b // 2 * 128 + 128]
        CT[b // 4, b % 4, 9:16, :] = jnp.zeros((7, 128), F32)
    sc.one()

    def store(ref, base=0):
        def put(r, total):
            ref[pl.ds(base + r.start, r.size)] = total.astype(ref.dtype)

        return put

    def spread(part, out):
        out[s] = part[pl.ds(pl.multiple_of(s * 16, 16), 16)]
        made = []
        for dy, dc in SEQ_PEERS:
            peer = moved(y, dy) * 2 + lax.rem(c + dc, 2)
            made.append(
                copies.start(
                    part.at[pl.ds(pl.multiple_of(peer * 16, 16), 16)], out.at[s], shifted(y=dy, c=dc)
                )
            )
        return made

    sa.three(store(gq_part))
    sb.three(store(gq_part, 64))
    backs = spread(gq_part, gq)
    so.three(store(go_part))
    out_copy = copies.make(go_part, go, source)

    @pl.when(differs)
    def _():
        out_copy.start()

    @pl.when(jnp.logical_not(differs))
    def _():
        go[...] = go_part[...]

    fq.mid()
    sc.mid()
    su.two()
    sd.two()
    fp.three(store(sp))
    sc.two()
    fq.three(store(sq))
    su.three(store(gu_part))
    backs += spread(gu_part, gu)
    sd.three(store(gd))
    sc.three(store(sv))

    @pl.when(differs)
    def _():
        out_copy.wait()

    for cp in backs:
        cp.wait_recv()
    copies.drain()


def back(g, f2, n, up, dn, act, ghl, gq, go, p, s, *small):
    any_ = pl.BlockSpec(memory_space=pl.ANY)
    vm = pl.BlockSpec(memory_space=pltpu.VMEM)
    n_d, n_u, n_q, n_o = dn.shape[3], up.shape[3], gq.shape[3], go.shape[3]
    S = pltpu.VMEM
    blocks = (4, 2, 128, C)

    def set_of(rows, cols, kind=BF16):
        return [S((2, 2, rows, cols), kind), S((2, 4, rows, cols), kind), S((3, rows, cols), kind)]

    seq = [S((4, 128, C), BF16), S((2, 64, C), BF16), S((2, 128, C), BF16)]
    held = [blocks, blocks, n.shape, up.shape, dn.shape, act.shape, ghl.shape, gq.shape, go.shape, dn.shape, up.shape]
    return pl.pallas_call(
        back_kernel,
        out_shape=[
            jax.ShapeDtypeStruct((128, C), F32), jax.ShapeDtypeStruct((128, C), F32),
            jax.ShapeDtypeStruct((64, n_d), F32), jax.ShapeDtypeStruct((8, 16, n_u), BF16),
            jax.ShapeDtypeStruct((8, 16, n_q), BF16), jax.ShapeDtypeStruct((16, n_o), BF16),
            jax.ShapeDtypeStruct((16, 128), F32),
        ],
        in_specs=[any_] * 11 + [vm] * 4,
        out_specs=[vm] * 7,
        scratch_shapes=[S(h, BF16) for h in held] + seq + seq
        + set_of(64, n_d) + set_of(128, n_u) + set_of(64, n_q) + set_of(64, n_q) + set_of(16, n_o)
        + [S((48, 128), F32), S((16, 8, 128), F32), S((7, 16, 8, 128), F32), S((4, 4, 16, 128), F32)] + set_of(16, 128, F32)
        + [S((8, C), F32), S((128, n_u), BF16), S((128, n_q), BF16), S((16, n_o), BF16),
           pltpu.SemaphoreType.DMA((96,)), pltpu.SemaphoreType.DMA((96,)), pltpu.SemaphoreType.DMA((12,))],
        compiler_params=pltpu.CompilerParams(
            collective_id=2, has_side_effects=True, vmem_limit_bytes=63 * 2**20
        ),
    )(g.reshape(blocks), f2.reshape(blocks), n, up, dn, act, ghl, gq, go, p.reshape(blocks), s.reshape(blocks), *small)


def tables(positions):
    half_rot = ROT // 2
    exponent = jnp.arange(half_rot).astype(F32) / half_rot
    frequency = jnp.power(10000.0, -exponent)
    angles = positions.astype(F32)[None] * frequency[:, None]
    return jnp.concatenate([jnp.cos(angles), jnp.sin(angles)])


def norm_stats(rows):
    average = jnp.mean(rows, -1, keepdims=True)
    centred = rows - average
    inverse = lax.rsqrt(jnp.mean(centred * centred, -1, keepdims=True) + EPS)
    return centred * inverse, inverse


def shards(
    inputs,
    positions,
    w_qkv,
    b_qkv,
    w_out,
    b_out,
    w_up,
    b_up,
    w_down,
    b_down,
    gain_attn,
    shift_attn,
    gain_mlp,
    shift_mlp,
    grad_out,
):
    _, block_len, width = inputs.shape
    groups = lax.axis_size("batch")
    parts = lax.axis_size("seq")
    me = lax.axis_index("seq")
    b_me = lax.axis_index("batch")
    heads = H // parts
    x_local = inputs[0]
    g_local = grad_out[0]
    unit = b_up.shape[0]
    cut = b_qkv.shape[0]
    rows16 = b_out.shape[0]

    lane = jnp.arange(128)
    vectors = jnp.stack([b_out, b_down, gain_attn, shift_attn, gain_mlp, shift_mlp])
    vectors = jnp.where(lane // rows16 == me, jnp.tile(vectors, (1, parts)), 0)
    three = jnp.where(jnp.arange(parts * cut) // cut == me, jnp.tile(b_qkv, parts), 0)
    ups = jnp.where(lane // unit == b_me % 2, jnp.tile(b_up, 2), 0)
    small = jnp.concatenate(
        [
            vectors,
            three.reshape(-1, 128),
            ups[None],
            jnp.zeros((6, 128), BF16),
        ]
    )
    up_cut = w_up.reshape(-1, groups, parts, unit).transpose(2, 0, 1, 3).reshape(parts, -1, groups * unit)
    qkv_cut = w_qkv.reshape(-1, 3, parts, heads * HD).transpose(2, 0, 1, 3).reshape(parts, -1, 3 * heads * HD)
    (G, F2, NB, UP, DN, ACT, GHL, GQ, GO, PM, SB, vec, g_sum, g_bu, g_bq) = front(
        x_local, g_local, small, tables(positions[0]), up_cut, qkv_cut, w_down, w_out
    )
    summed, back_sum, out_w_down, grad_w_up, grad_w_qkv, grad_w_out, sums = back(
        G, F2, NB, UP, DN, ACT, GHL, GQ, GO, PM, SB, vec, g_sum, g_bu, g_bq
    )

    x_f = x_local.astype(F32)
    layer_out = (x_f + summed + (vec[0] + vec[1])).astype(BF16)
    n_local, r_local = norm_stats(x_f)
    turned = r_local * (
        back_sum
        - jnp.mean(back_sum, -1, keepdims=True)
        - n_local * jnp.mean(back_sum * n_local, -1, keepdims=True)
    )
    grad_in = (g_local.astype(F32) + turned).astype(BF16)
    grad_w_up = grad_w_up.reshape(parts, -1, groups, unit).transpose(1, 2, 0, 3).reshape(w_up.shape)
    grad_w_qkv = grad_w_qkv.reshape(parts, -1, 3, heads * HD).transpose(1, 2, 0, 3).reshape(w_qkv.shape)
    pieces = lax.dynamic_slice_in_dim(sums[:5], me * rows16, rows16, 1)
    grad_b_qkv = lax.dynamic_slice_in_dim(sums[5:8].reshape(-1), me * cut, cut)
    grad_b_up = lax.dynamic_slice_in_dim(sums[8], b_me % 2 * unit, unit)
    return (
        layer_out[None],
        grad_in[None],
        grad_w_qkv.astype(F32),
        grad_b_qkv,
        grad_w_out.astype(F32),
        pieces[0],
        grad_w_up.astype(F32),
        grad_b_up,
        out_w_down,
        pieces[0],
        pieces[1],
        pieces[2],
        pieces[3],
        pieces[4],
    )


def solution(mesh):
    both = ("batch", "seq")
    rows = P("batch", "seq", None)
    matrix = P(both, None)
    vector = P(both)
    return jax.shard_map(
        shards,
        mesh=mesh,
        in_specs=(
            rows,
            P("batch", "seq"),
            matrix,
            vector,
            matrix,
            vector,
            matrix,
            vector,
            matrix,
            vector,
            vector,
            vector,
            vector,
            vector,
            rows,
        ),
        out_specs=(
            rows,
            rows,
            matrix,
            vector,
            matrix,
            vector,
            matrix,
            vector,
            matrix,
            vector,
            vector,
            vector,
            vector,
            vector,
        ),
        check_vma=False,
    )
```

```python
import jax
import jax.numpy as jnp
from jax import lax
from jax.experimental import pallas as pl
from jax.experimental.pallas import tpu as pltpu
from jax.sharding import PartitionSpec as P

H = 16
HD = 128
ROT = 32
EPS = 1e-05
C = 2048
SCALE = HD ** (-0.5)
F32 = jnp.float32
BF16 = jnp.bfloat16
MESH = pl.DeviceIdType.MESH
STEPS = (1, -1, 2)
SEQ_PEERS = [(dy, dc) for dc in (1, 0) for dy in (0, 1, -1, 2) if (dy, dc) != (0, 0)]


def place():
    b = lax.axis_index("batch")
    s = lax.axis_index("seq")
    return b // 4, b % 4, s // 2, s % 2


def shifted(x=0, z=0, y=0, c=0):
    px, pz, py, pc = place()
    px = lax.rem(px + x + 4, 4)
    pz = lax.rem(pz + z + 4, 4)
    py = lax.rem(py + y + 4, 4)
    pc = lax.rem(pc + c, 2)
    return (px * 4 + pz, py * 2 + pc)


def moved(pos, step):
    return lax.rem(pos + step + 4, 4)


class Copies:
    def __init__(self, send, recv):
        self.send, self.recv, self.count, self.made = send, recv, 0, []

    def make(self, src, dst, device):
        k = self.count
        self.count += 1
        return pltpu.make_async_remote_copy(
            src_ref=src,
            dst_ref=dst,
            send_sem=self.send.at[k],
            recv_sem=self.recv.at[k],
            device_id=device,
            device_id_type=MESH,
        )

    def start(self, src, dst, device):
        copy = self.make(src, dst, device)
        copy.start()
        self.made.append(copy)
        return copy

    def drain(self):
        for copy in self.made:
            copy.wait_send()


class Locals:
    def __init__(self, sems):
        self.sems, self.count = sems, 0

    def start(self, src, dst):
        copy = pltpu.make_async_copy(src, dst, self.sems.at[self.count])
        self.count += 1
        copy.start()
        return copy


def greet(*extra):
    barrier = pltpu.get_barrier_semaphore()
    peers = [dict(x=d) for d in STEPS] + [dict(z=d) for d in STEPS]
    peers += [dict(y=dy, c=dc) for dy, dc in SEQ_PEERS]
    for p in peers:
        pl.semaphore_signal(barrier, inc=1, device_id=shifted(**p), device_id_type=MESH)
    count = len(peers)
    for differs, device in extra:

        @pl.when(differs)
        def _(device=device):
            pl.semaphore_signal(barrier, inc=1, device_id=device, device_id_type=MESH)

        count = jnp.where(differs, count + 1, count)
    pl.semaphore_wait(barrier, count)


def group(buf, first, at, half=None, rows=None):
    span = pl.ds(0, 4) if half is None else pl.ds(2 * half, 2)
    index = (span, at) if first == "x" else (at, span)
    if rows is not None:
        index += (pl.ds(*rows),)
    return buf.at[index]


class Gather:
    def __init__(self, copies, buf, first, rows=None):
        self.copies, self.buf, self.first, self.rows = copies, buf, first, rows
        self.other = "z" if first == "x" else "x"
        x, z, _, _ = place()
        self.at = z if first == "x" else x
        self.own = buf.at[x, z] if rows is None else buf.at[x, z, pl.ds(*rows)]

    def part(self, step, half=None):
        return group(self.buf, self.first, moved(self.at, step), half, self.rows)

    def one(self, src=None):
        src = self.own if src is None else src
        self.sent = [self.copies.start(src, self.own, shifted(**{self.first: d})) for d in STEPS]
        self.all = list(self.sent)

    def two(self):
        for c in self.sent:
            c.wait_recv()
        send = lambda d, half: self.copies.start(
            self.part(0, half), self.part(0, half), shifted(**{self.other: d})
        )
        self.early = [send(1, 0), send(-1, 1)]
        self.late = [send(1, 1), send(-1, 0)]
        self.all += self.early + self.late

    def three(self):
        for c, d, half in zip(self.early, (1, -1), (0, 1)):
            c.wait_recv()
            passed = self.part(-d, half)
            self.late.append(self.copies.start(passed, passed, shifted(**{self.other: d})))
        self.all += self.late[2:]

    def done(self):
        for c in self.late:
            c.wait_recv()


def out_route(groups=16, parts=8, heads=2):
    b = lax.axis_index("batch")
    s = lax.axis_index("seq")
    to = ((b % heads) * parts + s, b // heads)
    source = (s * heads + b // parts, b % parts)
    differs = jnp.logical_or(to[0] != b, to[1] != s)
    return to, source, differs


def dot(a, b, ca=1, cb=0):
    return lax.dot_general(a, b, (((ca,), (cb,)), ((), ())), preferred_element_type=F32)


Q_AT, K_AT, V_AT, U_AT, L_AT, M_AT = 0, 256, 512, 768, 1024, 1792


def turn(v, tc, ta, tb):
    return v * tc + pltpu.roll(v, 112, 1) * ta + pltpu.roll(v, 16, 1) * tb


def project(i, F1, QK, bq, TC, TA, TB, A):
    r = pl.ds(pl.multiple_of(i * 256, 256), 256)
    two = pl.ds(2 * i, 2)
    full = dot(F1[i].reshape(256, C), QK[...].reshape(C, 768)) + bq[...]
    tc, ta, tb = TC[r], TA[r], TB[r]

    def put(at, v):
        A[two, :, at : at + 128] = v.astype(BF16).reshape(2, 128, 128)

    for at in (0, 128):
        put(Q_AT + at, turn(full[:, at : at + 128], tc, ta, tb) * SCALE)
        put(K_AT + at, turn(full[:, 256 + at : 384 + at], tc, ta, tb))
        put(V_AT + at, full[:, 512 + at : 640 + at])


def head_pass(h, A, DK, DV, TC, TA, TB, gb):
    at = h * 128

    def rows(first, count, column):
        return A[first : first + count, :, column + at : column + at + 128].reshape(count * 128, 128)

    def put(first, count, column, v):
        A[first : first + count, :, column + at : column + at + 128] = v.astype(BF16).reshape(count, 128, 128)

    for i in reversed(range(4)):
        r = pl.ds(i * 256, 256)
        m = 2 * (i + 1)
        n = 128 * m
        q, g = rows(2 * i, 2, Q_AT), rows(2 * i, 2, U_AT)
        k, v = rows(0, m, K_AT), rows(0, m, V_AT)
        s = dot(q, k, 1, 1)
        row = lax.broadcasted_iota(jnp.int32, (256, n), 0) + i * 256
        col = lax.broadcasted_iota(jnp.int32, (256, n), 1)
        s = jnp.where(row >= col, s, -1e30)
        p = jnp.exp(s - jnp.max(s, -1, keepdims=True))
        p = p * (1.0 / jnp.sum(p, -1, keepdims=True))
        p_low = p.astype(BF16)
        put(2 * i, 2, M_AT, dot(p_low, v))
        gp = dot(g, v, 1, 1)
        gs = (p * (gp - jnp.sum(p * gp, -1, keepdims=True))).astype(BF16)
        dk, dv = dot(gs, q, 0, 0), dot(p_low, g, 0, 0)
        if i == 3:
            DK[...], DV[...] = dk, dv
        else:
            DK[0:n, :] += dk
            DV[0:n, :] += dv
        gq = dot(gs, k) * SCALE
        gq = turn(gq, TC[r], -TA[r], -TB[r])
        put(2 * i, 2, L_AT, gq)
        part = jnp.sum(gq, 0, keepdims=True)
        total = part if i == 3 else total + part
    gb[:, at : at + 128] = total
    gk = turn(DK[...], TC[...], -TA[...], -TB[...])
    put(0, 8, L_AT + 256, gk)
    gb[:, 256 + at : 384 + at] = jnp.sum(gk, 0, keepdims=True)
    gv = DV[...]
    put(0, 8, L_AT + 512, gv)
    gb[:, 512 + at : 640 + at] = jnp.sum(gv, 0, keepdims=True)


def add_rows(shape, into, parts):
    slabs, rows = shape
    step = min(rows, 16)

    def add(t, _):
        i = t // (rows // step)
        r = pl.ds(pl.multiple_of(t % (rows // step) * step, step), step)
        total = parts[0](i, r).astype(F32)
        for p in parts[1:]:
            total += p(i, r).astype(F32)
        into(i, r, total)
        return 0

    lax.fori_loop(0, slabs * (rows // step), add, 0)


class Scatter:
    def __init__(self, copies, buf, pool, first, rows=None):
        self.copies, self.buf, self.first, self.rows = copies, buf, first, rows
        cut = () if rows is None else (pl.ds(*rows),)
        self.pool = pool
        self.cut = cut
        self.other = "z" if first == "x" else "x"
        x, z, _, _ = place()
        self.at, self.mine = (z, x) if first == "x" else (x, z)
        self.count = buf.shape[2] if rows is None else rows[1]
        self.base = 0 if rows is None else rows[0]

    def part(self, step, half=None):
        return group(self.buf, self.first, moved(self.at, step), half, self.rows)

    def slab(self, step, i, r):
        at = moved(self.at, step)
        r = pl.ds(self.base + r.start, r.size)
        return (i, at, r) if self.first == "x" else (at, i, r)

    def relay(self, k):
        return self.pool.at[(0, pl.ds(2 * k, 2)) + self.cut]

    def land(self, k, half):
        return self.pool.at[(1 + k, pl.ds(2 * half, 2)) + self.cut]

    def last(self, k):
        return self.pool.at[(3, k) + self.cut]

    def held(self, i, j, r):
        return self.pool[i, j, pl.ds(self.base + r.start, r.size)]

    def one(self):
        start, to = self.copies.start, self.other
        self.far = [
            start(self.part(2, k), self.relay(k), shifted(**{to: d})) for k, d in enumerate((1, -1))
        ]
        self.near = [
            start(self.part(d, 1 - k), self.land(k, 1 - k), shifted(**{to: d}))
            for k, d in enumerate((1, -1))
        ]

    def mid(self):
        for k, d in enumerate((1, -1)):
            self.far[k].wait_recv()

            def put(i, r, total, k=k, d=d):
                self.buf[self.slab(d, i + 2 * k, r)] = total.astype(self.buf.dtype)

            add_rows(
                (2, self.count),
                put,
                [lambda i, r, k=k, d=d: self.buf[self.slab(d, i + 2 * k, r)],
                 lambda i, r, k=k: self.held(0, 2 * k + i, r)],
            )
            self.near.append(
                self.copies.start(
                    self.part(d, k), self.land(k, k), shifted(**{self.other: d})
                )
            )

    def two(self):
        for cp in self.near:
            cp.wait_recv()

        def put(i, r, total):
            self.buf[self.slab(0, i, r)] = total.astype(self.buf.dtype)

        add_rows(
            (4, self.count),
            put,
            [lambda i, r: self.buf[self.slab(0, i, r)],
             lambda i, r: self.held(1, i, r), lambda i, r: self.held(2, i, r)],
        )
        x, z, _, _ = place()
        self.sent = []
        for k, d in enumerate(STEPS):
            there = moved(self.mine, d)
            index = (there, self.at) if self.first == "x" else (self.at, there)
            if self.rows is not None:
                index += (pl.ds(*self.rows),)
            self.sent.append(
                self.copies.start(self.buf.at[index], self.last(k), shifted(**{self.first: d}))
            )

    def three(self, put):
        for cp in self.sent:
            cp.wait_recv()
        add_rows(
            (1, self.count),
            lambda i, r, total: put(r, total),
            [lambda i, r: self.buf[self.slab(0, self.mine, r)]]
            + [lambda i, r, k=k: self.held(3, k, r) for k in range(3)],
        )


class SeqScatter:
    def __init__(self, copies, buf, pool):
        self.copies, self.buf, self.pool = copies, buf, pool
        _, _, self.y, self.c = place()

    def one(self):
        self.sent = self.copies.start(self.buf.at[:, 1 - self.c], self.pool.at[pl.ds(0, 4)], shifted(c=1))

    def two(self):
        self.sent.wait_recv()
        buf, c = self.buf, self.c

        def put(i, r, total):
            buf[i, c, r] = total.astype(BF16)

        add_rows((4, 128), put, [lambda i, r: buf[i, c, r], lambda i, r: self.pool[i, r]])
        start = self.copies.start
        far = moved(self.y, 2)
        halves = (pl.ds(0, 64), pl.ds(64, 64))
        self.far = [
            start(buf.at[far, c, halves[k]], self.pool.at[4, halves[k]], shifted(y=d)) for k, d in enumerate((1, -1))
        ]
        self.near = [
            start(buf.at[moved(self.y, d), c, halves[1 - k]], self.pool.at[5 + k, halves[1 - k]], shifted(y=d))
            for k, d in enumerate((1, -1))
        ]

    def mid(self):
        buf, c = self.buf, self.c
        for k, d in enumerate((1, -1)):
            self.far[k].wait_recv()
            to = moved(self.y, d)

            def rows(r, k=k):
                return pl.ds(64 * k + r.start, r.size)

            def put(i, r, total, rows=rows, to=to):
                buf[to, c, rows(r)] = total.astype(BF16)

            add_rows(
                (1, 64),
                put,
                [lambda i, r, rows=rows, to=to: buf[to, c, rows(r)],
                 lambda i, r, rows=rows: self.pool[4, rows(r)]],
            )
            self.near.append(
                self.copies.start(
                    buf.at[to, c, pl.ds(64 * k, 64)], self.pool.at[5 + k, pl.ds(64 * k, 64)], shifted(y=d)
                )
            )

    def three(self, put):
        for cp in self.near:
            cp.wait_recv()
        buf, y, c = self.buf, self.y, self.c
        add_rows(
            (1, 128),
            lambda i, r, total: put(r, total),
            [lambda i, r: buf[y, c, r], lambda i, r: self.pool[5, r], lambda i, r: self.pool[6, r]],
        )


def layer_kernel(x_ref, g_ref, pos_ref, freq_ref, bo_ref, bd_ref, ga_ref, sa_ref, gm_ref, sm_ref, bq_ref, bu_ref,
                 up_ref, qkv_ref, down_ref, out_ref,
                 y_out, x_out, gd_out, gu_all, gq_all, go_all, sv,
                 X, G, SA, RA, SM, UP, QK, DN, WO, F1, F2, NB, ACT, GHL, GQ, GO, GD, GU, PP,
                 DK, DV, TC, TA, TB,
                 BQ, VT, v_land, CT, CP, vec, gsum, gbu, gbq, go_part,
                 send, recv, ready, loc):
    copies, local = Copies(send, recv), Locals(loc)
    x, z, y, c = place()
    s = y * 2 + c
    b_me = lax.axis_index("batch")
    to, source, differs = out_route()
    loads = [
        local.start(qkv_ref.at[:, pl.ds(C * p, C)], F1.at[0, 0, pl.ds(16 * p, 16)]) for p in range(3)
    ]
    x_load = local.start(x_ref, X.at[y, c])
    up_loads = [
        local.start(up_ref.at[:, pl.ds(C * p, C)], F2.at[0, 0, pl.ds(16 * p, 16)]) for p in range(4)
    ]
    down_load = local.start(down_ref, DN.at[x, z])
    g_load = local.start(g_ref, G.at[y, c])
    greet((differs, source), (differs, to))
    xz_peers = [shifted(**{a: d}) for a in ("x", "z") for d in STEPS]
    y_peers = [shifted(c=1)] + [shifted(y=d) for d in (1, -1)]

    def tell(k, peers):
        for p in peers:
            pl.semaphore_signal(ready.at[k], inc=1, device_id=p, device_id_type=MESH)

    def hear(k, peers):
        pl.semaphore_wait(ready.at[k], len(peers))

    def sent(group):
        for cp in group:
            cp.wait_send()
        copies.made = [cp for cp in copies.made if all(cp is not m for m in group)]

    down = [Gather(copies, DN, "x", (0, 32)), Gather(copies, DN, "z", (32, 32))]
    for g in down:
        g.one(down_ref.at[pl.ds(*g.rows)])

    def across(src, width, dst):
        def piece(k):
            return src.at[pl.ds(pl.multiple_of(k * 16, 16), 16), pl.ds(0, width)]

        dst[...] = piece(s)[...]
        return [
            copies.start(piece(moved(y, dy) * 2 + lax.rem(c + dc, 2)), dst, shifted(y=dy, c=dc))
            for dy, dc in SEQ_PEERS
        ]

    rows16 = pl.ds(pl.multiple_of(s * 16, 16), 16)
    for cp in loads:
        cp.wait()
    for k in range(8):
        for part in range(3):
            GHL[16 * k : 16 * (k + 1), 256 * part : 256 * (part + 1)] = (
                F1[0, 0, 16 * part : 16 * (part + 1), 256 * k : 256 * (k + 1)]
            )
    qk = across(GHL, 768, QK.at[x, z, rows16])
    out_copy = copies.make(out_ref, WO.at[to[0] // 4, to[0] % 4], to)

    @pl.when(differs)
    def _():
        out_copy.start()

    out_load = pltpu.make_async_copy(out_ref, WO.at[x, z], loc.at[15])

    @pl.when(jnp.logical_not(differs))
    def _():
        out_load.start()

    def placed(ref, width, at):
        v = jnp.concatenate([ref[...].astype(F32), jnp.zeros((1, width - ref.shape[1]), F32)], 1)
        return pltpu.roll(jnp.broadcast_to(v, (8, width)), at, 1)[0:1]

    vec[16:32, 0:128] = jnp.zeros((16, 128), F32)
    for k, ref in enumerate((bo_ref, bd_ref, ga_ref, sa_ref, gm_ref, sm_ref)):
        vec[16 + k : 17 + k, 0:128] = placed(ref, 128, s * 16)
    wide = placed(bq_ref, 384, s * 48)
    for k in range(3):
        vec[22 + k : 23 + k, 0:128] = wide[:, 128 * k : 128 * (k + 1)]
    vec[25:26, 0:128] = placed(bu_ref, 128, b_me % 2 * 64)
    SA[s] = vec[16:32, 0:128].astype(BF16)
    sm = [copies.start(SA.at[s], SA.at[s], shifted(y=dy, c=dc)) for dy, dc in SEQ_PEERS]

    def seq_one(src, dst):
        own = dst.at[y, c]
        return [copies.start(src, own, shifted(y=d)) for d in (1, -1)] + [
            copies.start(src, own, shifted(c=1))
        ]

    def seq_two(sent, dst):
        more = []
        for cp, d in zip(sent[:2], (1, -1)):
            cp.wait_recv()
            got = dst.at[moved(y, -d), c]
            more.append(copies.start(got, got, shifted(c=1)))
        up_way = c == 0
        got = dst.at[jnp.where(up_way, moved(y, -1), moved(y, 1)), c]
        py = jnp.where(up_way, moved(y, 1), moved(y, -1))
        fwd = copies.start(got, got, (b_me, py * 2 + c))
        sent[2].wait_recv()
        return more, fwd

    def seq_three(more, fwd, dst):
        fwd.wait_recv()
        got = dst.at[moved(y, 2), c]
        return more + [copies.start(got, got, shifted(c=1))]

    xs = seq_one(x_ref, X)
    angle = pos_ref[...].astype(F32) * freq_ref[...]
    RA[s, 0:16, :] = jnp.cos(angle)
    RA[s, 16:32, :] = jnp.sin(angle)
    ra = [copies.start(RA.at[s], RA.at[s], shifted(y=dy, c=dc)) for dy, dc in SEQ_PEERS]
    for cp in up_loads:
        cp.wait()
    lane = lax.broadcasted_iota(jnp.int32, (16, 128), 1)
    for k in range(8):
        for p in range(8):
            at = (8 * p + k // 2) * 128
            r, at = 16 * (at // C), at % C
            one = F2[0, 0, r : r + 16, at : at + 128].astype(F32)
            two = F2[0, 0, r : r + 16, at + 512 : at + 640].astype(F32)
            if k % 2 == 0:
                two = pltpu.roll(two, 64, 1)
            else:
                one = pltpu.roll(one, 64, 1)
            ACT[16 * k : 16 * (k + 1), 128 * p : 128 * (p + 1)] = jnp.where(lane < 64, one, two).astype(BF16)
    up = across(ACT, 1024, UP.at[x, z, rows16])

    for cp in qk:
        cp.wait_recv()
    qa = Gather(copies, QK, "x", (0, 48))
    qb = Gather(copies, QK, "z", (48, 80))
    qa.one()
    qb.one()

    @pl.when(differs)
    def _():
        out_copy.wait()

    @pl.when(jnp.logical_not(differs))
    def _():
        out_load.wait()

    wo = Gather(copies, WO, "x")
    wo.one()
    for cp in sm:
        cp.wait_recv()
    total = SA[0].astype(F32)
    for k in range(1, 8):
        total += SA[k].astype(F32)
    row = lax.broadcasted_iota(jnp.int32, (16, 128), 0)
    SM[x, z] = jnp.where(row == 9, SA[s].astype(F32), total).astype(BF16)
    small = Gather(copies, SM, "z")
    small.one()
    g_load.wait()
    total = jnp.zeros((1, C), F32)
    for k in range(8):
        total += jnp.sum(G[y, c, 16 * k : 16 * (k + 1)].astype(F32), 0, keepdims=True)
    gsum[...] = total
    qa.two()
    qb.two()
    small.two()
    wo.two()
    xs2, xf = seq_two(xs, X)
    gs = seq_one(g_ref, G)
    small.three()
    qa.three()
    qb.three()
    for cp in up:
        cp.wait_recv()
    upg = [Gather(copies, UP, "x", (0, 64)), Gather(copies, UP, "z", (64, 64))]
    for g in upg:
        g.one()
    wo.three()
    down_load.wait()
    for g in down:
        g.two()
    small.done()
    for i in range(4):
        for j in range(4):
            b = i * 4 + j
            tile = SM[i, j].astype(F32)
            vec[0:6, b * 128 : (b + 1) * 128] = tile[0:6]
            for k in range(3):
                BQ[3 * b + k : 3 * b + k + 1, :] = tile[6 + k : 7 + k]
            if b % 2 == 0:
                kept = tile[9:10]
            else:
                vec[6:7, b // 2 * 128 : (b // 2 + 1) * 128] = kept + tile[9:10]

    def norm(ky, kc):
        def step(t, _):
            r = pl.ds(pl.multiple_of(t * 16, 16), 16)
            v = X[ky, kc, r].astype(F32)
            v = v - jnp.mean(v, -1, keepdims=True)
            n = v * lax.rsqrt(jnp.mean(v * v, -1, keepdims=True) + EPS)
            NB[ky * 2 + kc, r] = n.astype(BF16)
            F1[ky, kc, r] = (n * vec[2:3, :] + vec[3:4, :]).astype(BF16)
            F2[ky, kc, r] = (n * vec[4:5, :] + vec[5:6, :]).astype(BF16)
            return 0

        lax.fori_loop(0, 8, step, 0)

    x_load.wait()
    norm(y, c)
    norm(y, 1 - c)
    norm(moved(y, -1), c)
    norm(moved(y, 1), c)
    xs3 = seq_three(xs2, xf, X)
    xs3[0].wait_recv()
    norm(moved(y, -1), 1 - c)
    xs3[1].wait_recv()
    norm(moved(y, 1), 1 - c)
    gs2, gf = seq_two(gs, G)
    norm(moved(y, 2), c)
    xs3[2].wait_recv()
    norm(moved(y, 2), 1 - c)
    for cp in ra:
        cp.wait_recv()

    lane = lax.broadcasted_iota(jnp.int32, (128, 128), 1)
    for k in range(8):
        r = pl.ds(k * 128, 128)
        tile = jnp.concatenate([RA[k], jnp.zeros((96, 128), F32)], 0).T
        TC[r] = jnp.where(lane < 16, tile, jnp.where(lane < 32, pltpu.roll(tile, 16, 1), 1.0))
        TA[r] = jnp.where(lane < 16, -pltpu.roll(tile, 112, 1), 0.0)
        TB[r] = jnp.where((lane >= 16) & (lane < 32), tile, 0.0)
    for gth in (qa, qb):
        gth.done()
    for part in range(3):
        pair = BQ[pl.ds(part * 16 + s * 2, 2), :]
        for k in range(2):
            at = part * 256 + k * 128
            vec[9:10, at : at + 128] = pair[k : k + 1]

    def first(i, _):
        project(i, F1, QK, vec.at[9:10, 0:768], TC, TA, TB, PP)
        return 0

    lax.fori_loop(0, 4, first, 0)
    for g in upg:
        g.two()
    gs3 = seq_three(gs2, gf, G)
    wo.done()
    for cp in gs3:
        cp.wait_recv()

    def mixed(i, _):
        total = dot(G[i].reshape(256, C), WO[...].reshape(256, C), 1, 1)
        PP[pl.ds(2 * i, 2), :, U_AT:L_AT] = total.astype(BF16).reshape(2, 128, 256)
        return 0

    lax.fori_loop(0, 4, mixed, 0)
    for g in down:
        g.three()
    for h in range(2):
        head_pass(h, PP, DK, DV, TC, TA, TB, gbq)
    for g in upg:
        g.three()

    def grad_out(j, _):
        q = pl.ds(pl.multiple_of(j * 1024, 1024), 1024)
        mix = PP[:, :, M_AT:].reshape(1024, 256)
        GO[:, :, :, q] = dot(mix, G[:, :, :, q].reshape(1024, 1024), 0, 0).astype(BF16).reshape(4, 4, 16, 1024)
        return 0

    lax.fori_loop(0, 2, grad_out, 0)

    def grad_qkv(i, _):
        r = pl.ds(pl.multiple_of(i * 512, 512), 512)
        right = PP[:, :, L_AT:M_AT].reshape(1024, 768)
        GQ[i] = dot(F1[:, :, :, r].reshape(1024, 512), right, 0, 0).astype(BF16).reshape(4, 128, 768)
        return 0

    lax.fori_loop(0, 4, grad_qkv, 0)
    sent(xs + xs2 + [xf, xs3[2]])

    def attend(t, _):
        i, j = t // 2, t % 2
        q = pl.ds(pl.multiple_of(j * 1024, 1024), 1024)
        mix = PP[pl.ds(4 * i, 4), :, M_AT:].reshape(512, 256)
        total = dot(mix, WO[:, :, :, q].reshape(256, 1024))
        X[pl.ds(2 * i, 2), :, :, q] = total.astype(BF16).reshape(2, 2, 128, 1024)
        return 0

    lax.fori_loop(0, 4, attend, 0)
    vec[10:12, :] = jnp.zeros((2, C), F32)

    def grad_first(t, _):
        i, j = t // 4, t % 4
        q = pl.ds(pl.multiple_of(j * 512, 512), 512)
        left = PP[pl.ds(2 * i, 2), :, L_AT:M_AT].reshape(256, 768)
        u = dot(left, QK[j].reshape(512, 768), 1, 1)
        n = NB[pl.ds(2 * i, 2), :, q].reshape(256, 512).astype(F32)
        vec[10:11, q] += jnp.sum(u * n, 0, keepdims=True)
        vec[11:12, q] += jnp.sum(u, 0, keepdims=True)
        F1[i, :, :, q] = (u * vec[2:3, q]).astype(BF16).reshape(2, 128, 512)
        return 0

    lax.fori_loop(0, 16, grad_first, 0)

    for g in (qa, qb, wo):
        sent(g.all)
    sent(qk + up)
    tell(0, xz_peers)
    tell(4, y_peers)

    sa = Scatter(copies, GQ, QK, "x", (0, 48))
    sb = Scatter(copies, GQ, QK, "z", (48, 80))
    so = Scatter(copies, GO, WO, "x")
    fp = SeqScatter(copies, X, PP)
    fq = SeqScatter(copies, F1, NB)
    gbu[...] = jnp.zeros_like(gbu)
    hear(0, xz_peers)
    for g in (sa, sb, so):
        g.one()
    for g in down + upg:
        g.done()

    def hidden(t, _):
        i, j = t // 2, t % 2
        r = pl.ds(pl.multiple_of(i * 256, 256), 256)
        q = pl.ds(pl.multiple_of(j * 512, 512), 512)
        h = dot(F2[i].reshape(256, C), UP[:, :, :, q].reshape(C, 512)) + vec[6:7, q]
        ga = dot(G[i].reshape(256, C), DN[pl.ds(2 * j, 2)].reshape(512, C), 1, 1)
        cdf = 0.5 + 0.5 * lax.erf(h * (0.5**0.5))
        ACT[r, q] = (h * cdf).astype(BF16)
        gh = ga * (cdf + h * (jnp.exp(h * h * -0.5) * 0.3989422804014327))
        gbu[:, q] += jnp.sum(gh, 0, keepdims=True)
        GHL[r, q] = gh.astype(BF16)
        return 0

    lax.fori_loop(0, 8, hidden, 0)
    for g in (sa, sb, so):
        g.mid()

    def feed(t, _):
        i, j = t // 4, t % 4
        r = pl.ds(pl.multiple_of(i * 512, 512), 512)
        q = pl.ds(pl.multiple_of(j * 512, 512), 512)
        two = pl.ds(2 * i, 2)
        total = dot(ACT[r], DN[:, :, :, q].reshape(1024, 512)) + X[two, :, :, q].reshape(512, 512).astype(F32)
        X[two, :, :, q] = total.astype(BF16).reshape(2, 2, 128, 512)
        return 0

    lax.fori_loop(0, 8, feed, 0)
    hear(4, y_peers)
    fp.one()
    for g in down:
        sent(g.all)
    tell(1, xz_peers)

    sd = [Scatter(copies, GD, DN, "x", (0, 32)), Scatter(copies, GD, DN, "z", (32, 32))]
    su = [Scatter(copies, GU, UP, "x", (0, 64)), Scatter(copies, GU, UP, "z", (64, 64))]
    sc = Scatter(copies, CT, CP, "z")

    def grad_down(t, _):
        i, j = t // 2, t % 2
        u = pl.ds(pl.multiple_of(i * 256, 256), 256)
        q = pl.ds(pl.multiple_of(j * 1024, 1024), 1024)
        right = G[:, :, :, q].reshape(1024, 1024)
        GD[i, :, :, q] = dot(ACT[:, u], right, 0, 0).astype(BF16).reshape(4, 64, 1024)
        return 0

    lax.fori_loop(0, 8, grad_down, 0)
    sent(gs3 + [gf])
    again = [local.start(x_ref, G.at[0, 0]), local.start(g_ref, G.at[0, 1])]
    hear(1, xz_peers)
    for g in sd:
        g.one()
    for g in (sa, sb, so):
        g.two()
    fp.two()
    vec[12:14, :] = jnp.zeros((2, C), F32)

    def second(t, _):
        i, j = t // 4, t % 4
        r = pl.ds(pl.multiple_of(i * 256, 256), 256)
        q = pl.ds(pl.multiple_of(j * 512, 512), 512)
        u = dot(GHL[r], UP[j].reshape(512, 1024), 1, 1)
        n = NB[pl.ds(2 * i, 2), :, q].reshape(256, 512).astype(F32)
        vec[12:13, q] += jnp.sum(u * n, 0, keepdims=True)
        vec[13:14, q] += jnp.sum(u, 0, keepdims=True)
        total = u * vec[4:5, q] + F1[i, :, :, q].reshape(256, 512).astype(F32)
        F1[i, :, :, q] = total.astype(BF16).reshape(2, 128, 512)
        return 0

    lax.fori_loop(0, 16, second, 0)
    for g in upg:
        sent(g.all)
    tell(2, xz_peers)
    tell(3, y_peers)

    def grad_up(t, _):
        i, j = t // 2, t % 2
        r = pl.ds(pl.multiple_of(i * 512, 512), 512)
        q = pl.ds(pl.multiple_of(j * 512, 512), 512)
        left = F2[:, :, :, r].reshape(1024, 512)
        GU[i, :, :, q] = dot(left, GHL[:, q], 0, 0).astype(BF16).reshape(4, 128, 512)
        return 0

    lax.fori_loop(0, 8, grad_up, 0)
    hear(2, xz_peers)
    for g in su:
        g.one()
    hear(3, y_peers)
    fq.one()

    BQ[...] = jnp.zeros_like(BQ)
    for part in range(3):
        for k in range(2):
            at = part * 256 + k * 128
            BQ[pl.ds(part * 16 + s * 2 + k, 1), :] = gbq[:, at : at + 128]
    for b in range(16):
        at = b * 128
        VT[b, 0:1, :] = gsum[:, at : at + 128]
        VT[b, 1:5, :] = vec[10:14, at : at + 128]
        VT[b, 5:8, :] = BQ[3 * b : 3 * b + 3, :]
    vs = [
        copies.start(VT, v_land.at[k], shifted(y=dy, c=dc)) for k, (dy, dc) in enumerate(SEQ_PEERS)
    ]
    for g in sd:
        g.mid()
    fp.mid()

    def store(ref, base=0):
        def put(r, total):
            ref[pl.ds(base + r.start, r.size)] = total.astype(ref.dtype)

        return put

    gu_part = ACT.at[pl.ds(0, 128)]
    gq_part = ACT.at[pl.ds(128, 128), pl.ds(0, 768)]

    def spread(part, out):
        out[s] = part[pl.ds(pl.multiple_of(s * 16, 16), 16)]
        made = []
        for dy, dc in SEQ_PEERS:
            peer = moved(y, dy) * 2 + lax.rem(c + dc, 2)
            made.append(
                copies.start(
                    part.at[pl.ds(pl.multiple_of(peer * 16, 16), 16)], out.at[s], shifted(y=dy, c=dc)
                )
            )
        return made

    fq.two()
    sa.three(store(gq_part))
    sb.three(store(gq_part, 48))
    backs = spread(gq_part, gq_all)
    so.three(store(go_part))
    out_back = copies.make(go_part, go_all, source)

    @pl.when(differs)
    def _():
        out_back.start()

    @pl.when(jnp.logical_not(differs))
    def _():
        go_all[...] = go_part[...]

    for cp in vs:
        cp.wait_recv()
    for b in range(16):
        total = VT[b]
        for k in range(7):
            total += v_land[k, b]
        CT[b // 4, b % 4, 0:8, :] = total
        CT[b // 4, b % 4, 8:9, :] = gbu[:, b // 2 * 128 : b // 2 * 128 + 128]
        CT[b // 4, b % 4, 9:16, :] = jnp.zeros((7, 128), F32)
    sc.one()
    for g in su:
        g.mid()
    for g in sd:
        g.two()
    fq.mid()
    sc.mid()

    def layer_out(r, total):
        bias = vec[0:1, :] + vec[1:2, :]
        y_out[r] = (G[0, 0, r].astype(F32) + total + bias).astype(BF16)

    for cp in again:
        cp.wait()
    fp.three(layer_out)
    sc.two()
    for g in su:
        g.two()
    for k, g in enumerate(sd):
        g.three(store(gd_out, 32 * k))

    def grad_in(r, total):
        v = G[0, 0, r].astype(F32)
        v = v - jnp.mean(v, -1, keepdims=True)
        inv = lax.rsqrt(jnp.mean(v * v, -1, keepdims=True) + EPS)
        n = v * inv
        total = total - jnp.mean(total, -1, keepdims=True) - n * jnp.mean(total * n, -1, keepdims=True)
        x_out[r] = (G[0, 1, r].astype(F32) + total * inv).astype(BF16)

    fq.three(grad_in)
    for k, g in enumerate(su):
        g.three(store(gu_part, 64 * k))
    backs += spread(gu_part, gu_all)
    sc.three(store(sv))

    @pl.when(differs)
    def _():
        out_back.wait()

    for cp in backs:
        cp.wait_recv()
    copies.drain()


def layer(x, g, pos, freq, vectors, up, qkv, down, out):
    any_ = pl.BlockSpec(memory_space=pl.ANY)
    vm = pl.BlockSpec(memory_space=pltpu.VMEM)
    n_up, n_qkv = up.shape[-1] // 8, qkv.shape[-1] // 8
    up_all, qk_all = (4, 4, 128, n_up), (4, 4, 128, n_qkv)
    dn_all, wo_all = (4, 4) + down.shape, (4, 4) + out.shape
    blocks, unit = (4, 2, 128, C), (1024, n_up)
    S = pltpu.VMEM
    scratch = [
        (blocks, BF16), (blocks, BF16), ((8, 16, 128), BF16), ((8, 32, 128), F32), ((4, 4, 16, 128), BF16),
        (up_all, BF16), (qk_all, BF16), (dn_all, BF16), (wo_all, BF16),
        (blocks, BF16), (blocks, BF16), ((8, 128, C), BF16), (unit, BF16), (unit, BF16),
        (qk_all, BF16), (wo_all, BF16), (dn_all, BF16), (up_all, BF16), ((8, 128, C), BF16),
        ((1024, HD), F32), ((1024, HD), F32), ((1024, HD), F32), ((1024, HD), F32), ((1024, HD), F32),
        ((48, 128), F32), ((16, 8, 128), F32), ((7, 16, 8, 128), F32), ((4, 4, 16, 128), F32), ((4, 4, 16, 128), F32),
        ((32, C), F32), ((1, C), F32), ((1, n_up), F32), ((1, n_qkv), F32),
        (out.shape, BF16),
    ]
    outs = [
        (x.shape, BF16), (x.shape, BF16), (down.shape, F32),
        ((8, 16, n_up), BF16), ((8, 16, n_qkv), BF16), (out.shape, BF16), ((16, 128), F32),
    ]
    return pl.pallas_call(
        layer_kernel,
        out_shape=[jax.ShapeDtypeStruct(*o) for o in outs],
        in_specs=[any_, any_] + [vm] * 10 + [any_] * 4,
        out_specs=[vm] * 7,
        scratch_shapes=[S(*h) for h in scratch]
        + [pltpu.SemaphoreType.DMA((230,)), pltpu.SemaphoreType.DMA((230,)), pltpu.SemaphoreType.REGULAR((5,)), pltpu.SemaphoreType.DMA((16,))],
        compiler_params=pltpu.CompilerParams(
            collective_id=1, has_side_effects=True, vmem_limit_bytes=64 * 2**20 - 2**16
        ),
    )(x, g, pos, freq, *vectors, up, qkv, down, out)


def finish_kernel(y_in, x_in, gd_in, gu_in, gq_in, go_in, sv,
                  y_out, x_out, gd, gu, gq, go, b_out, b_down, ga, sa, gm, sm, bq, bu):
    s = lax.axis_index("seq")
    b = lax.axis_index("batch")
    y_out[...] = y_in[...]
    x_out[...] = x_in[...]
    gd[...] = gd_in[...]
    go[...] = go_in[...].astype(F32)
    for k in range(8):
        for part in range(3):
            piece = gq_in[k, :, 256 * part : 256 * (part + 1)]
            gq[:, C * part + 256 * k : C * part + 256 * (k + 1)] = piece.astype(F32)
    lane = lax.broadcasted_iota(jnp.int32, (16, 128), 1)
    for j in range(4):
        for p in range(8):
            one = gu_in[2 * j, :, 128 * p : 128 * (p + 1)].astype(F32)
            two = gu_in[2 * j + 1, :, 128 * p : 128 * (p + 1)].astype(F32)
            at = (8 * p + j) * 128
            gu[:, at : at + 128] = jnp.where(lane < 64, one, pltpu.roll(two, 64, 1))
            gu[:, at + 512 : at + 640] = jnp.where(lane < 64, pltpu.roll(one, 64, 1), two)
    mine = pltpu.roll(sv[...], lax.rem(128 - s * 16, 128), 1)
    for k, ref in enumerate((b_out, ga, sa, gm, sm)):
        ref[...] = mine[k : k + 1, 0:16]
    b_down[...] = mine[0:1, 0:16]
    wide = jnp.concatenate([jnp.broadcast_to(sv[k : k + 1, :], (8, 128)) for k in (5, 6, 7)], 1)
    bq[...] = pltpu.roll(wide, lax.rem(384 - s * 48, 384), 1)[0:1, 0:48]
    tail = pltpu.roll(sv[8:16, :], lax.rem(b, 2) * 64, 1)
    bu[...] = tail[0:1, 0:64]


def finish(*parts):
    vm = pl.BlockSpec(memory_space=pltpu.VMEM)
    y, xg, gd, gu, gq, go, _ = parts
    outs = [(y.shape, BF16), (xg.shape, BF16), (gd.shape, F32), ((16, 8 * gu.shape[-1]), F32), ((16, 8 * gq.shape[-1]), F32), (go.shape, F32)]
    outs += [((1, 16), F32)] * 6 + [((1, 48), F32), ((1, 64), F32)]
    return pl.pallas_call(
        finish_kernel,
        out_shape=[jax.ShapeDtypeStruct(*o) for o in outs],
        in_specs=[vm] * 7,
        out_specs=[vm] * len(outs),
    )(*parts)


def shards(
    inputs,
    positions,
    w_qkv,
    b_qkv,
    w_out,
    b_out,
    w_up,
    b_up,
    w_down,
    b_down,
    gain_attn,
    shift_attn,
    gain_mlp,
    shift_mlp,
    grad_out,
):
    half_rot = ROT // 2
    exponent = jnp.arange(half_rot).astype(F32) / half_rot
    frequency = jnp.broadcast_to(jnp.power(10000.0, -exponent)[:, None], (half_rot, 128))
    vectors = [
        v[None] for v in (b_out, b_down, gain_attn, shift_attn, gain_mlp, shift_mlp, b_qkv, b_up)
    ]
    parts = layer(inputs[0], grad_out[0], positions, frequency, vectors, w_up, w_qkv, w_down, w_out)
    layer_out, grad_in, g_down, g_up, g_qkv, g_out, *rest = finish(*parts)
    g_b_out, g_b_down, g_gain_a, g_shift_a, g_gain_m, g_shift_m, g_b_qkv, g_b_up = [v[0] for v in rest]
    return (
        layer_out[None],
        grad_in[None],
        g_qkv,
        g_b_qkv,
        g_out,
        g_b_out,
        g_up,
        g_b_up,
        g_down,
        g_b_down,
        g_gain_a,
        g_shift_a,
        g_gain_m,
        g_shift_m,
    )


def solution(mesh):
    both = ("batch", "seq")
    rows = P("batch", "seq", None)
    matrix = P(both, None)
    vector = P(both)
    return jax.shard_map(
        shards,
        mesh=mesh,
        in_specs=(
            rows,
            P("batch", "seq"),
            matrix,
            vector,
            matrix,
            vector,
            matrix,
            vector,
            matrix,
            vector,
            vector,
            vector,
            vector,
            vector,
            rows,
        ),
        out_specs=(
            rows,
            rows,
            matrix,
            vector,
            matrix,
            vector,
            matrix,
            vector,
            matrix,
            vector,
            vector,
            vector,
            vector,
            vector,
        ),
        check_vma=False,
    )
```

```python
import jax
import jax.numpy as jnp
from jax import lax
from jax.experimental import pallas as pl
from jax.experimental.pallas import tpu as pltpu
from jax.sharding import PartitionSpec as P

H = 16
HD = 128
ROT = 32
EPS = 1e-05
C = 2048
SCALE = HD ** (-0.5)
F32 = jnp.float32
BF16 = jnp.bfloat16
MESH = pl.DeviceIdType.MESH
STEPS = (1, -1, 2)
SEQ_PEERS = [(dy, dc) for dc in (1, 0) for dy in (0, 1, -1, 2) if (dy, dc) != (0, 0)]


def place():
    b = lax.axis_index("batch")
    s = lax.axis_index("seq")
    return b // 4, b % 4, s // 2, s % 2


def shifted(x=0, z=0, y=0, c=0):
    px, pz, py, pc = place()
    px = lax.rem(px + x + 4, 4)
    pz = lax.rem(pz + z + 4, 4)
    py = lax.rem(py + y + 4, 4)
    pc = lax.rem(pc + c, 2)
    return (px * 4 + pz, py * 2 + pc)


def moved(pos, step):
    return lax.rem(pos + step + 4, 4)


class Copies:
    def __init__(self, send, recv):
        self.send, self.recv, self.count, self.made = send, recv, 0, []

    def make(self, src, dst, device):
        k = self.count
        self.count += 1
        return pltpu.make_async_remote_copy(
            src_ref=src,
            dst_ref=dst,
            send_sem=self.send.at[k],
            recv_sem=self.recv.at[k],
            device_id=device,
            device_id_type=MESH,
        )

    def start(self, src, dst, device):
        copy = self.make(src, dst, device)
        copy.start()
        self.made.append(copy)
        return copy

    def drain(self):
        for copy in self.made:
            copy.wait_send()


class Locals:
    def __init__(self, sems):
        self.sems, self.count = sems, 0

    def start(self, src, dst):
        copy = pltpu.make_async_copy(src, dst, self.sems.at[self.count])
        self.count += 1
        copy.start()
        return copy


def greet(*extra):
    barrier = pltpu.get_barrier_semaphore()
    peers = [dict(x=d) for d in STEPS] + [dict(z=d) for d in STEPS]
    peers += [dict(y=dy, c=dc) for dy, dc in SEQ_PEERS]
    for p in peers:
        pl.semaphore_signal(barrier, inc=1, device_id=shifted(**p), device_id_type=MESH)
    count = len(peers)
    for differs, device in extra:

        @pl.when(differs)
        def _(device=device):
            pl.semaphore_signal(barrier, inc=1, device_id=device, device_id_type=MESH)

        count = jnp.where(differs, count + 1, count)
    pl.semaphore_wait(barrier, count)


def group(buf, first, at, half=None, rows=None):
    span = pl.ds(0, 4) if half is None else pl.ds(2 * half, 2)
    index = (span, at) if first == "x" else (at, span)
    if rows is not None:
        index += (pl.ds(*rows),)
    return buf.at[index]


class Gather:
    def __init__(self, copies, buf, first, rows=None):
        self.copies, self.buf, self.first, self.rows = copies, buf, first, rows
        self.other = "z" if first == "x" else "x"
        x, z, _, _ = place()
        self.at = z if first == "x" else x
        self.own = buf.at[x, z] if rows is None else buf.at[x, z, pl.ds(*rows)]

    def part(self, step, half=None):
        return group(self.buf, self.first, moved(self.at, step), half, self.rows)

    def one(self, src=None):
        src = self.own if src is None else src
        self.sent = [self.copies.start(src, self.own, shifted(**{self.first: d})) for d in STEPS]
        self.all = list(self.sent)

    def two(self):
        for c in self.sent:
            c.wait_recv()
        send = lambda d, half: self.copies.start(
            self.part(0, half), self.part(0, half), shifted(**{self.other: d})
        )
        self.early = [send(1, 0), send(-1, 1)]
        self.late = [send(1, 1), send(-1, 0)]
        self.all += self.early + self.late

    def three(self):
        for c, d, half in zip(self.early, (1, -1), (0, 1)):
            c.wait_recv()
            passed = self.part(-d, half)
            self.late.append(self.copies.start(passed, passed, shifted(**{self.other: d})))
        self.all += self.late[2:]

    def done(self):
        for c in self.late:
            c.wait_recv()


def out_route(groups=16, parts=8, heads=2):
    b = lax.axis_index("batch")
    s = lax.axis_index("seq")
    to = ((b % heads) * parts + s, b // heads)
    source = (s * heads + b // parts, b % parts)
    differs = jnp.logical_or(to[0] != b, to[1] != s)
    return to, source, differs


def dot(a, b, ca=1, cb=0):
    return lax.dot_general(a, b, (((ca,), (cb,)), ((), ())), preferred_element_type=F32)


Q_AT, K_AT, V_AT, U_AT, L_AT, M_AT = 0, 256, 512, 768, 1024, 1792


def turn(v, tc, ta, tb):
    return v * tc + pltpu.roll(v, 112, 1) * ta + pltpu.roll(v, 16, 1) * tb


def project(i, F1, QK, bq, TC, TA, TB, A):
    r = pl.ds(pl.multiple_of(i * 256, 256), 256)
    two = pl.ds(2 * i, 2)
    full = dot(F1[i].reshape(256, C), QK[...].reshape(C, 768)) + bq[...]
    tc, ta, tb = TC[r], TA[r], TB[r]

    def put(at, v):
        A[two, :, at : at + 128] = v.astype(BF16).reshape(2, 128, 128)

    for at in (0, 128):
        put(Q_AT + at, turn(full[:, at : at + 128], tc, ta, tb) * SCALE)
        put(K_AT + at, turn(full[:, 256 + at : 384 + at], tc, ta, tb))
        put(V_AT + at, full[:, 512 + at : 640 + at])


def head_pass(h, A, DK, DV, TC, TA, TB, gb):
    at = h * 128

    def rows(first, count, column):
        return A[first : first + count, :, column + at : column + at + 128].reshape(count * 128, 128)

    def put(first, count, column, v):
        A[first : first + count, :, column + at : column + at + 128] = v.astype(BF16).reshape(count, 128, 128)

    for i in reversed(range(4)):
        r = pl.ds(i * 256, 256)
        m = 2 * (i + 1)
        n = 128 * m
        q, g = rows(2 * i, 2, Q_AT), rows(2 * i, 2, U_AT)
        k, v = rows(0, m, K_AT), rows(0, m, V_AT)
        s = dot(q, k, 1, 1)
        row = lax.broadcasted_iota(jnp.int32, (256, n), 0) + i * 256
        col = lax.broadcasted_iota(jnp.int32, (256, n), 1)
        s = jnp.where(row >= col, s, -1e30)
        p = jnp.exp(s - jnp.max(s, -1, keepdims=True))
        p = p * (1.0 / jnp.sum(p, -1, keepdims=True))
        p_low = p.astype(BF16)
        put(2 * i, 2, M_AT, dot(p_low, v))
        gp = dot(g, v, 1, 1)
        gs = (p * (gp - jnp.sum(p * gp, -1, keepdims=True))).astype(BF16)
        dk, dv = dot(gs, q, 0, 0), dot(p_low, g, 0, 0)
        if i == 3:
            DK[...], DV[...] = dk, dv
        else:
            DK[0:n, :] += dk
            DV[0:n, :] += dv
        gq = dot(gs, k) * SCALE
        gq = turn(gq, TC[r], -TA[r], -TB[r])
        put(2 * i, 2, L_AT, gq)
        part = jnp.sum(gq, 0, keepdims=True)
        total = part if i == 3 else total + part
    gb[:, at : at + 128] = total
    gk = turn(DK[...], TC[...], -TA[...], -TB[...])
    put(0, 8, L_AT + 256, gk)
    gb[:, 256 + at : 384 + at] = jnp.sum(gk, 0, keepdims=True)
    gv = DV[...]
    put(0, 8, L_AT + 512, gv)
    gb[:, 512 + at : 640 + at] = jnp.sum(gv, 0, keepdims=True)


def add_rows(shape, into, parts):
    slabs, rows = shape
    step = min(rows, 16)

    def add(t, _):
        i = t // (rows // step)
        r = pl.ds(pl.multiple_of(t % (rows // step) * step, step), step)
        total = parts[0](i, r).astype(F32)
        for p in parts[1:]:
            total += p(i, r).astype(F32)
        into(i, r, total)
        return 0

    lax.fori_loop(0, slabs * (rows // step), add, 0)


class Scatter:
    def __init__(self, copies, buf, pool, first, rows=None):
        self.copies, self.buf, self.first, self.rows = copies, buf, first, rows
        cut = () if rows is None else (pl.ds(*rows),)
        self.pool = pool
        self.cut = cut
        self.other = "z" if first == "x" else "x"
        x, z, _, _ = place()
        self.at, self.mine = (z, x) if first == "x" else (x, z)
        self.count = buf.shape[2] if rows is None else rows[1]
        self.base = 0 if rows is None else rows[0]

    def part(self, step, half=None):
        return group(self.buf, self.first, moved(self.at, step), half, self.rows)

    def slab(self, step, i, r):
        at = moved(self.at, step)
        r = pl.ds(self.base + r.start, r.size)
        return (i, at, r) if self.first == "x" else (at, i, r)

    def relay(self, k):
        return self.pool.at[(0, pl.ds(2 * k, 2)) + self.cut]

    def land(self, k, half):
        return self.pool.at[(1 + k, pl.ds(2 * half, 2)) + self.cut]

    def last(self, k):
        return self.pool.at[(3, k) + self.cut]

    def held(self, i, j, r):
        return self.pool[i, j, pl.ds(self.base + r.start, r.size)]

    def one(self):
        start, to = self.copies.start, self.other
        self.far = [
            start(self.part(2, k), self.relay(k), shifted(**{to: d})) for k, d in enumerate((1, -1))
        ]
        self.near = [
            start(self.part(d, 1 - k), self.land(k, 1 - k), shifted(**{to: d}))
            for k, d in enumerate((1, -1))
        ]

    def mid(self):
        for k, d in enumerate((1, -1)):
            self.far[k].wait_recv()

            def put(i, r, total, k=k, d=d):
                self.buf[self.slab(d, i + 2 * k, r)] = total.astype(self.buf.dtype)

            add_rows(
                (2, self.count),
                put,
                [lambda i, r, k=k, d=d: self.buf[self.slab(d, i + 2 * k, r)],
                 lambda i, r, k=k: self.held(0, 2 * k + i, r)],
            )
            self.near.append(
                self.copies.start(
                    self.part(d, k), self.land(k, k), shifted(**{self.other: d})
                )
            )

    def two(self):
        for cp in self.near:
            cp.wait_recv()

        def put(i, r, total):
            self.buf[self.slab(0, i, r)] = total.astype(self.buf.dtype)

        add_rows(
            (4, self.count),
            put,
            [lambda i, r: self.buf[self.slab(0, i, r)],
             lambda i, r: self.held(1, i, r), lambda i, r: self.held(2, i, r)],
        )
        x, z, _, _ = place()
        self.sent = []
        for k, d in enumerate(STEPS):
            there = moved(self.mine, d)
            index = (there, self.at) if self.first == "x" else (self.at, there)
            if self.rows is not None:
                index += (pl.ds(*self.rows),)
            self.sent.append(
                self.copies.start(self.buf.at[index], self.last(k), shifted(**{self.first: d}))
            )

    def three(self, put):
        for cp in self.sent:
            cp.wait_recv()
        add_rows(
            (1, self.count),
            lambda i, r, total: put(r, total),
            [lambda i, r: self.buf[self.slab(0, self.mine, r)]]
            + [lambda i, r, k=k: self.held(3, k, r) for k in range(3)],
        )


class SeqScatter:
    def __init__(self, copies, buf, pool):
        self.copies, self.buf, self.pool = copies, buf, pool
        _, _, self.y, self.c = place()

    def one(self):
        self.sent = self.copies.start(self.buf.at[:, 1 - self.c], self.pool.at[pl.ds(0, 4)], shifted(c=1))

    def two(self):
        self.sent.wait_recv()
        buf, c = self.buf, self.c

        def put(i, r, total):
            buf[i, c, r] = total.astype(BF16)

        add_rows((4, 128), put, [lambda i, r: buf[i, c, r], lambda i, r: self.pool[i, r]])
        start = self.copies.start
        far = moved(self.y, 2)
        halves = (pl.ds(0, 64), pl.ds(64, 64))
        self.far = [
            start(buf.at[far, c, halves[k]], self.pool.at[4, halves[k]], shifted(y=d)) for k, d in enumerate((1, -1))
        ]
        self.near = [
            start(buf.at[moved(self.y, d), c, halves[1 - k]], self.pool.at[5 + k, halves[1 - k]], shifted(y=d))
            for k, d in enumerate((1, -1))
        ]

    def mid(self):
        buf, c = self.buf, self.c
        for k, d in enumerate((1, -1)):
            self.far[k].wait_recv()
            to = moved(self.y, d)

            def rows(r, k=k):
                return pl.ds(64 * k + r.start, r.size)

            def put(i, r, total, rows=rows, to=to):
                buf[to, c, rows(r)] = total.astype(BF16)

            add_rows(
                (1, 64),
                put,
                [lambda i, r, rows=rows, to=to: buf[to, c, rows(r)],
                 lambda i, r, rows=rows: self.pool[4, rows(r)]],
            )
            self.near.append(
                self.copies.start(
                    buf.at[to, c, pl.ds(64 * k, 64)], self.pool.at[5 + k, pl.ds(64 * k, 64)], shifted(y=d)
                )
            )

    def three(self, put):
        for cp in self.near:
            cp.wait_recv()
        buf, y, c = self.buf, self.y, self.c
        add_rows(
            (1, 128),
            lambda i, r, total: put(r, total),
            [lambda i, r: buf[y, c, r], lambda i, r: self.pool[5, r], lambda i, r: self.pool[6, r]],
        )


def layer_kernel(x_ref, g_ref, pos_ref, freq_ref, bo_ref, bd_ref, ga_ref, sa_ref, gm_ref, sm_ref, bq_ref, bu_ref,
                 up_ref, qkv_ref, down_ref, out_ref,
                 y_out, x_out, gd_out, gu_all, gq_all, go_all, sv,
                 X, G, SA, RA, SM, UP, QK, DN, WO, F1, F2, NB, ACT, GHL, GQ, GO, GD, GU, PP,
                 DK, DV, TC, TA, TB,
                 BQ, VT, v_land, CT, CP, vec, gsum, gbu, gbq, go_part,
                 send, recv, ready, loc):
    copies, local = Copies(send, recv), Locals(loc)
    x, z, y, c = place()
    s = y * 2 + c
    b_me = lax.axis_index("batch")
    to, source, differs = out_route()
    loads = [
        local.start(qkv_ref.at[:, pl.ds(C * p, C)], F1.at[0, 0, pl.ds(16 * p, 16)]) for p in range(3)
    ]
    x_load = local.start(x_ref, X.at[y, c])
    up_loads = [
        local.start(up_ref.at[:, pl.ds(C * p, C)], F2.at[0, 0, pl.ds(16 * p, 16)]) for p in range(4)
    ]
    down_load = local.start(down_ref, DN.at[x, z])
    g_load = local.start(g_ref, G.at[y, c])
    greet((differs, source), (differs, to))
    xz_peers = [shifted(**{a: d}) for a in ("x", "z") for d in STEPS]
    y_peers = [shifted(c=1)] + [shifted(y=d) for d in (1, -1)]

    def tell(k, peers):
        for p in peers:
            pl.semaphore_signal(ready.at[k], inc=1, device_id=p, device_id_type=MESH)

    def hear(k, peers):
        pl.semaphore_wait(ready.at[k], len(peers))

    def sent(group):
        for cp in group:
            cp.wait_send()
        copies.made = [cp for cp in copies.made if all(cp is not m for m in group)]

    down = [Gather(copies, DN, "x", (0, 32)), Gather(copies, DN, "z", (32, 32))]
    for g in down:
        g.one(down_ref.at[pl.ds(*g.rows)])

    def across(src, width, dst):
        def piece(k):
            return src.at[pl.ds(pl.multiple_of(k * 16, 16), 16), pl.ds(0, width)]

        dst[...] = piece(s)[...]
        return [
            copies.start(piece(moved(y, dy) * 2 + lax.rem(c + dc, 2)), dst, shifted(y=dy, c=dc))
            for dy, dc in SEQ_PEERS
        ]

    rows16 = pl.ds(pl.multiple_of(s * 16, 16), 16)
    for cp in loads:
        cp.wait()
    for k in range(8):
        for part in range(3):
            GHL[16 * k : 16 * (k + 1), 256 * part : 256 * (part + 1)] = (
                F1[0, 0, 16 * part : 16 * (part + 1), 256 * k : 256 * (k + 1)]
            )
    qk = across(GHL, 768, QK.at[x, z, rows16])
    out_copy = copies.make(out_ref, WO.at[to[0] // 4, to[0] % 4], to)

    @pl.when(differs)
    def _():
        out_copy.start()

    out_load = pltpu.make_async_copy(out_ref, WO.at[x, z], loc.at[15])

    @pl.when(jnp.logical_not(differs))
    def _():
        out_load.start()

    def placed(ref, width, at):
        v = jnp.concatenate([ref[...].astype(F32), jnp.zeros((1, width - ref.shape[1]), F32)], 1)
        return pltpu.roll(jnp.broadcast_to(v, (8, width)), at, 1)[0:1]

    vec[16:32, 0:128] = jnp.zeros((16, 128), F32)
    for k, ref in enumerate((bo_ref, bd_ref, ga_ref, sa_ref, gm_ref, sm_ref)):
        vec[16 + k : 17 + k, 0:128] = placed(ref, 128, s * 16)
    wide = placed(bq_ref, 384, s * 48)
    for k in range(3):
        vec[22 + k : 23 + k, 0:128] = wide[:, 128 * k : 128 * (k + 1)]
    vec[25:26, 0:128] = placed(bu_ref, 128, b_me % 2 * 64)
    SA[s] = vec[16:32, 0:128].astype(BF16)
    sm = [copies.start(SA.at[s], SA.at[s], shifted(y=dy, c=dc)) for dy, dc in SEQ_PEERS]

    def seq_one(src, dst):
        own = dst.at[y, c]
        return [copies.start(src, own, shifted(y=d)) for d in (1, -1)] + [
            copies.start(src, own, shifted(c=1))
        ]

    def seq_two(sent, dst):
        more = []
        for cp, d in zip(sent[:2], (1, -1)):
            cp.wait_recv()
            got = dst.at[moved(y, -d), c]
            more.append(copies.start(got, got, shifted(c=1)))
        up_way = c == 0
        got = dst.at[jnp.where(up_way, moved(y, -1), moved(y, 1)), c]
        py = jnp.where(up_way, moved(y, 1), moved(y, -1))
        fwd = copies.start(got, got, (b_me, py * 2 + c))
        sent[2].wait_recv()
        return more, fwd

    def seq_three(more, fwd, dst):
        fwd.wait_recv()
        got = dst.at[moved(y, 2), c]
        return more + [copies.start(got, got, shifted(c=1))]

    xs = seq_one(x_ref, X)
    angle = pos_ref[...].astype(F32) * freq_ref[...]
    RA[s, 0:16, :] = jnp.cos(angle)
    RA[s, 16:32, :] = jnp.sin(angle)
    ra = [copies.start(RA.at[s], RA.at[s], shifted(y=dy, c=dc)) for dy, dc in SEQ_PEERS]
    for cp in up_loads:
        cp.wait()
    lane = lax.broadcasted_iota(jnp.int32, (16, 128), 1)
    for k in range(8):
        for p in range(8):
            at = (8 * p + k // 2) * 128
            r, at = 16 * (at // C), at % C
            one = F2[0, 0, r : r + 16, at : at + 128].astype(F32)
            two = F2[0, 0, r : r + 16, at + 512 : at + 640].astype(F32)
            if k % 2 == 0:
                two = pltpu.roll(two, 64, 1)
            else:
                one = pltpu.roll(one, 64, 1)
            ACT[16 * k : 16 * (k + 1), 128 * p : 128 * (p + 1)] = jnp.where(lane < 64, one, two).astype(BF16)
    up = across(ACT, 1024, UP.at[x, z, rows16])

    for cp in qk:
        cp.wait_recv()
    qa = Gather(copies, QK, "x", (0, 48))
    qb = Gather(copies, QK, "z", (48, 80))
    qa.one()
    qb.one()

    @pl.when(differs)
    def _():
        out_copy.wait()

    @pl.when(jnp.logical_not(differs))
    def _():
        out_load.wait()

    wo = Gather(copies, WO, "x")
    wo.one()
    for cp in sm:
        cp.wait_recv()
    total = SA[0].astype(F32)
    for k in range(1, 8):
        total += SA[k].astype(F32)
    row = lax.broadcasted_iota(jnp.int32, (16, 128), 0)
    SM[x, z] = jnp.where(row == 9, SA[s].astype(F32), total).astype(BF16)
    small = Gather(copies, SM, "z")
    small.one()
    g_load.wait()
    total = jnp.zeros((1, C), F32)
    for k in range(8):
        total += jnp.sum(G[y, c, 16 * k : 16 * (k + 1)].astype(F32), 0, keepdims=True)
    gsum[...] = total
    qa.two()
    qb.two()
    small.two()
    wo.two()
    xs2, xf = seq_two(xs, X)
    gs = seq_one(g_ref, G)
    small.three()
    qa.three()
    qb.three()
    for cp in up:
        cp.wait_recv()
    upg = [Gather(copies, UP, "x", (0, 64)), Gather(copies, UP, "z", (64, 64))]
    for g in upg:
        g.one()
    wo.three()
    down_load.wait()
    for g in down:
        g.two()
    small.done()
    for i in range(4):
        for j in range(4):
            b = i * 4 + j
            tile = SM[i, j].astype(F32)
            vec[0:6, b * 128 : (b + 1) * 128] = tile[0:6]
            for k in range(3):
                BQ[3 * b + k : 3 * b + k + 1, :] = tile[6 + k : 7 + k]
            if b % 2 == 0:
                kept = tile[9:10]
            else:
                vec[6:7, b // 2 * 128 : (b // 2 + 1) * 128] = kept + tile[9:10]

    def norm(ky, kc):
        def step(t, _):
            r = pl.ds(pl.multiple_of(t * 16, 16), 16)
            v = X[ky, kc, r].astype(F32)
            v = v - jnp.mean(v, -1, keepdims=True)
            n = v * lax.rsqrt(jnp.mean(v * v, -1, keepdims=True) + EPS)
            NB[ky * 2 + kc, r] = n.astype(BF16)
            F1[ky, kc, r] = (n * vec[2:3, :] + vec[3:4, :]).astype(BF16)
            F2[ky, 2 * kc + t // 4, pl.ds(pl.multiple_of(t % 4 * 16, 16), 16)] = (
                n * vec[4:5, :] + vec[5:6, :]
            ).astype(BF16)
            return 0

        lax.fori_loop(0, 8, step, 0)

    x_load.wait()
    norm(y, c)
    norm(y, 1 - c)
    norm(moved(y, -1), c)
    norm(moved(y, 1), c)
    xs3 = seq_three(xs2, xf, X)
    xs3[0].wait_recv()
    norm(moved(y, -1), 1 - c)
    xs3[1].wait_recv()
    norm(moved(y, 1), 1 - c)
    gs2, gf = seq_two(gs, G)
    norm(moved(y, 2), c)
    xs3[2].wait_recv()
    norm(moved(y, 2), 1 - c)
    for cp in ra:
        cp.wait_recv()

    lane = lax.broadcasted_iota(jnp.int32, (128, 128), 1)
    for k in range(8):
        r = pl.ds(k * 128, 128)
        tile = jnp.concatenate([RA[k], jnp.zeros((96, 128), F32)], 0).T
        TC[r] = jnp.where(lane < 16, tile, jnp.where(lane < 32, pltpu.roll(tile, 16, 1), 1.0))
        TA[r] = jnp.where(lane < 16, -pltpu.roll(tile, 112, 1), 0.0)
        TB[r] = jnp.where((lane >= 16) & (lane < 32), tile, 0.0)
    for gth in (qa, qb):
        gth.done()
    for part in range(3):
        pair = BQ[pl.ds(part * 16 + s * 2, 2), :]
        for k in range(2):
            at = part * 256 + k * 128
            vec[9:10, at : at + 128] = pair[k : k + 1]

    def first(i, _):
        project(i, F1, QK, vec.at[9:10, 0:768], TC, TA, TB, PP)
        return 0

    lax.fori_loop(0, 4, first, 0)
    for g in upg:
        g.two()
    gs3 = seq_three(gs2, gf, G)
    wo.done()
    for cp in gs3:
        cp.wait_recv()

    def mixed(i, _):
        total = dot(G[i].reshape(256, C), WO[...].reshape(256, C), 1, 1)
        PP[pl.ds(2 * i, 2), :, U_AT:L_AT] = total.astype(BF16).reshape(2, 128, 256)
        return 0

    lax.fori_loop(0, 4, mixed, 0)
    for g in down:
        g.three()
    for h in range(2):
        head_pass(h, PP, DK, DV, TC, TA, TB, gbq)
    for g in upg:
        g.three()

    def grad_out(j, _):
        q = pl.ds(pl.multiple_of(j * 1024, 1024), 1024)
        mix = PP[:, :, M_AT:].reshape(1024, 256)
        GO[:, :, :, q] = dot(mix, G[:, :, :, q].reshape(1024, 1024), 0, 0).astype(BF16).reshape(4, 4, 16, 1024)
        return 0

    lax.fori_loop(0, 2, grad_out, 0)

    def grad_qkv(i, _):
        r = pl.ds(pl.multiple_of(i * 512, 512), 512)
        right = PP[:, :, L_AT:M_AT].reshape(1024, 768)
        GQ[i] = dot(F1[:, :, :, r].reshape(1024, 512), right, 0, 0).astype(BF16).reshape(4, 128, 768)
        return 0

    lax.fori_loop(0, 4, grad_qkv, 0)
    sent(xs + xs2 + [xf, xs3[2]])

    def attend(t, _):
        i, j = t // 2, t % 2
        q = pl.ds(pl.multiple_of(j * 1024, 1024), 1024)
        mix = PP[pl.ds(4 * i, 4), :, M_AT:].reshape(512, 256)
        total = dot(mix, WO[:, :, :, q].reshape(256, 1024))
        X[pl.ds(2 * i, 2), :, :, q] = total.astype(BF16).reshape(2, 2, 128, 1024)
        return 0

    lax.fori_loop(0, 4, attend, 0)
    vec[10:12, :] = jnp.zeros((2, C), F32)

    def grad_first(t, _):
        i, j = t // 4, t % 4
        q = pl.ds(pl.multiple_of(j * 512, 512), 512)
        left = PP[pl.ds(2 * i, 2), :, L_AT:M_AT].reshape(256, 768)
        u = dot(left, QK[j].reshape(512, 768), 1, 1)
        n = NB[pl.ds(2 * i, 2), :, q].reshape(256, 512).astype(F32)
        vec[10:11, q] += jnp.sum(u * n, 0, keepdims=True)
        vec[11:12, q] += jnp.sum(u, 0, keepdims=True)
        F1[i, :, :, q] = (u * vec[2:3, q]).astype(BF16).reshape(2, 128, 512)
        return 0

    lax.fori_loop(0, 16, grad_first, 0)

    for g in (qa, qb, wo):
        sent(g.all)
    sent(qk + up)
    tell(0, xz_peers)
    tell(4, y_peers)

    sa = Scatter(copies, GQ, QK, "x", (0, 48))
    sb = Scatter(copies, GQ, QK, "z", (48, 80))
    so = Scatter(copies, GO, WO, "x")
    fp = SeqScatter(copies, X, PP)
    fq = SeqScatter(copies, F1, NB)
    gbu[...] = jnp.zeros_like(gbu)
    hear(0, xz_peers)
    for g in (sa, sb, so):
        g.one()
    for g in down + upg:
        g.done()

    def hidden(t, _):
        i, j = t // 2, t % 2
        r = pl.ds(pl.multiple_of(i * 256, 256), 256)
        q = pl.ds(pl.multiple_of(j * 512, 512), 512)
        h = dot(F2[i].reshape(256, C), UP[:, :, :, q].reshape(C, 512)) + vec[6:7, q]
        ga = dot(G[i].reshape(256, C), DN[pl.ds(2 * j, 2)].reshape(512, C), 1, 1)
        cdf = 0.5 + 0.5 * lax.erf(h * (0.5**0.5))
        ACT[r, q] = (h * cdf).astype(BF16)
        gh = ga * (cdf + h * (jnp.exp(h * h * -0.5) * 0.3989422804014327))
        gbu[:, q] += jnp.sum(gh, 0, keepdims=True)
        GHL[r, q] = gh.astype(BF16)
        return 0

    lax.fori_loop(0, 8, hidden, 0)
    for g in (sa, sb, so):
        g.mid()

    sd = [Scatter(copies, GD, F2, "x", (0, 32)), Scatter(copies, GD, F2, "z", (32, 32))]
    su = [Scatter(copies, GU, UP, "x", (0, 64)), Scatter(copies, GU, UP, "z", (64, 64))]
    sc = Scatter(copies, CT, CP, "z")
    vec[12:14, :] = jnp.zeros((2, C), F32)

    def second(t, _):
        i, j = t // 4, t % 4
        r = pl.ds(pl.multiple_of(i * 256, 256), 256)
        q = pl.ds(pl.multiple_of(j * 512, 512), 512)
        u = dot(GHL[r], UP[j].reshape(512, 1024), 1, 1)
        n = NB[pl.ds(2 * i, 2), :, q].reshape(256, 512).astype(F32)
        vec[12:13, q] += jnp.sum(u * n, 0, keepdims=True)
        vec[13:14, q] += jnp.sum(u, 0, keepdims=True)
        total = u * vec[4:5, q] + F1[i, :, :, q].reshape(256, 512).astype(F32)
        F1[i, :, :, q] = total.astype(BF16).reshape(2, 128, 512)
        return 0

    lax.fori_loop(0, 16, second, 0)
    for g in upg:
        sent(g.all)
    tell(2, xz_peers)
    tell(3, y_peers)

    def grad_up(t, _):
        i, j = t // 2, t % 2
        r = pl.ds(pl.multiple_of(i * 512, 512), 512)
        q = pl.ds(pl.multiple_of(j * 512, 512), 512)
        left = F2[:, :, :, r].reshape(1024, 512)
        GU[i, :, :, q] = dot(left, GHL[:, q], 0, 0).astype(BF16).reshape(4, 128, 512)
        return 0

    lax.fori_loop(0, 8, grad_up, 0)
    tell(1, xz_peers)
    hear(3, y_peers)
    fq.one()
    hear(2, xz_peers)
    for g in su:
        g.one()

    def grad_down(t, _):
        i, j = t // 2, t % 2
        u = pl.ds(pl.multiple_of(i * 256, 256), 256)
        q = pl.ds(pl.multiple_of(j * 1024, 1024), 1024)
        right = G[:, :, :, q].reshape(1024, 1024)
        GD[i, :, :, q] = dot(ACT[:, u], right, 0, 0).astype(BF16).reshape(4, 64, 1024)
        return 0

    lax.fori_loop(0, 8, grad_down, 0)
    hear(1, xz_peers)
    for g in sd:
        g.one()
    fq.two()
    sent(gs3 + [gf])
    again = [local.start(x_ref, G.at[0, 0]), local.start(g_ref, G.at[0, 1])]

    BQ[...] = jnp.zeros_like(BQ)
    for part in range(3):
        for k in range(2):
            at = part * 256 + k * 128
            BQ[pl.ds(part * 16 + s * 2 + k, 1), :] = gbq[:, at : at + 128]
    for b in range(16):
        at = b * 128
        VT[b, 0:1, :] = gsum[:, at : at + 128]
        VT[b, 1:5, :] = vec[10:14, at : at + 128]
        VT[b, 5:8, :] = BQ[3 * b : 3 * b + 3, :]
    vs = [
        copies.start(VT, v_land.at[k], shifted(y=dy, c=dc)) for k, (dy, dc) in enumerate(SEQ_PEERS)
    ]
    def feed(t, _):
        i, j = t // 4, t % 4
        r = pl.ds(pl.multiple_of(i * 512, 512), 512)
        q = pl.ds(pl.multiple_of(j * 512, 512), 512)
        two = pl.ds(2 * i, 2)
        total = dot(ACT[r], DN[:, :, :, q].reshape(1024, 512)) + X[two, :, :, q].reshape(512, 512).astype(F32)
        X[two, :, :, q] = total.astype(BF16).reshape(2, 2, 128, 512)
        return 0

    lax.fori_loop(0, 8, feed, 0)
    hear(4, y_peers)
    fp.one()
    for g in (sa, sb, so):
        g.two()
    for g in su:
        g.mid()
    fq.mid()
    fp.two()

    for cp in vs:
        cp.wait_recv()
    for b in range(16):
        total = VT[b]
        for k in range(7):
            total += v_land[k, b]
        CT[b // 4, b % 4, 0:8, :] = total
        CT[b // 4, b % 4, 8:9, :] = gbu[:, b // 2 * 128 : b // 2 * 128 + 128]
        CT[b // 4, b % 4, 9:16, :] = jnp.zeros((7, 128), F32)
    sc.one()

    def store(ref, base=0):
        def put(r, total):
            ref[pl.ds(base + r.start, r.size)] = total.astype(ref.dtype)

        return put

    gu_part = ACT.at[pl.ds(0, 128)]
    gq_part = ACT.at[pl.ds(128, 128), pl.ds(0, 768)]

    def spread(part, out):
        out[s] = part[pl.ds(pl.multiple_of(s * 16, 16), 16)]
        made = []
        for dy, dc in SEQ_PEERS:
            peer = moved(y, dy) * 2 + lax.rem(c + dc, 2)
            made.append(
                copies.start(
                    part.at[pl.ds(pl.multiple_of(peer * 16, 16), 16)], out.at[s], shifted(y=dy, c=dc)
                )
            )
        return made

    sa.three(store(gq_part))
    sb.three(store(gq_part, 48))
    backs = spread(gq_part, gq_all)
    so.three(store(go_part))
    out_back = copies.make(go_part, go_all, source)

    @pl.when(differs)
    def _():
        out_back.start()

    @pl.when(jnp.logical_not(differs))
    def _():
        go_all[...] = go_part[...]

    for g in sd:
        g.mid()
    sc.mid()
    for g in su:
        g.two()
    fp.mid()
    for cp in again:
        cp.wait()

    def grad_in(r, total):
        v = G[0, 0, r].astype(F32)
        v = v - jnp.mean(v, -1, keepdims=True)
        inv = lax.rsqrt(jnp.mean(v * v, -1, keepdims=True) + EPS)
        n = v * inv
        total = total - jnp.mean(total, -1, keepdims=True) - n * jnp.mean(total * n, -1, keepdims=True)
        x_out[r] = (G[0, 1, r].astype(F32) + total * inv).astype(BF16)

    fq.three(grad_in)
    sc.two()
    for k, g in enumerate(su):
        g.three(store(gu_part, 64 * k))
    backs += spread(gu_part, gu_all)
    for g in sd:
        g.two()

    def layer_out(r, total):
        bias = vec[0:1, :] + vec[1:2, :]
        y_out[r] = (G[0, 0, r].astype(F32) + total + bias).astype(BF16)

    fp.three(layer_out)
    sc.three(store(sv))
    for k, g in enumerate(sd):
        g.three(store(gd_out, 32 * k))

    @pl.when(differs)
    def _():
        out_back.wait()

    for cp in backs:
        cp.wait_recv()
    copies.drain()


def layer(x, g, pos, freq, vectors, up, qkv, down, out):
    any_ = pl.BlockSpec(memory_space=pl.ANY)
    vm = pl.BlockSpec(memory_space=pltpu.VMEM)
    n_up, n_qkv = up.shape[-1] // 8, qkv.shape[-1] // 8
    up_all, qk_all = (4, 4, 128, n_up), (4, 4, 128, n_qkv)
    dn_all, wo_all = (4, 4) + down.shape, (4, 4) + out.shape
    blocks, unit = (4, 2, 128, C), (1024, n_up)
    S = pltpu.VMEM
    scratch = [
        (blocks, BF16), (blocks, BF16), ((8, 16, 128), BF16), ((8, 32, 128), F32), ((4, 4, 16, 128), BF16),
        (up_all, BF16), (qk_all, BF16), (dn_all, BF16), (wo_all, BF16),
        (blocks, BF16), ((4, 4, 64, C), BF16), ((8, 128, C), BF16), (unit, BF16), (unit, BF16),
        (qk_all, BF16), (wo_all, BF16), (dn_all, BF16), (up_all, BF16), ((8, 128, C), BF16),
        ((1024, HD), F32), ((1024, HD), F32), ((1024, HD), F32), ((1024, HD), F32), ((1024, HD), F32),
        ((48, 128), F32), ((16, 8, 128), F32), ((7, 16, 8, 128), F32), ((4, 4, 16, 128), F32), ((4, 4, 16, 128), F32),
        ((32, C), F32), ((1, C), F32), ((1, n_up), F32), ((1, n_qkv), F32),
        (out.shape, BF16),
    ]
    outs = [
        (x.shape, BF16), (x.shape, BF16), (down.shape, F32),
        ((8, 16, n_up), BF16), ((8, 16, n_qkv), BF16), (out.shape, BF16), ((16, 128), F32),
    ]
    return pl.pallas_call(
        layer_kernel,
        out_shape=[jax.ShapeDtypeStruct(*o) for o in outs],
        in_specs=[any_, any_] + [vm] * 10 + [any_] * 4,
        out_specs=[vm] * 7,
        scratch_shapes=[S(*h) for h in scratch]
        + [pltpu.SemaphoreType.DMA((230,)), pltpu.SemaphoreType.DMA((230,)), pltpu.SemaphoreType.REGULAR((5,)), pltpu.SemaphoreType.DMA((16,))],
        compiler_params=pltpu.CompilerParams(
            collective_id=1, has_side_effects=True, vmem_limit_bytes=64 * 2**20 - 2**16
        ),
    )(x, g, pos, freq, *vectors, up, qkv, down, out)


def finish_kernel(y_in, x_in, gd_in, gu_in, gq_in, go_in, sv,
                  y_out, x_out, gd, gu, gq, go, b_out, b_down, ga, sa, gm, sm, bq, bu):
    s = lax.axis_index("seq")
    b = lax.axis_index("batch")
    y_out[...] = y_in[...]
    x_out[...] = x_in[...]
    gd[...] = gd_in[...]
    go[...] = go_in[...].astype(F32)
    for k in range(8):
        for part in range(3):
            piece = gq_in[k, :, 256 * part : 256 * (part + 1)]
            gq[:, C * part + 256 * k : C * part + 256 * (k + 1)] = piece.astype(F32)
    lane = lax.broadcasted_iota(jnp.int32, (16, 128), 1)
    for j in range(4):
        for p in range(8):
            one = gu_in[2 * j, :, 128 * p : 128 * (p + 1)].astype(F32)
            two = gu_in[2 * j + 1, :, 128 * p : 128 * (p + 1)].astype(F32)
            at = (8 * p + j) * 128
            gu[:, at : at + 128] = jnp.where(lane < 64, one, pltpu.roll(two, 64, 1))
            gu[:, at + 512 : at + 640] = jnp.where(lane < 64, pltpu.roll(one, 64, 1), two)
    mine = pltpu.roll(sv[...], lax.rem(128 - s * 16, 128), 1)
    for k, ref in enumerate((b_out, ga, sa, gm, sm)):
        ref[...] = mine[k : k + 1, 0:16]
    b_down[...] = mine[0:1, 0:16]
    wide = jnp.concatenate([jnp.broadcast_to(sv[k : k + 1, :], (8, 128)) for k in (5, 6, 7)], 1)
    bq[...] = pltpu.roll(wide, lax.rem(384 - s * 48, 384), 1)[0:1, 0:48]
    tail = pltpu.roll(sv[8:16, :], lax.rem(b, 2) * 64, 1)
    bu[...] = tail[0:1, 0:64]


def finish(*parts):
    vm = pl.BlockSpec(memory_space=pltpu.VMEM)
    y, xg, gd, gu, gq, go, _ = parts
    outs = [(y.shape, BF16), (xg.shape, BF16), (gd.shape, F32), ((16, 8 * gu.shape[-1]), F32), ((16, 8 * gq.shape[-1]), F32), (go.shape, F32)]
    outs += [((1, 16), F32)] * 6 + [((1, 48), F32), ((1, 64), F32)]
    return pl.pallas_call(
        finish_kernel,
        out_shape=[jax.ShapeDtypeStruct(*o) for o in outs],
        in_specs=[vm] * 7,
        out_specs=[vm] * len(outs),
    )(*parts)


def shards(
    inputs,
    positions,
    w_qkv,
    b_qkv,
    w_out,
    b_out,
    w_up,
    b_up,
    w_down,
    b_down,
    gain_attn,
    shift_attn,
    gain_mlp,
    shift_mlp,
    grad_out,
):
    half_rot = ROT // 2
    exponent = jnp.arange(half_rot).astype(F32) / half_rot
    frequency = jnp.broadcast_to(jnp.power(10000.0, -exponent)[:, None], (half_rot, 128))
    vectors = [
        v[None] for v in (b_out, b_down, gain_attn, shift_attn, gain_mlp, shift_mlp, b_qkv, b_up)
    ]
    parts = layer(inputs[0], grad_out[0], positions, frequency, vectors, w_up, w_qkv, w_down, w_out)
    layer_out, grad_in, g_down, g_up, g_qkv, g_out, *rest = finish(*parts)
    g_b_out, g_b_down, g_gain_a, g_shift_a, g_gain_m, g_shift_m, g_b_qkv, g_b_up = [v[0] for v in rest]
    return (
        layer_out[None],
        grad_in[None],
        g_qkv,
        g_b_qkv,
        g_out,
        g_b_out,
        g_up,
        g_b_up,
        g_down,
        g_b_down,
        g_gain_a,
        g_shift_a,
        g_gain_m,
        g_shift_m,
    )


def solution(mesh):
    both = ("batch", "seq")
    rows = P("batch", "seq", None)
    matrix = P(both, None)
    vector = P(both)
    return jax.shard_map(
        shards,
        mesh=mesh,
        in_specs=(
            rows,
            P("batch", "seq"),
            matrix,
            vector,
            matrix,
            vector,
            matrix,
            vector,
            matrix,
            vector,
            vector,
            vector,
            vector,
            vector,
            rows,
        ),
        out_specs=(
            rows,
            rows,
            matrix,
            vector,
            matrix,
            vector,
            matrix,
            vector,
            matrix,
            vector,
            vector,
            vector,
            vector,
            vector,
        ),
        check_vma=False,
    )
```

```python
import jax
import jax.numpy as jnp
from jax import lax
from jax.experimental import pallas as pl
from jax.experimental.pallas import tpu as pltpu
from jax.sharding import PartitionSpec as P

H = 16
HD = 128
ROT = 32
EPS = 1e-05
C = 2048
SCALE = HD ** (-0.5)
F32 = jnp.float32
BF16 = jnp.bfloat16
MESH = pl.DeviceIdType.MESH
STEPS = (1, -1, 2)
SEQ_PEERS = [(dy, dc) for dc in (1, 0) for dy in (0, 1, -1, 2) if (dy, dc) != (0, 0)]


def place():
    b = lax.axis_index("batch")
    s = lax.axis_index("seq")
    return b // 4, b % 4, s // 2, s % 2


def shifted(x=0, z=0, y=0, c=0):
    px, pz, py, pc = place()
    px = lax.rem(px + x + 4, 4)
    pz = lax.rem(pz + z + 4, 4)
    py = lax.rem(py + y + 4, 4)
    pc = lax.rem(pc + c, 2)
    return (px * 4 + pz, py * 2 + pc)


def moved(pos, step):
    return lax.rem(pos + step + 4, 4)


class Copies:
    def __init__(self, send, recv):
        self.send, self.recv, self.count, self.made = send, recv, 0, []

    def make(self, src, dst, device):
        k = self.count
        self.count += 1
        return pltpu.make_async_remote_copy(
            src_ref=src,
            dst_ref=dst,
            send_sem=self.send.at[k],
            recv_sem=self.recv.at[k],
            device_id=device,
            device_id_type=MESH,
        )

    def start(self, src, dst, device):
        copy = self.make(src, dst, device)
        copy.start()
        self.made.append(copy)
        return copy

    def drain(self):
        for copy in self.made:
            copy.wait_send()


class Locals:
    def __init__(self, sems):
        self.sems, self.count = sems, 0

    def start(self, src, dst):
        copy = pltpu.make_async_copy(src, dst, self.sems.at[self.count])
        self.count += 1
        copy.start()
        return copy


def greet(*extra):
    barrier = pltpu.get_barrier_semaphore()
    peers = [dict(x=d) for d in STEPS] + [dict(z=d) for d in STEPS]
    peers += [dict(y=dy, c=dc) for dy, dc in SEQ_PEERS]
    for p in peers:
        pl.semaphore_signal(barrier, inc=1, device_id=shifted(**p), device_id_type=MESH)
    count = len(peers)
    for differs, device in extra:

        @pl.when(differs)
        def _(device=device):
            pl.semaphore_signal(barrier, inc=1, device_id=device, device_id_type=MESH)

        count = jnp.where(differs, count + 1, count)
    pl.semaphore_wait(barrier, count)


def group(buf, first, at, half=None, rows=None):
    span = pl.ds(0, 4) if half is None else pl.ds(2 * half, 2)
    index = (span, at) if first == "x" else (at, span)
    if rows is not None:
        index += (pl.ds(*rows),)
    return buf.at[index]


class Gather:
    def __init__(self, copies, buf, first, rows=None):
        self.copies, self.buf, self.first, self.rows = copies, buf, first, rows
        self.other = "z" if first == "x" else "x"
        x, z, _, _ = place()
        self.at = z if first == "x" else x
        self.own = buf.at[x, z] if rows is None else buf.at[x, z, pl.ds(*rows)]

    def part(self, step, half=None):
        return group(self.buf, self.first, moved(self.at, step), half, self.rows)

    def one(self, src=None):
        src = self.own if src is None else src
        self.sent = [self.copies.start(src, self.own, shifted(**{self.first: d})) for d in STEPS]
        self.all = list(self.sent)

    def two(self):
        for c in self.sent:
            c.wait_recv()
        send = lambda d, half: self.copies.start(
            self.part(0, half), self.part(0, half), shifted(**{self.other: d})
        )
        self.early = [send(1, 0), send(-1, 1)]
        self.late = [send(1, 1), send(-1, 0)]
        self.all += self.early + self.late

    def three(self):
        for c, d, half in zip(self.early, (1, -1), (0, 1)):
            c.wait_recv()
            passed = self.part(-d, half)
            self.late.append(self.copies.start(passed, passed, shifted(**{self.other: d})))
        self.all += self.late[2:]

    def done(self):
        for c in self.late:
            c.wait_recv()


def out_route(groups=16, parts=8, heads=2):
    b = lax.axis_index("batch")
    s = lax.axis_index("seq")
    to = ((b % heads) * parts + s, b // heads)
    source = (s * heads + b // parts, b % parts)
    differs = jnp.logical_or(to[0] != b, to[1] != s)
    return to, source, differs


def dot(a, b, ca=1, cb=0):
    return lax.dot_general(a, b, (((ca,), (cb,)), ((), ())), preferred_element_type=F32)


Q_AT, K_AT, V_AT, U_AT, L_AT, M_AT = 0, 256, 512, 768, 1024, 1792


def turn(v, tc, ta, tb):
    return v * tc + pltpu.roll(v, 112, 1) * ta + pltpu.roll(v, 16, 1) * tb


def project(i, F1, QK, bq, TC, TA, TB, A):
    r = pl.ds(pl.multiple_of(i * 256, 256), 256)
    two = pl.ds(2 * i, 2)
    full = dot(F1[i].reshape(256, C), QK[...].reshape(C, 768)) + bq[...]
    tc, ta, tb = TC[r], TA[r], TB[r]

    def put(at, v):
        A[two, :, at : at + 128] = v.astype(BF16).reshape(2, 128, 128)

    for at in (0, 128):
        put(Q_AT + at, turn(full[:, at : at + 128], tc, ta, tb) * SCALE)
        put(K_AT + at, turn(full[:, 256 + at : 384 + at], tc, ta, tb))
        put(V_AT + at, full[:, 512 + at : 640 + at])


def head_pass(h, A, DK, DV, TC, TA, TB, gb):
    at = h * 128

    def rows(first, count, column):
        return A[first : first + count, :, column + at : column + at + 128].reshape(count * 128, 128)

    def put(first, count, column, v):
        A[first : first + count, :, column + at : column + at + 128] = v.astype(BF16).reshape(count, 128, 128)

    for i in reversed(range(4)):
        r = pl.ds(i * 256, 256)
        m = 2 * (i + 1)
        n = 128 * m
        q, g = rows(2 * i, 2, Q_AT), rows(2 * i, 2, U_AT)
        k, v = rows(0, m, K_AT), rows(0, m, V_AT)
        s = dot(q, k, 1, 1)
        row = lax.broadcasted_iota(jnp.int32, (256, n), 0) + i * 256
        col = lax.broadcasted_iota(jnp.int32, (256, n), 1)
        s = jnp.where(row >= col, s, -1e30)
        p = jnp.exp(s - jnp.max(s, -1, keepdims=True))
        p = p * (1.0 / jnp.sum(p, -1, keepdims=True))
        p_low = p.astype(BF16)
        put(2 * i, 2, M_AT, dot(p_low, v))
        gp = dot(g, v, 1, 1)
        gs = (p * (gp - jnp.sum(p * gp, -1, keepdims=True))).astype(BF16)
        dk, dv = dot(gs, q, 0, 0), dot(p_low, g, 0, 0)
        if i == 3:
            DK[...], DV[...] = dk, dv
        else:
            DK[0:n, :] += dk
            DV[0:n, :] += dv
        gq = dot(gs, k) * SCALE
        gq = turn(gq, TC[r], -TA[r], -TB[r])
        put(2 * i, 2, L_AT, gq)
        part = jnp.sum(gq, 0, keepdims=True)
        total = part if i == 3 else total + part
    gb[:, at : at + 128] = total
    gk = turn(DK[...], TC[...], -TA[...], -TB[...])
    put(0, 8, L_AT + 256, gk)
    gb[:, 256 + at : 384 + at] = jnp.sum(gk, 0, keepdims=True)
    gv = DV[...]
    put(0, 8, L_AT + 512, gv)
    gb[:, 512 + at : 640 + at] = jnp.sum(gv, 0, keepdims=True)


def add_rows(shape, into, parts):
    slabs, rows = shape
    step = min(rows, 16)

    def add(t, _):
        i = t // (rows // step)
        r = pl.ds(pl.multiple_of(t % (rows // step) * step, step), step)
        total = parts[0](i, r).astype(F32)
        for p in parts[1:]:
            total += p(i, r).astype(F32)
        into(i, r, total)
        return 0

    lax.fori_loop(0, slabs * (rows // step), add, 0)


class Scatter:
    def __init__(self, copies, buf, pool, first, rows=None, wide=None):
        self.wide = wide
        self.copies, self.buf, self.first, self.rows = copies, buf, first, rows
        cut = () if rows is None else (pl.ds(*rows),)
        self.pool = pool
        self.cut = cut
        self.other = "z" if first == "x" else "x"
        x, z, _, _ = place()
        self.at, self.mine = (z, x) if first == "x" else (x, z)
        self.count = buf.shape[2] if rows is None else rows[1]
        self.base = 0 if rows is None else rows[0]

    def part(self, step, half=None):
        return group(self.buf, self.first, moved(self.at, step), half, self.rows)

    def slab(self, step, i, r):
        at = moved(self.at, step)
        r = pl.ds(self.base + r.start, r.size)
        return (i, at, r) if self.first == "x" else (at, i, r)

    def spot(self, i, span):
        if self.wide is None:
            return (i, span) + self.cut
        return (span, i % 2) + self.cut + (pl.ds(1024 * (i // 2), self.wide),)

    def relay(self, k):
        return self.pool.at[self.spot(0, pl.ds(2 * k, 2))]

    def land(self, k, half):
        return self.pool.at[self.spot(1 + k, pl.ds(2 * half, 2))]

    def last(self, k):
        return self.pool.at[self.spot(3, k)]

    def held(self, i, j, r):
        r = pl.ds(self.base + r.start, r.size)
        if self.wide is None:
            return self.pool[i, j, r]
        return self.pool[j, i % 2, r, pl.ds(1024 * (i // 2), self.wide)]

    def one(self):
        start, to = self.copies.start, self.other
        self.far = [
            start(self.part(2, k), self.relay(k), shifted(**{to: d})) for k, d in enumerate((1, -1))
        ]
        self.near = [
            start(self.part(d, 1 - k), self.land(k, 1 - k), shifted(**{to: d}))
            for k, d in enumerate((1, -1))
        ]

    def mid(self):
        for k, d in enumerate((1, -1)):
            self.far[k].wait_recv()

            def put(i, r, total, k=k, d=d):
                self.buf[self.slab(d, i + 2 * k, r)] = total.astype(self.buf.dtype)

            add_rows(
                (2, self.count),
                put,
                [lambda i, r, k=k, d=d: self.buf[self.slab(d, i + 2 * k, r)],
                 lambda i, r, k=k: self.held(0, 2 * k + i, r)],
            )
            self.near.append(
                self.copies.start(
                    self.part(d, k), self.land(k, k), shifted(**{self.other: d})
                )
            )

    def two(self):
        for cp in self.near:
            cp.wait_recv()

        def put(i, r, total):
            self.buf[self.slab(0, i, r)] = total.astype(self.buf.dtype)

        add_rows(
            (4, self.count),
            put,
            [lambda i, r: self.buf[self.slab(0, i, r)],
             lambda i, r: self.held(1, i, r), lambda i, r: self.held(2, i, r)],
        )
        x, z, _, _ = place()
        self.sent = []
        for k, d in enumerate(STEPS):
            there = moved(self.mine, d)
            index = (there, self.at) if self.first == "x" else (self.at, there)
            if self.rows is not None:
                index += (pl.ds(*self.rows),)
            self.sent.append(
                self.copies.start(self.buf.at[index], self.last(k), shifted(**{self.first: d}))
            )

    def three(self, put):
        for cp in self.sent:
            cp.wait_recv()
        add_rows(
            (1, self.count),
            lambda i, r, total: put(r, total),
            [lambda i, r: self.buf[self.slab(0, self.mine, r)]]
            + [lambda i, r, k=k: self.held(3, k, r) for k in range(3)],
        )


class SeqScatter:
    def __init__(self, copies, buf, pool):
        self.copies, self.buf, self.pool = copies, buf, pool
        _, _, self.y, self.c = place()

    def one(self):
        self.sent = self.copies.start(self.buf.at[:, 1 - self.c], self.pool.at[pl.ds(0, 4)], shifted(c=1))

    def two(self):
        self.sent.wait_recv()
        buf, c = self.buf, self.c

        def put(i, r, total):
            buf[i, c, r] = total.astype(BF16)

        add_rows((4, 128), put, [lambda i, r: buf[i, c, r], lambda i, r: self.pool[i, r]])
        start = self.copies.start
        far = moved(self.y, 2)
        halves = (pl.ds(0, 64), pl.ds(64, 64))
        self.far = [
            start(buf.at[far, c, halves[k]], self.pool.at[4, halves[k]], shifted(y=d)) for k, d in enumerate((1, -1))
        ]
        self.near = [
            start(buf.at[moved(self.y, d), c, halves[1 - k]], self.pool.at[5 + k, halves[1 - k]], shifted(y=d))
            for k, d in enumerate((1, -1))
        ]

    def mid(self):
        buf, c = self.buf, self.c
        for k, d in enumerate((1, -1)):
            self.far[k].wait_recv()
            to = moved(self.y, d)

            def rows(r, k=k):
                return pl.ds(64 * k + r.start, r.size)

            def put(i, r, total, rows=rows, to=to):
                buf[to, c, rows(r)] = total.astype(BF16)

            add_rows(
                (1, 64),
                put,
                [lambda i, r, rows=rows, to=to: buf[to, c, rows(r)],
                 lambda i, r, rows=rows: self.pool[4, rows(r)]],
            )
            self.near.append(
                self.copies.start(
                    buf.at[to, c, pl.ds(64 * k, 64)], self.pool.at[5 + k, pl.ds(64 * k, 64)], shifted(y=d)
                )
            )

    def three(self, put):
        for cp in self.near:
            cp.wait_recv()
        buf, y, c = self.buf, self.y, self.c
        add_rows(
            (1, 128),
            lambda i, r, total: put(r, total),
            [lambda i, r: buf[y, c, r], lambda i, r: self.pool[5, r], lambda i, r: self.pool[6, r]],
        )


def layer_kernel(x_ref, g_ref, pos_ref, freq_ref, bo_ref, bd_ref, ga_ref, sa_ref, gm_ref, sm_ref, bq_ref, bu_ref,
                 up_ref, qkv_ref, down_ref, out_ref,
                 y_out, x_out, gd_out, gu_all, gq_all, go_all, sv,
                 X, G, SA, RA, SM, UP, QK, DN, WO, F1, F2, NB, ACT, GHL, GQ, GO, GD, GU, PP,
                 DK, DV, TC, TA, TB,
                 BQ, VT, v_land, CT, CP, vec, gsum, gbu, gbq, go_part,
                 send, recv, ready, loc):
    copies, local = Copies(send, recv), Locals(loc)
    x, z, y, c = place()
    s = y * 2 + c
    b_me = lax.axis_index("batch")
    to, source, differs = out_route()
    loads = [
        local.start(qkv_ref.at[:, pl.ds(C * p, C)], F1.at[0, 0, pl.ds(16 * p, 16)]) for p in range(3)
    ]
    x_load = local.start(x_ref, X.at[y, c])
    up_loads = [
        local.start(up_ref.at[:, pl.ds(C * p, C)], F2.at[0, 0, pl.ds(16 * p, 16)]) for p in range(4)
    ]
    down_load = local.start(down_ref, DN.at[x, z])
    g_load = local.start(g_ref, G.at[y, c])
    greet((differs, source), (differs, to))
    xz_peers = [shifted(**{a: d}) for a in ("x", "z") for d in STEPS]
    y_peers = [shifted(c=1)] + [shifted(y=d) for d in (1, -1)]

    def tell(k, peers):
        for p in peers:
            pl.semaphore_signal(ready.at[k], inc=1, device_id=p, device_id_type=MESH)

    def hear(k, peers):
        pl.semaphore_wait(ready.at[k], len(peers))

    def sent(group):
        for cp in group:
            cp.wait_send()
        copies.made = [cp for cp in copies.made if all(cp is not m for m in group)]

    down = [Gather(copies, DN, "x", (0, 32)), Gather(copies, DN, "z", (32, 32))]
    for g in down:
        g.one(down_ref.at[pl.ds(*g.rows)])

    def across(src, width, dst):
        def piece(k):
            return src.at[pl.ds(pl.multiple_of(k * 16, 16), 16), pl.ds(0, width)]

        dst[...] = piece(s)[...]
        return [
            copies.start(piece(moved(y, dy) * 2 + lax.rem(c + dc, 2)), dst, shifted(y=dy, c=dc))
            for dy, dc in SEQ_PEERS
        ]

    rows16 = pl.ds(pl.multiple_of(s * 16, 16), 16)
    for cp in loads:
        cp.wait()
    for k in range(8):
        for part in range(3):
            GHL[16 * k : 16 * (k + 1), 256 * part : 256 * (part + 1)] = (
                F1[0, 0, 16 * part : 16 * (part + 1), 256 * k : 256 * (k + 1)]
            )
    qk = across(GHL, 768, QK.at[x, z, rows16])
    out_copy = copies.make(out_ref, WO.at[to[0] // 4, to[0] % 4], to)

    @pl.when(differs)
    def _():
        out_copy.start()

    out_load = pltpu.make_async_copy(out_ref, WO.at[x, z], loc.at[15])

    @pl.when(jnp.logical_not(differs))
    def _():
        out_load.start()

    def placed(ref, width, at):
        v = jnp.concatenate([ref[...].astype(F32), jnp.zeros((1, width - ref.shape[1]), F32)], 1)
        return pltpu.roll(jnp.broadcast_to(v, (8, width)), at, 1)[0:1]

    vec[16:32, 0:128] = jnp.zeros((16, 128), F32)
    for k, ref in enumerate((bo_ref, bd_ref, ga_ref, sa_ref, gm_ref, sm_ref)):
        vec[16 + k : 17 + k, 0:128] = placed(ref, 128, s * 16)
    wide = placed(bq_ref, 384, s * 48)
    for k in range(3):
        vec[22 + k : 23 + k, 0:128] = wide[:, 128 * k : 128 * (k + 1)]
    vec[25:26, 0:128] = placed(bu_ref, 128, b_me % 2 * 64)
    SA[s] = vec[16:32, 0:128].astype(BF16)
    sm = [copies.start(SA.at[s], SA.at[s], shifted(y=dy, c=dc)) for dy, dc in SEQ_PEERS]

    def seq_one(src, dst):
        own = dst.at[y, c]
        return [copies.start(src, own, shifted(y=d)) for d in (1, -1)] + [
            copies.start(src, own, shifted(c=1))
        ]

    def seq_two(sent, dst):
        more = []
        for cp, d in zip(sent[:2], (1, -1)):
            cp.wait_recv()
            got = dst.at[moved(y, -d), c]
            more.append(copies.start(got, got, shifted(c=1)))
        up_way = c == 0
        got = dst.at[jnp.where(up_way, moved(y, -1), moved(y, 1)), c]
        py = jnp.where(up_way, moved(y, 1), moved(y, -1))
        fwd = copies.start(got, got, (b_me, py * 2 + c))
        sent[2].wait_recv()
        return more, fwd

    def seq_three(more, fwd, dst):
        fwd.wait_recv()
        got = dst.at[moved(y, 2), c]
        return more + [copies.start(got, got, shifted(c=1))]

    xs = seq_one(x_ref, X)
    angle = pos_ref[...].astype(F32) * freq_ref[...]
    RA[s, 0:16, :] = jnp.cos(angle)
    RA[s, 16:32, :] = jnp.sin(angle)
    ra = [copies.start(RA.at[s], RA.at[s], shifted(y=dy, c=dc)) for dy, dc in SEQ_PEERS]
    for cp in up_loads:
        cp.wait()
    lane = lax.broadcasted_iota(jnp.int32, (16, 128), 1)
    for k in range(8):
        for p in range(8):
            at = (8 * p + k // 2) * 128
            r, at = 16 * (at // C), at % C
            one = F2[0, 0, r : r + 16, at : at + 128].astype(F32)
            two = F2[0, 0, r : r + 16, at + 512 : at + 640].astype(F32)
            if k % 2 == 0:
                two = pltpu.roll(two, 64, 1)
            else:
                one = pltpu.roll(one, 64, 1)
            ACT[16 * k : 16 * (k + 1), 128 * p : 128 * (p + 1)] = jnp.where(lane < 64, one, two).astype(BF16)
    up = across(ACT, 1024, UP.at[x, z, rows16])

    for cp in qk:
        cp.wait_recv()
    qa = Gather(copies, QK, "x", (0, 48))
    qb = Gather(copies, QK, "z", (48, 80))
    qa.one()
    qb.one()

    @pl.when(differs)
    def _():
        out_copy.wait()

    @pl.when(jnp.logical_not(differs))
    def _():
        out_load.wait()

    wo = Gather(copies, WO, "x")
    wo.one()
    for cp in sm:
        cp.wait_recv()
    total = SA[0].astype(F32)
    for k in range(1, 8):
        total += SA[k].astype(F32)
    row = lax.broadcasted_iota(jnp.int32, (16, 128), 0)
    SM[x, z] = jnp.where(row == 9, SA[s].astype(F32), total).astype(BF16)
    small = Gather(copies, SM, "z")
    small.one()
    g_load.wait()
    total = jnp.zeros((1, C), F32)
    for k in range(8):
        total += jnp.sum(G[y, c, 16 * k : 16 * (k + 1)].astype(F32), 0, keepdims=True)
    gsum[...] = total
    qa.two()
    qb.two()
    small.two()
    wo.two()
    xs2, xf = seq_two(xs, X)
    gs = seq_one(g_ref, G)
    small.three()
    qa.three()
    qb.three()
    for cp in up:
        cp.wait_recv()
    upg = [Gather(copies, UP, "x", (0, 64)), Gather(copies, UP, "z", (64, 64))]
    for g in upg:
        g.one()
    wo.three()
    down_load.wait()
    for g in down:
        g.two()
    small.done()
    for i in range(4):
        for j in range(4):
            b = i * 4 + j
            tile = SM[i, j].astype(F32)
            vec[0:6, b * 128 : (b + 1) * 128] = tile[0:6]
            for k in range(3):
                BQ[3 * b + k : 3 * b + k + 1, :] = tile[6 + k : 7 + k]
            if b % 2 == 0:
                kept = tile[9:10]
            else:
                vec[6:7, b // 2 * 128 : (b // 2 + 1) * 128] = kept + tile[9:10]

    def norm(ky, kc):
        def step(t, _):
            r = pl.ds(pl.multiple_of(t * 16, 16), 16)
            v = X[ky, kc, r].astype(F32)
            v = v - jnp.mean(v, -1, keepdims=True)
            n = v * lax.rsqrt(jnp.mean(v * v, -1, keepdims=True) + EPS)
            NB[ky * 2 + kc, r] = n.astype(BF16)
            F1[ky, kc, r] = (n * vec[2:3, :] + vec[3:4, :]).astype(BF16)
            F2[ky, 2 * kc + t // 4, pl.ds(pl.multiple_of(t % 4 * 16, 16), 16)] = (
                n * vec[4:5, :] + vec[5:6, :]
            ).astype(BF16)
            return 0

        lax.fori_loop(0, 8, step, 0)

    x_load.wait()
    norm(y, c)
    norm(y, 1 - c)
    norm(moved(y, -1), c)
    norm(moved(y, 1), c)
    xs3 = seq_three(xs2, xf, X)
    xs3[0].wait_recv()
    norm(moved(y, -1), 1 - c)
    xs3[1].wait_recv()
    norm(moved(y, 1), 1 - c)
    gs2, gf = seq_two(gs, G)
    norm(moved(y, 2), c)
    xs3[2].wait_recv()
    norm(moved(y, 2), 1 - c)
    for cp in ra:
        cp.wait_recv()

    lane = lax.broadcasted_iota(jnp.int32, (128, 128), 1)
    for k in range(8):
        r = pl.ds(k * 128, 128)
        tile = jnp.concatenate([RA[k], jnp.zeros((96, 128), F32)], 0).T
        TC[r] = jnp.where(lane < 16, tile, jnp.where(lane < 32, pltpu.roll(tile, 16, 1), 1.0))
        TA[r] = jnp.where(lane < 16, -pltpu.roll(tile, 112, 1), 0.0)
        TB[r] = jnp.where((lane >= 16) & (lane < 32), tile, 0.0)
    for gth in (qa, qb):
        gth.done()
    for part in range(3):
        pair = BQ[pl.ds(part * 16 + s * 2, 2), :]
        for k in range(2):
            at = part * 256 + k * 128
            vec[9:10, at : at + 128] = pair[k : k + 1]

    def first(i, _):
        project(i, F1, QK, vec.at[9:10, 0:768], TC, TA, TB, PP)
        return 0

    lax.fori_loop(0, 4, first, 0)
    for g in upg:
        g.two()
    gs3 = seq_three(gs2, gf, G)
    wo.done()
    for cp in gs3:
        cp.wait_recv()

    def mixed(i, _):
        total = dot(G[i].reshape(256, C), WO[...].reshape(256, C), 1, 1)
        PP[pl.ds(2 * i, 2), :, U_AT:L_AT] = total.astype(BF16).reshape(2, 128, 256)
        return 0

    lax.fori_loop(0, 4, mixed, 0)
    for g in down:
        g.three()
    sent(xs + xs2 + [xf, xs3[2]])
    tell(0, xz_peers)
    for h in range(2):
        head_pass(h, PP, DK, DV, TC, TA, TB, gbq)
    for g in upg:
        g.three()

    def grad_out(j, _):
        q = pl.ds(pl.multiple_of(j * 1024, 1024), 1024)
        mix = PP[:, :, M_AT:].reshape(1024, 256)
        GO[:, :, :, q] = dot(mix, G[:, :, :, q].reshape(1024, 1024), 0, 0).astype(BF16).reshape(4, 4, 16, 1024)
        return 0

    lax.fori_loop(0, 2, grad_out, 0)

    def grad_qkv(i, _):
        r = pl.ds(pl.multiple_of(i * 512, 512), 512)
        right = PP[:, :, L_AT:M_AT].reshape(1024, 768)
        GQ[i] = dot(F1[:, :, :, r].reshape(1024, 512), right, 0, 0).astype(BF16).reshape(4, 128, 768)
        return 0

    lax.fori_loop(0, 4, grad_qkv, 0)

    sa = Scatter(copies, GQ, X, "x", (0, 48), 768)
    sb = Scatter(copies, GQ, X, "z", (48, 80), 768)
    so = Scatter(copies, GO, WO, "x")
    fp = SeqScatter(copies, X, PP)
    fq = SeqScatter(copies, F1, NB)
    hear(0, xz_peers)
    sa.one()
    sb.one()

    gbu[...] = jnp.zeros_like(gbu)
    sent(qk + up)
    for g in down + upg:
        g.done()

    def hidden(t, _):
        i, j = t // 2, t % 2
        r = pl.ds(pl.multiple_of(i * 256, 256), 256)
        q = pl.ds(pl.multiple_of(j * 512, 512), 512)
        h = dot(F2[i].reshape(256, C), UP[:, :, :, q].reshape(C, 512)) + vec[6:7, q]
        ga = dot(G[i].reshape(256, C), DN[pl.ds(2 * j, 2)].reshape(512, C), 1, 1)
        cdf = 0.5 + 0.5 * lax.erf(h * (0.5**0.5))
        ACT[r, q] = (h * cdf).astype(BF16)
        gh = ga * (cdf + h * (jnp.exp(h * h * -0.5) * 0.3989422804014327))
        gbu[:, q] += jnp.sum(gh, 0, keepdims=True)
        GHL[r, q] = gh.astype(BF16)
        return 0

    lax.fori_loop(0, 8, hidden, 0)
    sa.mid()
    sb.mid()

    sd = [Scatter(copies, GD, F2, "x", (0, 32)), Scatter(copies, GD, F2, "z", (32, 32))]
    su = [Scatter(copies, GU, UP, "x", (0, 64)), Scatter(copies, GU, UP, "z", (64, 64))]
    sc = Scatter(copies, CT, CP, "z")
    vec[12:14, :] = jnp.zeros((2, C), F32)

    def second(t, _):
        i, j = t // 4, t % 4
        r = pl.ds(pl.multiple_of(i * 256, 256), 256)
        q = pl.ds(pl.multiple_of(j * 512, 512), 512)
        u = dot(GHL[r], UP[j].reshape(512, 1024), 1, 1)
        n = NB[pl.ds(2 * i, 2), :, q].reshape(256, 512).astype(F32)
        vec[12:13, q] += jnp.sum(u * n, 0, keepdims=True)
        vec[13:14, q] += jnp.sum(u, 0, keepdims=True)
        F1[i, :, :, q] = (u * vec[4:5, q]).astype(BF16).reshape(2, 128, 512)
        return 0

    lax.fori_loop(0, 16, second, 0)
    for g in upg:
        sent(g.all)
    tell(2, xz_peers)

    def grad_up(t, _):
        i, j = t // 2, t % 2
        r = pl.ds(pl.multiple_of(i * 512, 512), 512)
        q = pl.ds(pl.multiple_of(j * 512, 512), 512)
        left = F2[:, :, :, r].reshape(1024, 512)
        GU[i, :, :, q] = dot(left, GHL[:, q], 0, 0).astype(BF16).reshape(4, 128, 512)
        return 0

    lax.fori_loop(0, 8, grad_up, 0)
    tell(1, xz_peers)
    hear(2, xz_peers)
    for g in su:
        g.one()
    sa.two()
    sb.two()

    vec[10:12, :] = jnp.zeros((2, C), F32)

    def grad_first(t, _):
        i, j = t // 4, t % 4
        q = pl.ds(pl.multiple_of(j * 512, 512), 512)
        left = PP[pl.ds(2 * i, 2), :, L_AT:M_AT].reshape(256, 768)
        u = dot(left, QK[j].reshape(512, 768), 1, 1)
        n = NB[pl.ds(2 * i, 2), :, q].reshape(256, 512).astype(F32)
        vec[10:11, q] += jnp.sum(u * n, 0, keepdims=True)
        vec[11:12, q] += jnp.sum(u, 0, keepdims=True)
        total = u * vec[2:3, q] + F1[i, :, :, q].reshape(256, 512).astype(F32)
        F1[i, :, :, q] = total.astype(BF16).reshape(2, 128, 512)
        return 0

    lax.fori_loop(0, 16, grad_first, 0)

    tell(3, y_peers)

    def store(ref, base=0):
        def put(r, total):
            ref[pl.ds(base + r.start, r.size)] = total.astype(ref.dtype)

        return put

    gu_part = GHL.at[pl.ds(128, 128)]
    gq_part = GHL.at[pl.ds(0, 128), pl.ds(0, 768)]

    def spread(part, out):
        out[s] = part[pl.ds(pl.multiple_of(s * 16, 16), 16)]
        made = []
        for dy, dc in SEQ_PEERS:
            peer = moved(y, dy) * 2 + lax.rem(c + dc, 2)
            made.append(
                copies.start(
                    part.at[pl.ds(pl.multiple_of(peer * 16, 16), 16)], out.at[s], shifted(y=dy, c=dc)
                )
            )
        return made

    sa.three(store(gq_part))
    sb.three(store(gq_part, 48))
    backs = spread(gq_part, gq_all)

    def attend(t, _):
        i, j = t // 2, t % 2
        q = pl.ds(pl.multiple_of(j * 1024, 1024), 1024)
        mix = PP[pl.ds(4 * i, 4), :, M_AT:].reshape(512, 256)
        total = dot(mix, WO[:, :, :, q].reshape(256, 1024))
        X[pl.ds(2 * i, 2), :, :, q] = total.astype(BF16).reshape(2, 2, 128, 1024)
        return 0

    lax.fori_loop(0, 4, attend, 0)
    sent(wo.all)
    tell(5, xz_peers)
    tell(4, y_peers)
    hear(3, y_peers)
    fq.one()
    for g in su:
        g.mid()
    hear(5, xz_peers)
    so.one()

    def grad_down(t, _):
        i, j = t // 2, t % 2
        u = pl.ds(pl.multiple_of(i * 256, 256), 256)
        q = pl.ds(pl.multiple_of(j * 1024, 1024), 1024)
        right = G[:, :, :, q].reshape(1024, 1024)
        GD[i, :, :, q] = dot(ACT[:, u], right, 0, 0).astype(BF16).reshape(4, 64, 1024)
        return 0

    lax.fori_loop(0, 8, grad_down, 0)
    hear(1, xz_peers)
    for g in sd:
        g.one()
    fq.two()
    sent(gs3 + [gf])
    again = [local.start(x_ref, G.at[0, 0]), local.start(g_ref, G.at[0, 1])]

    BQ[...] = jnp.zeros_like(BQ)
    for part in range(3):
        for k in range(2):
            at = part * 256 + k * 128
            BQ[pl.ds(part * 16 + s * 2 + k, 1), :] = gbq[:, at : at + 128]
    for b in range(16):
        at = b * 128
        VT[b, 0:1, :] = gsum[:, at : at + 128]
        VT[b, 1:5, :] = vec[10:14, at : at + 128]
        VT[b, 5:8, :] = BQ[3 * b : 3 * b + 3, :]
    vs = [
        copies.start(VT, v_land.at[k], shifted(y=dy, c=dc)) for k, (dy, dc) in enumerate(SEQ_PEERS)
    ]
    def feed(t, _):
        i, j = t // 4, t % 4
        r = pl.ds(pl.multiple_of(i * 512, 512), 512)
        q = pl.ds(pl.multiple_of(j * 512, 512), 512)
        two = pl.ds(2 * i, 2)
        total = dot(ACT[r], DN[:, :, :, q].reshape(1024, 512)) + X[two, :, :, q].reshape(512, 512).astype(F32)
        X[two, :, :, q] = total.astype(BF16).reshape(2, 2, 128, 512)
        return 0

    lax.fori_loop(0, 8, feed, 0)
    hear(4, y_peers)
    fp.one()
    so.mid()
    for g in sd:
        g.mid()
    for g in su:
        g.two()
    fq.mid()
    fp.two()

    for cp in vs:
        cp.wait_recv()
    for b in range(16):
        total = VT[b]
        for k in range(7):
            total += v_land[k, b]
        CT[b // 4, b % 4, 0:8, :] = total
        CT[b // 4, b % 4, 8:9, :] = gbu[:, b // 2 * 128 : b // 2 * 128 + 128]
        CT[b // 4, b % 4, 9:16, :] = jnp.zeros((7, 128), F32)
    sc.one()

    so.two()
    sc.mid()
    for k, g in enumerate(su):
        g.three(store(gu_part, 64 * k))
    backs += spread(gu_part, gu_all)
    for g in sd:
        g.two()
    fp.mid()
    sc.two()
    so.three(store(go_part))
    out_back = copies.make(go_part, go_all, source)

    @pl.when(differs)
    def _():
        out_back.start()

    @pl.when(jnp.logical_not(differs))
    def _():
        go_all[...] = go_part[...]

    for cp in again:
        cp.wait()

    def grad_in(r, total):
        v = G[0, 0, r].astype(F32)
        v = v - jnp.mean(v, -1, keepdims=True)
        inv = lax.rsqrt(jnp.mean(v * v, -1, keepdims=True) + EPS)
        n = v * inv
        total = total - jnp.mean(total, -1, keepdims=True) - n * jnp.mean(total * n, -1, keepdims=True)
        x_out[r] = (G[0, 1, r].astype(F32) + total * inv).astype(BF16)

    fq.three(grad_in)

    def layer_out(r, total):
        bias = vec[0:1, :] + vec[1:2, :]
        y_out[r] = (G[0, 0, r].astype(F32) + total + bias).astype(BF16)

    fp.three(layer_out)
    sc.three(store(sv))
    for k, g in enumerate(sd):
        g.three(store(gd_out, 32 * k))

    @pl.when(differs)
    def _():
        out_back.wait()

    for cp in backs:
        cp.wait_recv()
    copies.drain()


def layer(x, g, pos, freq, vectors, up, qkv, down, out):
    any_ = pl.BlockSpec(memory_space=pl.ANY)
    vm = pl.BlockSpec(memory_space=pltpu.VMEM)
    n_up, n_qkv = up.shape[-1] // 8, qkv.shape[-1] // 8
    up_all, qk_all = (4, 4, 128, n_up), (4, 4, 128, n_qkv)
    dn_all, wo_all = (4, 4) + down.shape, (4, 4) + out.shape
    blocks, unit = (4, 2, 128, C), (1024, n_up)
    S = pltpu.VMEM
    scratch = [
        (blocks, BF16), (blocks, BF16), ((8, 16, 128), BF16), ((8, 32, 128), F32), ((4, 4, 16, 128), BF16),
        (up_all, BF16), (qk_all, BF16), (dn_all, BF16), (wo_all, BF16),
        (blocks, BF16), ((4, 4, 64, C), BF16), ((8, 128, C), BF16), (unit, BF16), (unit, BF16),
        (qk_all, BF16), (wo_all, BF16), (dn_all, BF16), (up_all, BF16), ((8, 128, C), BF16),
        ((1024, HD), F32), ((1024, HD), F32), ((1024, HD), F32), ((1024, HD), F32), ((1024, HD), F32),
        ((48, 128), F32), ((16, 8, 128), F32), ((7, 16, 8, 128), F32), ((4, 4, 16, 128), F32), ((4, 4, 16, 128), F32),
        ((32, C), F32), ((1, C), F32), ((1, n_up), F32), ((1, n_qkv), F32),
        (out.shape, BF16),
    ]
    outs = [
        (x.shape, BF16), (x.shape, BF16), (down.shape, F32),
        ((8, 16, n_up), BF16), ((8, 16, n_qkv), BF16), (out.shape, BF16), ((16, 128), F32),
    ]
    return pl.pallas_call(
        layer_kernel,
        out_shape=[jax.ShapeDtypeStruct(*o) for o in outs],
        in_specs=[any_, any_] + [vm] * 10 + [any_] * 4,
        out_specs=[vm] * 7,
        scratch_shapes=[S(*h) for h in scratch]
        + [pltpu.SemaphoreType.DMA((230,)), pltpu.SemaphoreType.DMA((230,)), pltpu.SemaphoreType.REGULAR((6,)), pltpu.SemaphoreType.DMA((16,))],
        compiler_params=pltpu.CompilerParams(
            collective_id=1, has_side_effects=True, vmem_limit_bytes=64 * 2**20 - 2**16
        ),
    )(x, g, pos, freq, *vectors, up, qkv, down, out)


def finish_kernel(y_in, x_in, gd_in, gu_in, gq_in, go_in, sv,
                  y_out, x_out, gd, gu, gq, go, b_out, b_down, ga, sa, gm, sm, bq, bu):
    s = lax.axis_index("seq")
    b = lax.axis_index("batch")
    y_out[...] = y_in[...]
    x_out[...] = x_in[...]
    gd[...] = gd_in[...]
    go[...] = go_in[...].astype(F32)
    for k in range(8):
        for part in range(3):
            piece = gq_in[k, :, 256 * part : 256 * (part + 1)]
            gq[:, C * part + 256 * k : C * part + 256 * (k + 1)] = piece.astype(F32)
    lane = lax.broadcasted_iota(jnp.int32, (16, 128), 1)
    for j in range(4):
        for p in range(8):
            one = gu_in[2 * j, :, 128 * p : 128 * (p + 1)].astype(F32)
            two = gu_in[2 * j + 1, :, 128 * p : 128 * (p + 1)].astype(F32)
            at = (8 * p + j) * 128
            gu[:, at : at + 128] = jnp.where(lane < 64, one, pltpu.roll(two, 64, 1))
            gu[:, at + 512 : at + 640] = jnp.where(lane < 64, pltpu.roll(one, 64, 1), two)
    mine = pltpu.roll(sv[...], lax.rem(128 - s * 16, 128), 1)
    for k, ref in enumerate((b_out, ga, sa, gm, sm)):
        ref[...] = mine[k : k + 1, 0:16]
    b_down[...] = mine[0:1, 0:16]
    wide = jnp.concatenate([jnp.broadcast_to(sv[k : k + 1, :], (8, 128)) for k in (5, 6, 7)], 1)
    bq[...] = pltpu.roll(wide, lax.rem(384 - s * 48, 384), 1)[0:1, 0:48]
    tail = pltpu.roll(sv[8:16, :], lax.rem(b, 2) * 64, 1)
    bu[...] = tail[0:1, 0:64]


def finish(*parts):
    vm = pl.BlockSpec(memory_space=pltpu.VMEM)
    y, xg, gd, gu, gq, go, _ = parts
    outs = [(y.shape, BF16), (xg.shape, BF16), (gd.shape, F32), ((16, 8 * gu.shape[-1]), F32), ((16, 8 * gq.shape[-1]), F32), (go.shape, F32)]
    outs += [((1, 16), F32)] * 6 + [((1, 48), F32), ((1, 64), F32)]
    return pl.pallas_call(
        finish_kernel,
        out_shape=[jax.ShapeDtypeStruct(*o) for o in outs],
        in_specs=[vm] * 7,
        out_specs=[vm] * len(outs),
    )(*parts)


def shards(
    inputs,
    positions,
    w_qkv,
    b_qkv,
    w_out,
    b_out,
    w_up,
    b_up,
    w_down,
    b_down,
    gain_attn,
    shift_attn,
    gain_mlp,
    shift_mlp,
    grad_out,
):
    half_rot = ROT // 2
    exponent = jnp.arange(half_rot).astype(F32) / half_rot
    frequency = jnp.broadcast_to(jnp.power(10000.0, -exponent)[:, None], (half_rot, 128))
    vectors = [
        v[None] for v in (b_out, b_down, gain_attn, shift_attn, gain_mlp, shift_mlp, b_qkv, b_up)
    ]
    parts = layer(inputs[0], grad_out[0], positions, frequency, vectors, w_up, w_qkv, w_down, w_out)
    layer_out, grad_in, g_down, g_up, g_qkv, g_out, *rest = finish(*parts)
    g_b_out, g_b_down, g_gain_a, g_shift_a, g_gain_m, g_shift_m, g_b_qkv, g_b_up = [v[0] for v in rest]
    return (
        layer_out[None],
        grad_in[None],
        g_qkv,
        g_b_qkv,
        g_out,
        g_b_out,
        g_up,
        g_b_up,
        g_down,
        g_b_down,
        g_gain_a,
        g_shift_a,
        g_gain_m,
        g_shift_m,
    )


def solution(mesh):
    both = ("batch", "seq")
    rows = P("batch", "seq", None)
    matrix = P(both, None)
    vector = P(both)
    return jax.shard_map(
        shards,
        mesh=mesh,
        in_specs=(
            rows,
            P("batch", "seq"),
            matrix,
            vector,
            matrix,
            vector,
            matrix,
            vector,
            matrix,
            vector,
            vector,
            vector,
            vector,
            vector,
            rows,
        ),
        out_specs=(
            rows,
            rows,
            matrix,
            vector,
            matrix,
            vector,
            matrix,
            vector,
            matrix,
            vector,
            vector,
            vector,
            vector,
            vector,
        ),
        check_vma=False,
    )
```

```python
import jax
import jax.numpy as jnp
from jax import lax
from jax.experimental import pallas as pl
from jax.experimental.pallas import tpu as pltpu
from jax.sharding import PartitionSpec as P

H = 16
HD = 128
ROT = 32
EPS = 1e-05
C = 2048
SCALE = HD ** (-0.5)
F32 = jnp.float32
BF16 = jnp.bfloat16
MESH = pl.DeviceIdType.MESH
STEPS = (1, -1, 2)
SEQ_PEERS = [(dy, dc) for dc in (1, 0) for dy in (0, 1, -1, 2) if (dy, dc) != (0, 0)]


def place():
    b = lax.axis_index("batch")
    s = lax.axis_index("seq")
    return b // 4, b % 4, s // 2, s % 2


def shifted(x=0, z=0, y=0, c=0):
    px, pz, py, pc = place()
    px = lax.rem(px + x + 4, 4)
    pz = lax.rem(pz + z + 4, 4)
    py = lax.rem(py + y + 4, 4)
    pc = lax.rem(pc + c, 2)
    return (px * 4 + pz, py * 2 + pc)


def moved(pos, step):
    return lax.rem(pos + step + 4, 4)


class Copies:
    def __init__(self, send, recv):
        self.send, self.recv, self.count, self.made = send, recv, 0, []

    def make(self, src, dst, device):
        k = self.count
        self.count += 1
        return pltpu.make_async_remote_copy(
            src_ref=src,
            dst_ref=dst,
            send_sem=self.send.at[k],
            recv_sem=self.recv.at[k],
            device_id=device,
            device_id_type=MESH,
        )

    def start(self, src, dst, device):
        copy = self.make(src, dst, device)
        copy.start()
        self.made.append(copy)
        return copy

    def drain(self):
        for copy in self.made:
            copy.wait_send()


class Locals:
    def __init__(self, sems):
        self.sems, self.count = sems, 0

    def start(self, src, dst):
        copy = pltpu.make_async_copy(src, dst, self.sems.at[self.count])
        self.count += 1
        copy.start()
        return copy


def greet(*extra):
    barrier = pltpu.get_barrier_semaphore()
    peers = [dict(x=d) for d in STEPS] + [dict(z=d) for d in STEPS]
    peers += [dict(y=dy, c=dc) for dy, dc in SEQ_PEERS]
    for p in peers:
        pl.semaphore_signal(barrier, inc=1, device_id=shifted(**p), device_id_type=MESH)
    count = len(peers)
    for differs, device in extra:

        @pl.when(differs)
        def _(device=device):
            pl.semaphore_signal(barrier, inc=1, device_id=device, device_id_type=MESH)

        count = jnp.where(differs, count + 1, count)
    pl.semaphore_wait(barrier, count)


def group(buf, first, at, half=None, rows=None):
    span = pl.ds(0, 4) if half is None else pl.ds(2 * half, 2)
    index = (span, at) if first == "x" else (at, span)
    if rows is not None:
        index += (pl.ds(*rows),)
    return buf.at[index]


class Gather:
    def __init__(self, copies, buf, first, rows=None):
        self.copies, self.buf, self.first, self.rows = copies, buf, first, rows
        self.other = "z" if first == "x" else "x"
        x, z, _, _ = place()
        self.at = z if first == "x" else x
        self.own = buf.at[x, z] if rows is None else buf.at[x, z, pl.ds(*rows)]

    def part(self, step, half=None):
        return group(self.buf, self.first, moved(self.at, step), half, self.rows)

    def one(self, src=None):
        src = self.own if src is None else src
        self.sent = [self.copies.start(src, self.own, shifted(**{self.first: d})) for d in STEPS]
        self.all = list(self.sent)

    def two(self):
        for c in self.sent:
            c.wait_recv()
        send = lambda d, half: self.copies.start(
            self.part(0, half), self.part(0, half), shifted(**{self.other: d})
        )
        self.early = [send(1, 0), send(-1, 1)]
        self.late = [send(1, 1), send(-1, 0)]
        self.all += self.early + self.late

    def three(self):
        for c, d, half in zip(self.early, (1, -1), (0, 1)):
            c.wait_recv()
            passed = self.part(-d, half)
            self.late.append(self.copies.start(passed, passed, shifted(**{self.other: d})))
        self.all += self.late[2:]

    def done(self):
        for c in self.late:
            c.wait_recv()


def out_route(groups=16, parts=8, heads=2):
    b = lax.axis_index("batch")
    s = lax.axis_index("seq")
    to = ((b % heads) * parts + s, b // heads)
    source = (s * heads + b // parts, b % parts)
    differs = jnp.logical_or(to[0] != b, to[1] != s)
    return to, source, differs


def dot(a, b, ca=1, cb=0):
    return lax.dot_general(a, b, (((ca,), (cb,)), ((), ())), preferred_element_type=F32)


Q_AT, K_AT, V_AT, U_AT, L_AT, M_AT = 0, 256, 512, 768, 1024, 1792


def turn(v, tc, ta, tb):
    return v * tc + pltpu.roll(v, 112, 1) * ta + pltpu.roll(v, 16, 1) * tb


def project(i, F1, QK, bq, TC, TA, TB, A):
    r = pl.ds(pl.multiple_of(i * 256, 256), 256)
    two = pl.ds(2 * i, 2)
    full = dot(F1[i].reshape(256, C), QK[...].reshape(C, 768)) + bq[...]
    tc, ta, tb = TC[r], TA[r], TB[r]

    def put(at, v):
        A[two, :, at : at + 128] = v.astype(BF16).reshape(2, 128, 128)

    for at in (0, 128):
        put(Q_AT + at, turn(full[:, at : at + 128], tc, ta, tb) * SCALE)
        put(K_AT + at, turn(full[:, 256 + at : 384 + at], tc, ta, tb))
        put(V_AT + at, full[:, 512 + at : 640 + at])


def head_pass(h, A, DK, DV, TC, TA, TB, gb):
    at = h * 128

    def rows(first, count, column):
        return A[first : first + count, :, column + at : column + at + 128].reshape(count * 128, 128)

    def put(first, count, column, v):
        A[first : first + count, :, column + at : column + at + 128] = v.astype(BF16).reshape(count, 128, 128)

    for i in reversed(range(4)):
        r = pl.ds(i * 256, 256)
        m = 2 * (i + 1)
        n = 128 * m
        q, g = rows(2 * i, 2, Q_AT), rows(2 * i, 2, U_AT)
        k, v = rows(0, m, K_AT), rows(0, m, V_AT)
        s = dot(q, k, 1, 1)
        row = lax.broadcasted_iota(jnp.int32, (256, n), 0) + i * 256
        col = lax.broadcasted_iota(jnp.int32, (256, n), 1)
        s = jnp.where(row >= col, s, -1e30)
        p = jnp.exp(s - jnp.max(s, -1, keepdims=True))
        p = p * (1.0 / jnp.sum(p, -1, keepdims=True))
        p_low = p.astype(BF16)
        put(2 * i, 2, M_AT, dot(p_low, v))
        gp = dot(g, v, 1, 1)
        gs = (p * (gp - jnp.sum(p * gp, -1, keepdims=True))).astype(BF16)
        dk, dv = dot(gs, q, 0, 0), dot(p_low, g, 0, 0)
        if i == 3:
            DK[...], DV[...] = dk, dv
        else:
            DK[0:n, :] += dk
            DV[0:n, :] += dv
        gq = dot(gs, k) * SCALE
        gq = turn(gq, TC[r], -TA[r], -TB[r])
        put(2 * i, 2, L_AT, gq)
        part = jnp.sum(gq, 0, keepdims=True)
        total = part if i == 3 else total + part
    gb[:, at : at + 128] = total
    gk = turn(DK[...], TC[...], -TA[...], -TB[...])
    put(0, 8, L_AT + 256, gk)
    gb[:, 256 + at : 384 + at] = jnp.sum(gk, 0, keepdims=True)
    gv = DV[...]
    put(0, 8, L_AT + 512, gv)
    gb[:, 512 + at : 640 + at] = jnp.sum(gv, 0, keepdims=True)


def add_rows(shape, into, parts):
    slabs, rows = shape
    step = min(rows, 16)

    def add(t, _):
        i = t // (rows // step)
        r = pl.ds(pl.multiple_of(t % (rows // step) * step, step), step)
        total = parts[0](i, r).astype(F32)
        for p in parts[1:]:
            total += p(i, r).astype(F32)
        into(i, r, total)
        return 0

    lax.fori_loop(0, slabs * (rows // step), add, 0)


class Scatter:
    def __init__(self, copies, buf, pool, first, rows=None):
        self.copies, self.buf, self.first, self.rows = copies, buf, first, rows
        cut = () if rows is None else (pl.ds(*rows),)
        self.pool = pool
        self.cut = cut
        self.other = "z" if first == "x" else "x"
        x, z, _, _ = place()
        self.at, self.mine = (z, x) if first == "x" else (x, z)
        self.count = buf.shape[2] if rows is None else rows[1]
        self.base = 0 if rows is None else rows[0]

    def part(self, step, half=None):
        return group(self.buf, self.first, moved(self.at, step), half, self.rows)

    def slab(self, step, i, r):
        at = moved(self.at, step)
        r = pl.ds(self.base + r.start, r.size)
        return (i, at, r) if self.first == "x" else (at, i, r)

    def relay(self, k):
        return self.pool.at[(0, pl.ds(2 * k, 2)) + self.cut]

    def land(self, k, half):
        return self.pool.at[(1 + k, pl.ds(2 * half, 2)) + self.cut]

    def last(self, k):
        return self.pool.at[(3, k) + self.cut]

    def held(self, i, j, r):
        return self.pool[i, j, pl.ds(self.base + r.start, r.size)]

    def one(self):
        start, to = self.copies.start, self.other
        self.far = [
            start(self.part(2, k), self.relay(k), shifted(**{to: d})) for k, d in enumerate((1, -1))
        ]
        self.near = [
            start(self.part(d, 1 - k), self.land(k, 1 - k), shifted(**{to: d}))
            for k, d in enumerate((1, -1))
        ]

    def mid(self):
        for k, d in enumerate((1, -1)):
            self.far[k].wait_recv()

            def put(i, r, total, k=k, d=d):
                self.buf[self.slab(d, i + 2 * k, r)] = total.astype(self.buf.dtype)

            add_rows(
                (2, self.count),
                put,
                [lambda i, r, k=k, d=d: self.buf[self.slab(d, i + 2 * k, r)],
                 lambda i, r, k=k: self.held(0, 2 * k + i, r)],
            )
            self.near.append(
                self.copies.start(
                    self.part(d, k), self.land(k, k), shifted(**{self.other: d})
                )
            )

    def two(self):
        for cp in self.near:
            cp.wait_recv()

        def put(i, r, total):
            self.buf[self.slab(0, i, r)] = total.astype(self.buf.dtype)

        add_rows(
            (4, self.count),
            put,
            [lambda i, r: self.buf[self.slab(0, i, r)],
             lambda i, r: self.held(1, i, r), lambda i, r: self.held(2, i, r)],
        )
        x, z, _, _ = place()
        self.sent = []
        for k, d in enumerate(STEPS):
            there = moved(self.mine, d)
            index = (there, self.at) if self.first == "x" else (self.at, there)
            if self.rows is not None:
                index += (pl.ds(*self.rows),)
            self.sent.append(
                self.copies.start(self.buf.at[index], self.last(k), shifted(**{self.first: d}))
            )

    def three(self, put):
        for cp in self.sent:
            cp.wait_recv()
        add_rows(
            (1, self.count),
            lambda i, r, total: put(r, total),
            [lambda i, r: self.buf[self.slab(0, self.mine, r)]]
            + [lambda i, r, k=k: self.held(3, k, r) for k in range(3)],
        )


class SeqScatter:
    def __init__(self, copies, buf, pool):
        self.copies, self.buf, self.pool = copies, buf, pool
        _, _, self.y, self.c = place()

    def one(self):
        self.sent = self.copies.start(self.buf.at[:, 1 - self.c], self.pool.at[pl.ds(0, 4)], shifted(c=1))

    def two(self):
        self.sent.wait_recv()
        buf, c = self.buf, self.c

        def put(i, r, total):
            buf[i, c, r] = total.astype(BF16)

        add_rows((4, 128), put, [lambda i, r: buf[i, c, r], lambda i, r: self.pool[i, r]])
        start = self.copies.start
        far = moved(self.y, 2)
        halves = (pl.ds(0, 64), pl.ds(64, 64))
        self.far = [
            start(buf.at[far, c, halves[k]], self.pool.at[4, halves[k]], shifted(y=d)) for k, d in enumerate((1, -1))
        ]
        self.near = [
            start(buf.at[moved(self.y, d), c, halves[1 - k]], self.pool.at[5 + k, halves[1 - k]], shifted(y=d))
            for k, d in enumerate((1, -1))
        ]

    def mid(self):
        buf, c = self.buf, self.c
        for k, d in enumerate((1, -1)):
            self.far[k].wait_recv()
            to = moved(self.y, d)

            def rows(r, k=k):
                return pl.ds(64 * k + r.start, r.size)

            def put(i, r, total, rows=rows, to=to):
                buf[to, c, rows(r)] = total.astype(BF16)

            add_rows(
                (1, 64),
                put,
                [lambda i, r, rows=rows, to=to: buf[to, c, rows(r)],
                 lambda i, r, rows=rows: self.pool[4, rows(r)]],
            )
            self.near.append(
                self.copies.start(
                    buf.at[to, c, pl.ds(64 * k, 64)], self.pool.at[5 + k, pl.ds(64 * k, 64)], shifted(y=d)
                )
            )

    def three(self, put):
        for cp in self.near:
            cp.wait_recv()
        buf, y, c = self.buf, self.y, self.c
        add_rows(
            (1, 128),
            lambda i, r, total: put(r, total),
            [lambda i, r: buf[y, c, r], lambda i, r: self.pool[5, r], lambda i, r: self.pool[6, r]],
        )


def layer_kernel(x_ref, g_ref, pos_ref, freq_ref, bo_ref, bd_ref, ga_ref, sa_ref, gm_ref, sm_ref, bq_ref, bu_ref,
                 up_ref, qkv_ref, down_ref, out_ref,
                 y_out, x_out, gd_out, gu_all, gq_all, go_all, sv,
                 X, G, SA, RA, SM, UP, QK, DN, WO, F1, F2, NB, ACT, GHL, GQ, GO, GD, GU, PP,
                 DK, DV, TC, TA, TB,
                 BQ, VT, v_land, CT, CP, vec, gsum, gbu, gbq, go_part,
                 send, recv, ready, loc):
    copies, local = Copies(send, recv), Locals(loc)
    x, z, y, c = place()
    s = y * 2 + c
    b_me = lax.axis_index("batch")
    to, source, differs = out_route()
    loads = [
        local.start(qkv_ref.at[:, pl.ds(C * p, C)], F1.at[0, 0, pl.ds(16 * p, 16)]) for p in range(3)
    ]
    x_load = local.start(x_ref, X.at[y, c])
    up_loads = [
        local.start(up_ref.at[:, pl.ds(C * p, C)], F2.at[0, 0, pl.ds(16 * p, 16)]) for p in range(4)
    ]
    down_load = local.start(down_ref, DN.at[x, z])
    g_load = local.start(g_ref, G.at[y, c])
    greet((differs, source), (differs, to))
    xz_peers = [shifted(**{a: d}) for a in ("x", "z") for d in STEPS]
    y_peers = [shifted(c=1)] + [shifted(y=d) for d in (1, -1)]

    def tell(k, peers):
        for p in peers:
            pl.semaphore_signal(ready.at[k], inc=1, device_id=p, device_id_type=MESH)

    def hear(k, peers):
        pl.semaphore_wait(ready.at[k], len(peers))

    def sent(group):
        for cp in group:
            cp.wait_send()
        copies.made = [cp for cp in copies.made if all(cp is not m for m in group)]

    down = [Gather(copies, DN, "x", (0, 32)), Gather(copies, DN, "z", (32, 32))]
    for g in down:
        g.one(down_ref.at[pl.ds(*g.rows)])

    def across(src, width, dst):
        def piece(k):
            return src.at[pl.ds(pl.multiple_of(k * 16, 16), 16), pl.ds(0, width)]

        dst[...] = piece(s)[...]
        return [
            copies.start(piece(moved(y, dy) * 2 + lax.rem(c + dc, 2)), dst, shifted(y=dy, c=dc))
            for dy, dc in SEQ_PEERS
        ]

    rows16 = pl.ds(pl.multiple_of(s * 16, 16), 16)
    for cp in loads:
        cp.wait()
    for k in range(8):
        for part in range(3):
            GHL[16 * k : 16 * (k + 1), 256 * part : 256 * (part + 1)] = (
                F1[0, 0, 16 * part : 16 * (part + 1), 256 * k : 256 * (k + 1)]
            )
    qk = across(GHL, 768, QK.at[x, z, rows16])
    out_copy = copies.make(out_ref, WO.at[to[0] // 4, to[0] % 4], to)

    @pl.when(differs)
    def _():
        out_copy.start()

    out_load = pltpu.make_async_copy(out_ref, WO.at[x, z], loc.at[15])

    @pl.when(jnp.logical_not(differs))
    def _():
        out_load.start()

    def placed(ref, width, at):
        v = jnp.concatenate([ref[...].astype(F32), jnp.zeros((1, width - ref.shape[1]), F32)], 1)
        return pltpu.roll(jnp.broadcast_to(v, (8, width)), at, 1)[0:1]

    vec[16:32, 0:128] = jnp.zeros((16, 128), F32)
    for k, ref in enumerate((bo_ref, bd_ref, ga_ref, sa_ref, gm_ref, sm_ref)):
        vec[16 + k : 17 + k, 0:128] = placed(ref, 128, s * 16)
    wide = placed(bq_ref, 384, s * 48)
    for k in range(3):
        vec[22 + k : 23 + k, 0:128] = wide[:, 128 * k : 128 * (k + 1)]
    vec[25:26, 0:128] = placed(bu_ref, 128, b_me % 2 * 64)
    SA[s] = vec[16:32, 0:128].astype(BF16)
    sm = [copies.start(SA.at[s], SA.at[s], shifted(y=dy, c=dc)) for dy, dc in SEQ_PEERS]

    def seq_one(src, dst):
        own = dst.at[y, c]
        return [copies.start(src, own, shifted(y=d)) for d in (1, -1)] + [
            copies.start(src, own, shifted(c=1))
        ]

    def seq_two(sent, dst):
        more = []
        for cp, d in zip(sent[:2], (1, -1)):
            cp.wait_recv()
            got = dst.at[moved(y, -d), c]
            more.append(copies.start(got, got, shifted(c=1)))
        up_way = c == 0
        got = dst.at[jnp.where(up_way, moved(y, -1), moved(y, 1)), c]
        py = jnp.where(up_way, moved(y, 1), moved(y, -1))
        fwd = copies.start(got, got, (b_me, py * 2 + c))
        sent[2].wait_recv()
        return more, fwd

    def seq_three(more, fwd, dst):
        fwd.wait_recv()
        got = dst.at[moved(y, 2), c]
        return more + [copies.start(got, got, shifted(c=1))]

    xs = seq_one(x_ref, X)
    angle = pos_ref[...].astype(F32) * freq_ref[...]
    RA[s, 0:16, :] = jnp.cos(angle)
    RA[s, 16:32, :] = jnp.sin(angle)
    ra = [copies.start(RA.at[s], RA.at[s], shifted(y=dy, c=dc)) for dy, dc in SEQ_PEERS]
    for cp in up_loads:
        cp.wait()
    lane = lax.broadcasted_iota(jnp.int32, (16, 128), 1)
    for k in range(8):
        for p in range(8):
            at = (8 * p + k // 2) * 128
            r, at = 16 * (at // C), at % C
            one = F2[0, 0, r : r + 16, at : at + 128].astype(F32)
            two = F2[0, 0, r : r + 16, at + 512 : at + 640].astype(F32)
            if k % 2 == 0:
                two = pltpu.roll(two, 64, 1)
            else:
                one = pltpu.roll(one, 64, 1)
            ACT[16 * k : 16 * (k + 1), 128 * p : 128 * (p + 1)] = jnp.where(lane < 64, one, two).astype(BF16)
    up = across(ACT, 1024, UP.at[x, z, rows16])

    for cp in qk:
        cp.wait_recv()
    qa = Gather(copies, QK, "x", (0, 48))
    qb = Gather(copies, QK, "z", (48, 80))
    qa.one()
    qb.one()

    @pl.when(differs)
    def _():
        out_copy.wait()

    @pl.when(jnp.logical_not(differs))
    def _():
        out_load.wait()

    wo = Gather(copies, WO, "x")
    wo.one()
    for cp in sm:
        cp.wait_recv()
    total = SA[0].astype(F32)
    for k in range(1, 8):
        total += SA[k].astype(F32)
    row = lax.broadcasted_iota(jnp.int32, (16, 128), 0)
    SM[x, z] = jnp.where(row == 9, SA[s].astype(F32), total).astype(BF16)
    small = Gather(copies, SM, "z")
    small.one()
    g_load.wait()
    total = jnp.zeros((1, C), F32)
    for k in range(8):
        total += jnp.sum(G[y, c, 16 * k : 16 * (k + 1)].astype(F32), 0, keepdims=True)
    gsum[...] = total
    qa.two()
    qb.two()
    small.two()
    wo.two()
    xs2, xf = seq_two(xs, X)
    gs = seq_one(g_ref, G)
    small.three()
    qa.three()
    qb.three()
    for cp in up:
        cp.wait_recv()
    upg = [Gather(copies, UP, "x", (0, 64)), Gather(copies, UP, "z", (64, 64))]
    for g in upg:
        g.one()
    wo.three()
    down_load.wait()
    for g in down:
        g.two()
    small.done()
    for i in range(4):
        for j in range(4):
            b = i * 4 + j
            tile = SM[i, j].astype(F32)
            vec[0:6, b * 128 : (b + 1) * 128] = tile[0:6]
            for k in range(3):
                BQ[3 * b + k : 3 * b + k + 1, :] = tile[6 + k : 7 + k]
            if b % 2 == 0:
                kept = tile[9:10]
            else:
                vec[6:7, b // 2 * 128 : (b // 2 + 1) * 128] = kept + tile[9:10]

    def norm(ky, kc):
        def step(t, _):
            r = pl.ds(pl.multiple_of(t * 16, 16), 16)
            v = X[ky, kc, r].astype(F32)
            v = v - jnp.mean(v, -1, keepdims=True)
            n = v * lax.rsqrt(jnp.mean(v * v, -1, keepdims=True) + EPS)
            NB[ky * 2 + kc, r] = n.astype(BF16)
            F1[ky, kc, r] = (n * vec[2:3, :] + vec[3:4, :]).astype(BF16)
            F2[ky, 2 * kc + t // 4, pl.ds(pl.multiple_of(t % 4 * 16, 16), 16)] = (
                n * vec[4:5, :] + vec[5:6, :]
            ).astype(BF16)
            return 0

        lax.fori_loop(0, 8, step, 0)

    x_load.wait()
    norm(y, c)
    norm(y, 1 - c)
    norm(moved(y, -1), c)
    norm(moved(y, 1), c)
    xs3 = seq_three(xs2, xf, X)
    xs3[0].wait_recv()
    norm(moved(y, -1), 1 - c)
    xs3[1].wait_recv()
    norm(moved(y, 1), 1 - c)
    gs2, gf = seq_two(gs, G)
    norm(moved(y, 2), c)
    xs3[2].wait_recv()
    norm(moved(y, 2), 1 - c)
    for cp in ra:
        cp.wait_recv()

    lane = lax.broadcasted_iota(jnp.int32, (128, 128), 1)
    for k in range(8):
        r = pl.ds(k * 128, 128)
        tile = jnp.concatenate([RA[k], jnp.zeros((96, 128), F32)], 0).T
        TC[r] = jnp.where(lane < 16, tile, jnp.where(lane < 32, pltpu.roll(tile, 16, 1), 1.0))
        TA[r] = jnp.where(lane < 16, -pltpu.roll(tile, 112, 1), 0.0)
        TB[r] = jnp.where((lane >= 16) & (lane < 32), tile, 0.0)
    for gth in (qa, qb):
        gth.done()
    for part in range(3):
        pair = BQ[pl.ds(part * 16 + s * 2, 2), :]
        for k in range(2):
            at = part * 256 + k * 128
            vec[9:10, at : at + 128] = pair[k : k + 1]

    def first(i, _):
        project(i, F1, QK, vec.at[9:10, 0:768], TC, TA, TB, PP)
        return 0

    lax.fori_loop(0, 4, first, 0)
    for g in upg:
        g.two()
    gs3 = seq_three(gs2, gf, G)
    wo.done()
    for cp in gs3:
        cp.wait_recv()

    def mixed(i, _):
        total = dot(G[i].reshape(256, C), WO[...].reshape(256, C), 1, 1)
        PP[pl.ds(2 * i, 2), :, U_AT:L_AT] = total.astype(BF16).reshape(2, 128, 256)
        return 0

    lax.fori_loop(0, 4, mixed, 0)
    for g in down:
        g.three()
    for h in range(2):
        head_pass(h, PP, DK, DV, TC, TA, TB, gbq)
    for g in upg:
        g.three()

    def grad_out(j, _):
        q = pl.ds(pl.multiple_of(j * 1024, 1024), 1024)
        mix = PP[:, :, M_AT:].reshape(1024, 256)
        GO[:, :, :, q] = dot(mix, G[:, :, :, q].reshape(1024, 1024), 0, 0).astype(BF16).reshape(4, 4, 16, 1024)
        return 0

    lax.fori_loop(0, 2, grad_out, 0)

    def grad_qkv(i, _):
        r = pl.ds(pl.multiple_of(i * 512, 512), 512)
        right = PP[:, :, L_AT:M_AT].reshape(1024, 768)
        GQ[i] = dot(F1[:, :, :, r].reshape(1024, 512), right, 0, 0).astype(BF16).reshape(4, 128, 768)
        return 0

    lax.fori_loop(0, 4, grad_qkv, 0)
    sent(xs + xs2 + [xf, xs3[2]])

    def attend(t, _):
        i, j = t // 2, t % 2
        q = pl.ds(pl.multiple_of(j * 1024, 1024), 1024)
        mix = PP[pl.ds(4 * i, 4), :, M_AT:].reshape(512, 256)
        total = dot(mix, WO[:, :, :, q].reshape(256, 1024))
        X[pl.ds(2 * i, 2), :, :, q] = total.astype(BF16).reshape(2, 2, 128, 1024)
        return 0

    lax.fori_loop(0, 4, attend, 0)
    vec[10:12, :] = jnp.zeros((2, C), F32)

    def grad_first(t, _):
        i, j = t // 4, t % 4
        q = pl.ds(pl.multiple_of(j * 512, 512), 512)
        left = PP[pl.ds(2 * i, 2), :, L_AT:M_AT].reshape(256, 768)
        u = dot(left, QK[j].reshape(512, 768), 1, 1)
        n = NB[pl.ds(2 * i, 2), :, q].reshape(256, 512).astype(F32)
        vec[10:11, q] += jnp.sum(u * n, 0, keepdims=True)
        vec[11:12, q] += jnp.sum(u, 0, keepdims=True)
        F1[i, :, :, q] = (u * vec[2:3, q]).astype(BF16).reshape(2, 128, 512)
        return 0

    lax.fori_loop(0, 16, grad_first, 0)

    for g in (qa, qb, wo):
        sent(g.all)
    sent(qk + up)
    tell(0, xz_peers)
    tell(4, y_peers)

    sa = Scatter(copies, GQ, QK, "x", (0, 48))
    sb = Scatter(copies, GQ, QK, "z", (48, 80))
    so = Scatter(copies, GO, WO, "x")
    fp = SeqScatter(copies, X, PP)
    fq = SeqScatter(copies, F1, NB)
    gbu[...] = jnp.zeros_like(gbu)
    hear(0, xz_peers)
    for g in (sa, sb, so):
        g.one()
    for g in down + upg:
        g.done()

    def hidden(t, _):
        i, j = t // 2, t % 2
        r = pl.ds(pl.multiple_of(i * 256, 256), 256)
        q = pl.ds(pl.multiple_of(j * 512, 512), 512)
        h = dot(F2[i].reshape(256, C), UP[:, :, :, q].reshape(C, 512)) + vec[6:7, q]
        ga = dot(G[i].reshape(256, C), DN[pl.ds(2 * j, 2)].reshape(512, C), 1, 1)
        cdf = 0.5 + 0.5 * lax.erf(h * (0.5**0.5))
        ACT[r, q] = (h * cdf).astype(BF16)
        gh = ga * (cdf + h * (jnp.exp(h * h * -0.5) * 0.3989422804014327))
        gbu[:, q] += jnp.sum(gh, 0, keepdims=True)
        GHL[r, q] = gh.astype(BF16)
        return 0

    lax.fori_loop(0, 8, hidden, 0)
    for g in (sa, sb, so):
        g.mid()

    sd = [Scatter(copies, GD, F2, "x", (0, 32)), Scatter(copies, GD, F2, "z", (32, 32))]
    su = [Scatter(copies, GU, UP, "x", (0, 64)), Scatter(copies, GU, UP, "z", (64, 64))]
    sc = Scatter(copies, CT, CP, "z")
    vec[12:14, :] = jnp.zeros((2, C), F32)

    def second(t, _):
        i, j = t // 4, t % 4
        r = pl.ds(pl.multiple_of(i * 256, 256), 256)
        q = pl.ds(pl.multiple_of(j * 512, 512), 512)
        u = dot(GHL[r], UP[j].reshape(512, 1024), 1, 1)
        n = NB[pl.ds(2 * i, 2), :, q].reshape(256, 512).astype(F32)
        vec[12:13, q] += jnp.sum(u * n, 0, keepdims=True)
        vec[13:14, q] += jnp.sum(u, 0, keepdims=True)
        total = u * vec[4:5, q] + F1[i, :, :, q].reshape(256, 512).astype(F32)
        F1[i, :, :, q] = total.astype(BF16).reshape(2, 128, 512)
        return 0

    lax.fori_loop(0, 16, second, 0)
    for g in upg:
        sent(g.all)
    tell(2, xz_peers)
    tell(3, y_peers)

    def grad_up(t, _):
        i, j = t // 2, t % 2
        r = pl.ds(pl.multiple_of(i * 512, 512), 512)
        q = pl.ds(pl.multiple_of(j * 512, 512), 512)
        left = F2[:, :, :, r].reshape(1024, 512)
        GU[i, :, :, q] = dot(left, GHL[:, q], 0, 0).astype(BF16).reshape(4, 128, 512)
        return 0

    lax.fori_loop(0, 8, grad_up, 0)
    tell(1, xz_peers)
    hear(3, y_peers)
    fq.one()
    hear(2, xz_peers)
    for g in su:
        g.one()
    for g in (sa, sb, so):
        g.two()

    def grad_down(t, _):
        i, j = t // 2, t % 2
        u = pl.ds(pl.multiple_of(i * 256, 256), 256)
        q = pl.ds(pl.multiple_of(j * 1024, 1024), 1024)
        right = G[:, :, :, q].reshape(1024, 1024)
        GD[i, :, :, q] = dot(ACT[:, u], right, 0, 0).astype(BF16).reshape(4, 64, 1024)
        return 0

    lax.fori_loop(0, 8, grad_down, 0)
    fq.two()
    sent(gs3 + [gf])
    again = [local.start(x_ref, G.at[0, 0]), local.start(g_ref, G.at[0, 1])]

    BQ[...] = jnp.zeros_like(BQ)
    for part in range(3):
        for k in range(2):
            at = part * 256 + k * 128
            BQ[pl.ds(part * 16 + s * 2 + k, 1), :] = gbq[:, at : at + 128]
    for b in range(16):
        at = b * 128
        VT[b, 0:1, :] = gsum[:, at : at + 128]
        VT[b, 1:5, :] = vec[10:14, at : at + 128]
        VT[b, 5:8, :] = BQ[3 * b : 3 * b + 3, :]
    vs = [
        copies.start(VT, v_land.at[k], shifted(y=dy, c=dc)) for k, (dy, dc) in enumerate(SEQ_PEERS)
    ]
    def feed(t, _):
        i, j = t // 4, t % 4
        r = pl.ds(pl.multiple_of(i * 512, 512), 512)
        q = pl.ds(pl.multiple_of(j * 512, 512), 512)
        two = pl.ds(2 * i, 2)
        total = dot(ACT[r], DN[:, :, :, q].reshape(1024, 512)) + X[two, :, :, q].reshape(512, 512).astype(F32)
        X[two, :, :, q] = total.astype(BF16).reshape(2, 2, 128, 512)
        return 0

    lax.fori_loop(0, 8, feed, 0)
    for g in su:
        g.mid()
    hear(1, xz_peers)
    for g in sd:
        g.one()
    hear(4, y_peers)
    fp.one()
    fq.mid()
    fp.two()

    for cp in vs:
        cp.wait_recv()
    for b in range(16):
        total = VT[b]
        for k in range(7):
            total += v_land[k, b]
        CT[b // 4, b % 4, 0:8, :] = total
        CT[b // 4, b % 4, 8:9, :] = gbu[:, b // 2 * 128 : b // 2 * 128 + 128]
        CT[b // 4, b % 4, 9:16, :] = jnp.zeros((7, 128), F32)
    sc.one()

    def store(ref, base=0):
        def put(r, total):
            ref[pl.ds(base + r.start, r.size)] = total.astype(ref.dtype)

        return put

    gu_part = ACT.at[pl.ds(0, 128)]
    gq_part = ACT.at[pl.ds(128, 128), pl.ds(0, 768)]

    def spread(part, out):
        out[s] = part[pl.ds(pl.multiple_of(s * 16, 16), 16)]
        made = []
        for dy, dc in SEQ_PEERS:
            peer = moved(y, dy) * 2 + lax.rem(c + dc, 2)
            made.append(
                copies.start(
                    part.at[pl.ds(pl.multiple_of(peer * 16, 16), 16)], out.at[s], shifted(y=dy, c=dc)
                )
            )
        return made

    sa.three(store(gq_part))
    sb.three(store(gq_part, 48))
    backs = spread(gq_part, gq_all)
    so.three(store(go_part))
    out_back = copies.make(go_part, go_all, source)

    @pl.when(differs)
    def _():
        out_back.start()

    @pl.when(jnp.logical_not(differs))
    def _():
        go_all[...] = go_part[...]

    for g in su:
        g.two()
    for g in sd:
        g.mid()
    sc.mid()
    fp.mid()
    sc.two()
    for k, g in enumerate(su):
        g.three(store(gu_part, 64 * k))
    backs += spread(gu_part, gu_all)
    for g in sd:
        g.two()

    for cp in again:
        cp.wait()

    def grad_in(r, total):
        v = G[0, 0, r].astype(F32)
        v = v - jnp.mean(v, -1, keepdims=True)
        inv = lax.rsqrt(jnp.mean(v * v, -1, keepdims=True) + EPS)
        n = v * inv
        total = total - jnp.mean(total, -1, keepdims=True) - n * jnp.mean(total * n, -1, keepdims=True)
        x_out[r] = (G[0, 1, r].astype(F32) + total * inv).astype(BF16)

    fq.three(grad_in)

    def layer_out(r, total):
        bias = vec[0:1, :] + vec[1:2, :]
        y_out[r] = (G[0, 0, r].astype(F32) + total + bias).astype(BF16)

    fp.three(layer_out)
    sc.three(store(sv))
    for k, g in enumerate(sd):
        g.three(store(gd_out, 32 * k))

    @pl.when(differs)
    def _():
        out_back.wait()

    for cp in backs:
        cp.wait_recv()
    copies.drain()


def layer(x, g, pos, freq, vectors, up, qkv, down, out):
    any_ = pl.BlockSpec(memory_space=pl.ANY)
    vm = pl.BlockSpec(memory_space=pltpu.VMEM)
    n_up, n_qkv = up.shape[-1] // 8, qkv.shape[-1] // 8
    up_all, qk_all = (4, 4, 128, n_up), (4, 4, 128, n_qkv)
    dn_all, wo_all = (4, 4) + down.shape, (4, 4) + out.shape
    blocks, unit = (4, 2, 128, C), (1024, n_up)
    S = pltpu.VMEM
    scratch = [
        (blocks, BF16), (blocks, BF16), ((8, 16, 128), BF16), ((8, 32, 128), F32), ((4, 4, 16, 128), BF16),
        (up_all, BF16), (qk_all, BF16), (dn_all, BF16), (wo_all, BF16),
        (blocks, BF16), ((4, 4, 64, C), BF16), ((8, 128, C), BF16), (unit, BF16), (unit, BF16),
        (qk_all, BF16), (wo_all, BF16), (dn_all, BF16), (up_all, BF16), ((8, 128, C), BF16),
        ((1024, HD), F32), ((1024, HD), F32), ((1024, HD), F32), ((1024, HD), F32), ((1024, HD), F32),
        ((48, 128), F32), ((16, 8, 128), F32), ((7, 16, 8, 128), F32), ((4, 4, 16, 128), F32), ((4, 4, 16, 128), F32),
        ((32, C), F32), ((1, C), F32), ((1, n_up), F32), ((1, n_qkv), F32),
        (out.shape, BF16),
    ]
    outs = [
        (x.shape, BF16), (x.shape, BF16), (down.shape, F32),
        ((8, 16, n_up), BF16), ((8, 16, n_qkv), BF16), (out.shape, BF16), ((16, 128), F32),
    ]
    return pl.pallas_call(
        layer_kernel,
        out_shape=[jax.ShapeDtypeStruct(*o) for o in outs],
        in_specs=[any_, any_] + [vm] * 10 + [any_] * 4,
        out_specs=[vm] * 7,
        scratch_shapes=[S(*h) for h in scratch]
        + [pltpu.SemaphoreType.DMA((230,)), pltpu.SemaphoreType.DMA((230,)), pltpu.SemaphoreType.REGULAR((5,)), pltpu.SemaphoreType.DMA((16,))],
        compiler_params=pltpu.CompilerParams(
            collective_id=1, has_side_effects=True, vmem_limit_bytes=64 * 2**20 - 2**16
        ),
    )(x, g, pos, freq, *vectors, up, qkv, down, out)


def finish_kernel(y_in, x_in, gd_in, gu_in, gq_in, go_in, sv,
                  y_out, x_out, gd, gu, gq, go, b_out, b_down, ga, sa, gm, sm, bq, bu):
    s = lax.axis_index("seq")
    b = lax.axis_index("batch")
    y_out[...] = y_in[...]
    x_out[...] = x_in[...]
    gd[...] = gd_in[...]
    go[...] = go_in[...].astype(F32)
    for k in range(8):
        for part in range(3):
            piece = gq_in[k, :, 256 * part : 256 * (part + 1)]
            gq[:, C * part + 256 * k : C * part + 256 * (k + 1)] = piece.astype(F32)
    lane = lax.broadcasted_iota(jnp.int32, (16, 128), 1)
    for j in range(4):
        for p in range(8):
            one = gu_in[2 * j, :, 128 * p : 128 * (p + 1)].astype(F32)
            two = gu_in[2 * j + 1, :, 128 * p : 128 * (p + 1)].astype(F32)
            at = (8 * p + j) * 128
            gu[:, at : at + 128] = jnp.where(lane < 64, one, pltpu.roll(two, 64, 1))
            gu[:, at + 512 : at + 640] = jnp.where(lane < 64, pltpu.roll(one, 64, 1), two)
    mine = pltpu.roll(sv[...], lax.rem(128 - s * 16, 128), 1)
    for k, ref in enumerate((b_out, ga, sa, gm, sm)):
        ref[...] = mine[k : k + 1, 0:16]
    b_down[...] = mine[0:1, 0:16]
    wide = jnp.concatenate([jnp.broadcast_to(sv[k : k + 1, :], (8, 128)) for k in (5, 6, 7)], 1)
    bq[...] = pltpu.roll(wide, lax.rem(384 - s * 48, 384), 1)[0:1, 0:48]
    tail = pltpu.roll(sv[8:16, :], lax.rem(b, 2) * 64, 1)
    bu[...] = tail[0:1, 0:64]


def finish(*parts):
    vm = pl.BlockSpec(memory_space=pltpu.VMEM)
    y, xg, gd, gu, gq, go, _ = parts
    outs = [(y.shape, BF16), (xg.shape, BF16), (gd.shape, F32), ((16, 8 * gu.shape[-1]), F32), ((16, 8 * gq.shape[-1]), F32), (go.shape, F32)]
    outs += [((1, 16), F32)] * 6 + [((1, 48), F32), ((1, 64), F32)]
    return pl.pallas_call(
        finish_kernel,
        out_shape=[jax.ShapeDtypeStruct(*o) for o in outs],
        in_specs=[vm] * 7,
        out_specs=[vm] * len(outs),
    )(*parts)


def shards(
    inputs,
    positions,
    w_qkv,
    b_qkv,
    w_out,
    b_out,
    w_up,
    b_up,
    w_down,
    b_down,
    gain_attn,
    shift_attn,
    gain_mlp,
    shift_mlp,
    grad_out,
):
    half_rot = ROT // 2
    exponent = jnp.arange(half_rot).astype(F32) / half_rot
    frequency = jnp.broadcast_to(jnp.power(10000.0, -exponent)[:, None], (half_rot, 128))
    vectors = [
        v[None] for v in (b_out, b_down, gain_attn, shift_attn, gain_mlp, shift_mlp, b_qkv, b_up)
    ]
    parts = layer(inputs[0], grad_out[0], positions, frequency, vectors, w_up, w_qkv, w_down, w_out)
    layer_out, grad_in, g_down, g_up, g_qkv, g_out, *rest = finish(*parts)
    g_b_out, g_b_down, g_gain_a, g_shift_a, g_gain_m, g_shift_m, g_b_qkv, g_b_up = [v[0] for v in rest]
    return (
        layer_out[None],
        grad_in[None],
        g_qkv,
        g_b_qkv,
        g_out,
        g_b_out,
        g_up,
        g_b_up,
        g_down,
        g_b_down,
        g_gain_a,
        g_shift_a,
        g_gain_m,
        g_shift_m,
    )


def solution(mesh):
    both = ("batch", "seq")
    rows = P("batch", "seq", None)
    matrix = P(both, None)
    vector = P(both)
    return jax.shard_map(
        shards,
        mesh=mesh,
        in_specs=(
            rows,
            P("batch", "seq"),
            matrix,
            vector,
            matrix,
            vector,
            matrix,
            vector,
            matrix,
            vector,
            vector,
            vector,
            vector,
            vector,
            rows,
        ),
        out_specs=(
            rows,
            rows,
            matrix,
            vector,
            matrix,
            vector,
            matrix,
            vector,
            matrix,
            vector,
            vector,
            vector,
            vector,
            vector,
        ),
        check_vma=False,
    )
```

```python
import jax
import jax.numpy as jnp
from jax import lax
from jax.experimental import pallas as pl
from jax.experimental.pallas import tpu as pltpu
from jax.sharding import PartitionSpec as P

H = 16
HD = 128
ROT = 32
EPS = 1e-05
C = 2048
SCALE = HD ** (-0.5)
F32 = jnp.float32
BF16 = jnp.bfloat16
MESH = pl.DeviceIdType.MESH
STEPS = (1, -1, 2)
SEQ_PEERS = [(dy, dc) for dc in (1, 0) for dy in (0, 1, -1, 2) if (dy, dc) != (0, 0)]


def place():
    b = lax.axis_index("batch")
    s = lax.axis_index("seq")
    return b // 4, b % 4, s // 2, s % 2


def shifted(x=0, z=0, y=0, c=0):
    px, pz, py, pc = place()
    px = lax.rem(px + x + 4, 4)
    pz = lax.rem(pz + z + 4, 4)
    py = lax.rem(py + y + 4, 4)
    pc = lax.rem(pc + c, 2)
    return (px * 4 + pz, py * 2 + pc)


def moved(pos, step):
    return lax.rem(pos + step + 4, 4)


class Copies:
    def __init__(self, send, recv):
        self.send, self.recv, self.count, self.made = send, recv, 0, []

    def make(self, src, dst, device):
        k = self.count
        self.count += 1
        return pltpu.make_async_remote_copy(
            src_ref=src,
            dst_ref=dst,
            send_sem=self.send.at[k],
            recv_sem=self.recv.at[k],
            device_id=device,
            device_id_type=MESH,
        )

    def start(self, src, dst, device):
        copy = self.make(src, dst, device)
        copy.start()
        self.made.append(copy)
        return copy

    def drain(self):
        for copy in self.made:
            copy.wait_send()


class Locals:
    def __init__(self, sems):
        self.sems, self.count = sems, 0

    def start(self, src, dst):
        copy = pltpu.make_async_copy(src, dst, self.sems.at[self.count])
        self.count += 1
        copy.start()
        return copy


def greet(*extra):
    barrier = pltpu.get_barrier_semaphore()
    peers = [dict(x=d) for d in STEPS] + [dict(z=d) for d in STEPS]
    peers += [dict(y=dy, c=dc) for dy, dc in SEQ_PEERS]
    for p in peers:
        pl.semaphore_signal(barrier, inc=1, device_id=shifted(**p), device_id_type=MESH)
    count = len(peers)
    for differs, device in extra:

        @pl.when(differs)
        def _(device=device):
            pl.semaphore_signal(barrier, inc=1, device_id=device, device_id_type=MESH)

        count = jnp.where(differs, count + 1, count)
    pl.semaphore_wait(barrier, count)


def group(buf, first, at, half=None, rows=None):
    span = pl.ds(0, 4) if half is None else pl.ds(2 * half, 2)
    index = (span, at) if first == "x" else (at, span)
    if rows is not None:
        index += (pl.ds(*rows),)
    return buf.at[index]


class Gather:
    def __init__(self, copies, buf, first, rows=None):
        self.copies, self.buf, self.first, self.rows = copies, buf, first, rows
        self.other = "z" if first == "x" else "x"
        x, z, _, _ = place()
        self.at = z if first == "x" else x
        self.own = buf.at[x, z] if rows is None else buf.at[x, z, pl.ds(*rows)]

    def part(self, step, half=None):
        return group(self.buf, self.first, moved(self.at, step), half, self.rows)

    def one(self, src=None):
        src = self.own if src is None else src
        self.sent = [self.copies.start(src, self.own, shifted(**{self.first: d})) for d in STEPS]
        self.all = list(self.sent)

    def two(self):
        for c in self.sent:
            c.wait_recv()
        send = lambda d, half: self.copies.start(
            self.part(0, half), self.part(0, half), shifted(**{self.other: d})
        )
        self.early = [send(1, 0), send(-1, 1)]
        self.late = [send(1, 1), send(-1, 0)]
        self.all += self.early + self.late

    def three(self):
        for c, d, half in zip(self.early, (1, -1), (0, 1)):
            c.wait_recv()
            passed = self.part(-d, half)
            self.late.append(self.copies.start(passed, passed, shifted(**{self.other: d})))
        self.all += self.late[2:]

    def done(self):
        for c in self.late:
            c.wait_recv()


def out_route(groups=16, parts=8, heads=2):
    b = lax.axis_index("batch")
    s = lax.axis_index("seq")
    to = ((b % heads) * parts + s, b // heads)
    source = (s * heads + b // parts, b % parts)
    differs = jnp.logical_or(to[0] != b, to[1] != s)
    return to, source, differs


def dot(a, b, ca=1, cb=0):
    return lax.dot_general(a, b, (((ca,), (cb,)), ((), ())), preferred_element_type=F32)


Q_AT, K_AT, V_AT, U_AT, L_AT, M_AT = 0, 256, 512, 768, 1024, 1792


def turn(v, tc, ta, tb):
    return v * tc + pltpu.roll(v, 112, 1) * ta + pltpu.roll(v, 16, 1) * tb


def project(i, F1, QK, bq, TC, TA, TB, A):
    r = pl.ds(pl.multiple_of(i * 256, 256), 256)
    two = pl.ds(2 * i, 2)
    full = dot(F1[i].reshape(256, C), QK[...].reshape(C, 768)) + bq[...]
    tc, ta, tb = TC[r], TA[r], TB[r]

    def put(at, v):
        A[two, :, at : at + 128] = v.astype(BF16).reshape(2, 128, 128)

    for at in (0, 128):
        put(Q_AT + at, turn(full[:, at : at + 128], tc, ta, tb) * SCALE)
        put(K_AT + at, turn(full[:, 256 + at : 384 + at], tc, ta, tb))
        put(V_AT + at, full[:, 512 + at : 640 + at])


def head_pass(h, A, DK, DV, TC, TA, TB, gb):
    at = h * 128

    def rows(first, count, column):
        return A[first : first + count, :, column + at : column + at + 128].reshape(count * 128, 128)

    def put(first, count, column, v):
        A[first : first + count, :, column + at : column + at + 128] = v.astype(BF16).reshape(count, 128, 128)

    for i in reversed(range(4)):
        r = pl.ds(i * 256, 256)
        m = 2 * (i + 1)
        n = 128 * m
        q, g = rows(2 * i, 2, Q_AT), rows(2 * i, 2, U_AT)
        k, v = rows(0, m, K_AT), rows(0, m, V_AT)
        s = dot(q, k, 1, 1)
        row = lax.broadcasted_iota(jnp.int32, (256, n), 0) + i * 256
        col = lax.broadcasted_iota(jnp.int32, (256, n), 1)
        s = jnp.where(row >= col, s, -1e30)
        p = jnp.exp(s - jnp.max(s, -1, keepdims=True))
        p = p * (1.0 / jnp.sum(p, -1, keepdims=True))
        p_low = p.astype(BF16)
        put(2 * i, 2, M_AT, dot(p_low, v))
        gp = dot(g, v, 1, 1)
        gs = (p * (gp - jnp.sum(p * gp, -1, keepdims=True))).astype(BF16)
        dk, dv = dot(gs, q, 0, 0), dot(p_low, g, 0, 0)
        if i == 3:
            DK[...], DV[...] = dk, dv
        else:
            DK[0:n, :] += dk
            DV[0:n, :] += dv
        gq = dot(gs, k) * SCALE
        gq = turn(gq, TC[r], -TA[r], -TB[r])
        put(2 * i, 2, L_AT, gq)
        part = jnp.sum(gq, 0, keepdims=True)
        total = part if i == 3 else total + part
    gb[:, at : at + 128] = total
    gk = turn(DK[...], TC[...], -TA[...], -TB[...])
    put(0, 8, L_AT + 256, gk)
    gb[:, 256 + at : 384 + at] = jnp.sum(gk, 0, keepdims=True)
    gv = DV[...]
    put(0, 8, L_AT + 512, gv)
    gb[:, 512 + at : 640 + at] = jnp.sum(gv, 0, keepdims=True)


def add_rows(shape, into, parts):
    slabs, rows = shape
    step = min(rows, 16)

    def add(t, _):
        i = t // (rows // step)
        r = pl.ds(pl.multiple_of(t % (rows // step) * step, step), step)
        total = parts[0](i, r).astype(F32)
        for p in parts[1:]:
            total += p(i, r).astype(F32)
        into(i, r, total)
        return 0

    lax.fori_loop(0, slabs * (rows // step), add, 0)


class Scatter:
    def __init__(self, copies, buf, pool, first, rows=None, wide=None):
        self.wide = wide
        self.copies, self.buf, self.first, self.rows = copies, buf, first, rows
        cut = () if rows is None else (pl.ds(*rows),)
        self.pool = pool
        self.cut = cut
        self.other = "z" if first == "x" else "x"
        x, z, _, _ = place()
        self.at, self.mine = (z, x) if first == "x" else (x, z)
        self.count = buf.shape[2] if rows is None else rows[1]
        self.base = 0 if rows is None else rows[0]

    def part(self, step, half=None):
        return group(self.buf, self.first, moved(self.at, step), half, self.rows)

    def slab(self, step, i, r):
        at = moved(self.at, step)
        r = pl.ds(self.base + r.start, r.size)
        return (i, at, r) if self.first == "x" else (at, i, r)

    def spot(self, i, span):
        if self.wide is None:
            return (i, span) + self.cut
        return (span, i % 2) + self.cut + (pl.ds(1024 * (i // 2), self.wide),)

    def relay(self, k):
        return self.pool.at[self.spot(0, pl.ds(2 * k, 2))]

    def land(self, k, half):
        return self.pool.at[self.spot(1 + k, pl.ds(2 * half, 2))]

    def last(self, k):
        return self.pool.at[self.spot(3, k)]

    def held(self, i, j, r):
        r = pl.ds(self.base + r.start, r.size)
        if self.wide is None:
            return self.pool[i, j, r]
        return self.pool[j, i % 2, r, pl.ds(1024 * (i // 2), self.wide)]

    def one(self):
        start, to = self.copies.start, self.other
        self.far = [
            start(self.part(2, k), self.relay(k), shifted(**{to: d})) for k, d in enumerate((1, -1))
        ]
        self.near = [
            start(self.part(d, 1 - k), self.land(k, 1 - k), shifted(**{to: d}))
            for k, d in enumerate((1, -1))
        ]

    def mid(self):
        for k, d in enumerate((1, -1)):
            self.far[k].wait_recv()

            def put(i, r, total, k=k, d=d):
                self.buf[self.slab(d, i + 2 * k, r)] = total.astype(self.buf.dtype)

            add_rows(
                (2, self.count),
                put,
                [lambda i, r, k=k, d=d: self.buf[self.slab(d, i + 2 * k, r)],
                 lambda i, r, k=k: self.held(0, 2 * k + i, r)],
            )
            self.near.append(
                self.copies.start(
                    self.part(d, k), self.land(k, k), shifted(**{self.other: d})
                )
            )

    def two(self):
        for cp in self.near:
            cp.wait_recv()

        def put(i, r, total):
            self.buf[self.slab(0, i, r)] = total.astype(self.buf.dtype)

        add_rows(
            (4, self.count),
            put,
            [lambda i, r: self.buf[self.slab(0, i, r)],
             lambda i, r: self.held(1, i, r), lambda i, r: self.held(2, i, r)],
        )
        x, z, _, _ = place()
        self.sent = []
        for k, d in enumerate(STEPS):
            there = moved(self.mine, d)
            index = (there, self.at) if self.first == "x" else (self.at, there)
            if self.rows is not None:
                index += (pl.ds(*self.rows),)
            self.sent.append(
                self.copies.start(self.buf.at[index], self.last(k), shifted(**{self.first: d}))
            )

    def three(self, put):
        for cp in self.sent:
            cp.wait_recv()
        add_rows(
            (1, self.count),
            lambda i, r, total: put(r, total),
            [lambda i, r: self.buf[self.slab(0, self.mine, r)]]
            + [lambda i, r, k=k: self.held(3, k, r) for k in range(3)],
        )


class SeqScatter:
    def __init__(self, copies, buf, pool):
        self.copies, self.buf, self.pool = copies, buf, pool
        _, _, self.y, self.c = place()

    def one(self):
        self.sent = self.copies.start(self.buf.at[:, 1 - self.c], self.pool.at[pl.ds(0, 4)], shifted(c=1))

    def two(self):
        self.sent.wait_recv()
        buf, c = self.buf, self.c

        def put(i, r, total):
            buf[i, c, r] = total.astype(BF16)

        add_rows((4, 128), put, [lambda i, r: buf[i, c, r], lambda i, r: self.pool[i, r]])
        start = self.copies.start
        far = moved(self.y, 2)
        halves = (pl.ds(0, 64), pl.ds(64, 64))
        self.far = [
            start(buf.at[far, c, halves[k]], self.pool.at[4, halves[k]], shifted(y=d)) for k, d in enumerate((1, -1))
        ]
        self.near = [
            start(buf.at[moved(self.y, d), c, halves[1 - k]], self.pool.at[5 + k, halves[1 - k]], shifted(y=d))
            for k, d in enumerate((1, -1))
        ]

    def mid(self):
        buf, c = self.buf, self.c
        for k, d in enumerate((1, -1)):
            self.far[k].wait_recv()
            to = moved(self.y, d)

            def rows(r, k=k):
                return pl.ds(64 * k + r.start, r.size)

            def put(i, r, total, rows=rows, to=to):
                buf[to, c, rows(r)] = total.astype(BF16)

            add_rows(
                (1, 64),
                put,
                [lambda i, r, rows=rows, to=to: buf[to, c, rows(r)],
                 lambda i, r, rows=rows: self.pool[4, rows(r)]],
            )
            self.near.append(
                self.copies.start(
                    buf.at[to, c, pl.ds(64 * k, 64)], self.pool.at[5 + k, pl.ds(64 * k, 64)], shifted(y=d)
                )
            )

    def three(self, put):
        for cp in self.near:
            cp.wait_recv()
        buf, y, c = self.buf, self.y, self.c
        add_rows(
            (1, 128),
            lambda i, r, total: put(r, total),
            [lambda i, r: buf[y, c, r], lambda i, r: self.pool[5, r], lambda i, r: self.pool[6, r]],
        )


def layer_kernel(x_ref, g_ref, pos_ref, freq_ref, bo_ref, bd_ref, ga_ref, sa_ref, gm_ref, sm_ref, bq_ref, bu_ref,
                 up_ref, qkv_ref, down_ref, out_ref,
                 y_out, x_out, gd_out, gu_all, gq_all, go_all, sv,
                 X, G, SA, RA, SM, UP, QK, DN, WO, F1, F2, NB, ACT, GHL, GQ, GO, SP, GU, PP,
                 DK, DV, TC, TA, TB,
                 BQ, VT, v_land, CT, CP, vec, gsum, gbu, gbq, go_part,
                 send, recv, ready, loc):
    copies, local = Copies(send, recv), Locals(loc)
    x, z, y, c = place()
    s = y * 2 + c
    b_me = lax.axis_index("batch")
    to, source, differs = out_route()
    loads = [
        local.start(qkv_ref.at[:, pl.ds(C * p, C)], F1.at[0, 0, pl.ds(16 * p, 16)]) for p in range(3)
    ]
    x_load = local.start(x_ref, X.at[y, c])
    up_loads = [
        local.start(up_ref.at[:, pl.ds(C * p, C)], F2.at[0, 0, pl.ds(16 * p, 16)]) for p in range(4)
    ]
    down_load = local.start(down_ref, DN.at[x, z])
    g_load = local.start(g_ref, G.at[y, c])
    greet((differs, source), (differs, to))
    xz_peers = [shifted(**{a: d}) for a in ("x", "z") for d in STEPS]
    y_peers = [shifted(c=1)] + [shifted(y=d) for d in (1, -1)]

    def tell(k, peers):
        for p in peers:
            pl.semaphore_signal(ready.at[k], inc=1, device_id=p, device_id_type=MESH)

    def hear(k, peers):
        pl.semaphore_wait(ready.at[k], len(peers))

    def sent(group):
        for cp in group:
            cp.wait_send()
        copies.made = [cp for cp in copies.made if all(cp is not m for m in group)]

    down = [Gather(copies, DN, "x", (0, 32)), Gather(copies, DN, "z", (32, 32))]
    for g in down:
        g.one(down_ref.at[pl.ds(*g.rows)])

    def across(src, width, dst):
        def piece(k):
            return src.at[pl.ds(pl.multiple_of(k * 16, 16), 16), pl.ds(0, width)]

        dst[...] = piece(s)[...]
        return [
            copies.start(piece(moved(y, dy) * 2 + lax.rem(c + dc, 2)), dst, shifted(y=dy, c=dc))
            for dy, dc in SEQ_PEERS
        ]

    rows16 = pl.ds(pl.multiple_of(s * 16, 16), 16)
    for cp in loads:
        cp.wait()
    for k in range(8):
        for part in range(3):
            GHL[16 * k : 16 * (k + 1), 256 * part : 256 * (part + 1)] = (
                F1[0, 0, 16 * part : 16 * (part + 1), 256 * k : 256 * (k + 1)]
            )
    qk = across(GHL, 768, QK.at[x, z, rows16])
    out_copy = copies.make(out_ref, WO.at[to[0] // 4, to[0] % 4], to)

    @pl.when(differs)
    def _():
        out_copy.start()

    out_load = pltpu.make_async_copy(out_ref, WO.at[x, z], loc.at[15])

    @pl.when(jnp.logical_not(differs))
    def _():
        out_load.start()

    def placed(ref, width, at):
        v = jnp.concatenate([ref[...].astype(F32), jnp.zeros((1, width - ref.shape[1]), F32)], 1)
        return pltpu.roll(jnp.broadcast_to(v, (8, width)), at, 1)[0:1]

    vec[16:32, 0:128] = jnp.zeros((16, 128), F32)
    for k, ref in enumerate((bo_ref, bd_ref, ga_ref, sa_ref, gm_ref, sm_ref)):
        vec[16 + k : 17 + k, 0:128] = placed(ref, 128, s * 16)
    wide = placed(bq_ref, 384, s * 48)
    for k in range(3):
        vec[22 + k : 23 + k, 0:128] = wide[:, 128 * k : 128 * (k + 1)]
    vec[25:26, 0:128] = placed(bu_ref, 128, b_me % 2 * 64)
    SA[s] = vec[16:32, 0:128].astype(BF16)
    sm = [copies.start(SA.at[s], SA.at[s], shifted(y=dy, c=dc)) for dy, dc in SEQ_PEERS]

    def seq_one(src, dst):
        own = dst.at[y, c]
        return [copies.start(src, own, shifted(y=d)) for d in (1, -1)] + [
            copies.start(src, own, shifted(c=1))
        ]

    def seq_two(sent, dst):
        more = []
        for cp, d in zip(sent[:2], (1, -1)):
            cp.wait_recv()
            got = dst.at[moved(y, -d), c]
            more.append(copies.start(got, got, shifted(c=1)))
        up_way = c == 0
        got = dst.at[jnp.where(up_way, moved(y, -1), moved(y, 1)), c]
        py = jnp.where(up_way, moved(y, 1), moved(y, -1))
        fwd = copies.start(got, got, (b_me, py * 2 + c))
        sent[2].wait_recv()
        return more, fwd

    def seq_three(more, fwd, dst):
        fwd.wait_recv()
        got = dst.at[moved(y, 2), c]
        return more + [copies.start(got, got, shifted(c=1))]

    xs = seq_one(x_ref, X)
    angle = pos_ref[...].astype(F32) * freq_ref[...]
    RA[s, 0:16, :] = jnp.cos(angle)
    RA[s, 16:32, :] = jnp.sin(angle)
    ra = [copies.start(RA.at[s], RA.at[s], shifted(y=dy, c=dc)) for dy, dc in SEQ_PEERS]
    for cp in up_loads:
        cp.wait()
    lane = lax.broadcasted_iota(jnp.int32, (16, 128), 1)
    for k in range(8):
        for p in range(8):
            at = (8 * p + k // 2) * 128
            r, at = 16 * (at // C), at % C
            one = F2[0, 0, r : r + 16, at : at + 128].astype(F32)
            two = F2[0, 0, r : r + 16, at + 512 : at + 640].astype(F32)
            if k % 2 == 0:
                two = pltpu.roll(two, 64, 1)
            else:
                one = pltpu.roll(one, 64, 1)
            ACT[16 * k : 16 * (k + 1), 128 * p : 128 * (p + 1)] = jnp.where(lane < 64, one, two).astype(BF16)
    up = across(ACT, 1024, UP.at[x, z, rows16])

    for cp in qk:
        cp.wait_recv()
    qa = Gather(copies, QK, "x", (0, 48))
    qb = Gather(copies, QK, "z", (48, 80))
    qa.one()
    qb.one()

    @pl.when(differs)
    def _():
        out_copy.wait()

    @pl.when(jnp.logical_not(differs))
    def _():
        out_load.wait()

    wo = Gather(copies, WO, "x")
    wo.one()
    for cp in sm:
        cp.wait_recv()
    total = SA[0].astype(F32)
    for k in range(1, 8):
        total += SA[k].astype(F32)
    row = lax.broadcasted_iota(jnp.int32, (16, 128), 0)
    SM[x, z] = jnp.where(row == 9, SA[s].astype(F32), total).astype(BF16)
    small = Gather(copies, SM, "z")
    small.one()
    g_load.wait()
    total = jnp.zeros((1, C), F32)
    for k in range(8):
        total += jnp.sum(G[y, c, 16 * k : 16 * (k + 1)].astype(F32), 0, keepdims=True)
    gsum[...] = total
    qa.two()
    qb.two()
    small.two()
    wo.two()
    xs2, xf = seq_two(xs, X)
    gs = seq_one(g_ref, G)
    small.three()
    qa.three()
    qb.three()
    for cp in up:
        cp.wait_recv()
    upg = [Gather(copies, UP, "x", (0, 64)), Gather(copies, UP, "z", (64, 64))]
    for g in upg:
        g.one()
    wo.three()
    down_load.wait()
    for g in down:
        g.two()
    small.done()
    for i in range(4):
        for j in range(4):
            b = i * 4 + j
            tile = SM[i, j].astype(F32)
            vec[0:6, b * 128 : (b + 1) * 128] = tile[0:6]
            for k in range(3):
                BQ[3 * b + k : 3 * b + k + 1, :] = tile[6 + k : 7 + k]
            if b % 2 == 0:
                kept = tile[9:10]
            else:
                vec[6:7, b // 2 * 128 : (b // 2 + 1) * 128] = kept + tile[9:10]

    def norm(ky, kc):
        def step(t, _):
            r = pl.ds(pl.multiple_of(t * 16, 16), 16)
            v = X[ky, kc, r].astype(F32)
            v = v - jnp.mean(v, -1, keepdims=True)
            n = v * lax.rsqrt(jnp.mean(v * v, -1, keepdims=True) + EPS)
            NB[ky * 2 + kc, r] = n.astype(BF16)
            F1[ky, kc, r] = (n * vec[2:3, :] + vec[3:4, :]).astype(BF16)
            F2[ky, 2 * kc + t // 4, pl.ds(pl.multiple_of(t % 4 * 16, 16), 16)] = (
                n * vec[4:5, :] + vec[5:6, :]
            ).astype(BF16)
            return 0

        lax.fori_loop(0, 8, step, 0)

    x_load.wait()
    norm(y, c)
    norm(y, 1 - c)
    norm(moved(y, -1), c)
    norm(moved(y, 1), c)
    xs3 = seq_three(xs2, xf, X)
    xs3[0].wait_recv()
    norm(moved(y, -1), 1 - c)
    xs3[1].wait_recv()
    norm(moved(y, 1), 1 - c)
    gs2, gf = seq_two(gs, G)
    norm(moved(y, 2), c)
    xs3[2].wait_recv()
    norm(moved(y, 2), 1 - c)
    for cp in ra:
        cp.wait_recv()

    lane = lax.broadcasted_iota(jnp.int32, (128, 128), 1)
    for k in range(8):
        r = pl.ds(k * 128, 128)
        tile = jnp.concatenate([RA[k], jnp.zeros((96, 128), F32)], 0).T
        TC[r] = jnp.where(lane < 16, tile, jnp.where(lane < 32, pltpu.roll(tile, 16, 1), 1.0))
        TA[r] = jnp.where(lane < 16, -pltpu.roll(tile, 112, 1), 0.0)
        TB[r] = jnp.where((lane >= 16) & (lane < 32), tile, 0.0)
    for gth in (qa, qb):
        gth.done()
    for part in range(3):
        pair = BQ[pl.ds(part * 16 + s * 2, 2), :]
        for k in range(2):
            at = part * 256 + k * 128
            vec[9:10, at : at + 128] = pair[k : k + 1]

    def first(i, _):
        project(i, F1, QK, vec.at[9:10, 0:768], TC, TA, TB, PP)
        return 0

    lax.fori_loop(0, 4, first, 0)
    for g in upg:
        g.two()
    gs3 = seq_three(gs2, gf, G)
    wo.done()
    for cp in gs3:
        cp.wait_recv()

    def mixed(i, _):
        total = dot(G[i].reshape(256, C), WO[...].reshape(256, C), 1, 1)
        PP[pl.ds(2 * i, 2), :, U_AT:L_AT] = total.astype(BF16).reshape(2, 128, 256)
        return 0

    lax.fori_loop(0, 4, mixed, 0)
    for g in down:
        g.three()
    for h in range(2):
        head_pass(h, PP, DK, DV, TC, TA, TB, gbq)
    for g in upg:
        g.three()

    def grad_out(j, _):
        q = pl.ds(pl.multiple_of(j * 1024, 1024), 1024)
        mix = PP[:, :, M_AT:].reshape(1024, 256)
        GO[:, :, :, q] = dot(mix, G[:, :, :, q].reshape(1024, 1024), 0, 0).astype(BF16).reshape(4, 4, 16, 1024)
        return 0

    lax.fori_loop(0, 2, grad_out, 0)

    def grad_qkv(i, _):
        r = pl.ds(pl.multiple_of(i * 512, 512), 512)
        right = PP[:, :, L_AT:M_AT].reshape(1024, 768)
        GQ[i] = dot(F1[:, :, :, r].reshape(1024, 512), right, 0, 0).astype(BF16).reshape(4, 128, 768)
        return 0

    lax.fori_loop(0, 4, grad_qkv, 0)
    sent(xs + xs2 + [xf, xs3[2]])

    def attend(t, _):
        i, j = t // 2, t % 2
        q = pl.ds(pl.multiple_of(j * 1024, 1024), 1024)
        mix = PP[pl.ds(4 * i, 4), :, M_AT:].reshape(512, 256)
        total = dot(mix, WO[:, :, :, q].reshape(256, 1024))
        X[pl.ds(2 * i, 2), :, :, q] = total.astype(BF16).reshape(2, 2, 128, 1024)
        return 0

    lax.fori_loop(0, 4, attend, 0)
    vec[10:12, :] = jnp.zeros((2, C), F32)

    def grad_first(t, _):
        i, j = t // 4, t % 4
        q = pl.ds(pl.multiple_of(j * 512, 512), 512)
        left = PP[pl.ds(2 * i, 2), :, L_AT:M_AT].reshape(256, 768)
        u = dot(left, QK[j].reshape(512, 768), 1, 1)
        n = NB[pl.ds(2 * i, 2), :, q].reshape(256, 512).astype(F32)
        vec[10:11, q] += jnp.sum(u * n, 0, keepdims=True)
        vec[11:12, q] += jnp.sum(u, 0, keepdims=True)
        F1[i, :, :, q] = (u * vec[2:3, q]).astype(BF16).reshape(2, 128, 512)
        return 0

    lax.fori_loop(0, 16, grad_first, 0)

    for g in (qa, qb, wo):
        sent(g.all)
    sent(qk + up)
    tell(0, xz_peers)
    tell(4, y_peers)

    sa = Scatter(copies, GQ, QK, "x", (0, 48))
    sb = Scatter(copies, GQ, QK, "z", (48, 80))
    so = Scatter(copies, GO, WO, "x")
    fp = SeqScatter(copies, X, PP)
    fq = SeqScatter(copies, F1, NB)
    gbu[...] = jnp.zeros_like(gbu)
    hear(0, xz_peers)
    for g in (sa, sb, so):
        g.one()
    for g in down + upg:
        g.done()

    def hidden(t, _):
        i, j = t // 2, t % 2
        r = pl.ds(pl.multiple_of(i * 256, 256), 256)
        q = pl.ds(pl.multiple_of(j * 512, 512), 512)
        h = dot(F2[i].reshape(256, C), UP[:, :, :, q].reshape(C, 512)) + vec[6:7, q]
        ga = dot(G[i].reshape(256, C), DN[pl.ds(2 * j, 2)].reshape(512, C), 1, 1)
        cdf = 0.5 + 0.5 * lax.erf(h * (0.5**0.5))
        ACT[r, q] = (h * cdf).astype(BF16)
        gh = ga * (cdf + h * (jnp.exp(h * h * -0.5) * 0.3989422804014327))
        gbu[:, q] += jnp.sum(gh, 0, keepdims=True)
        GHL[r, q] = gh.astype(BF16)
        return 0

    lax.fori_loop(0, 8, hidden, 0)
    for g in (sa, sb, so):
        g.mid()

    GD = F2
    sd = [Scatter(copies, GD, DN, "x", (0, 32)), Scatter(copies, GD, DN, "z", (32, 32))]
    su = [Scatter(copies, GU, SP, "x", (0, 64), 1024), Scatter(copies, GU, SP, "z", (64, 64), 1024)]
    sc = Scatter(copies, CT, CP, "z")
    def grad_up(t, _):
        i, j = t // 2, t % 2
        r = pl.ds(pl.multiple_of(i * 512, 512), 512)
        q = pl.ds(pl.multiple_of(j * 512, 512), 512)
        left = F2[:, :, :, r].reshape(1024, 512)
        GU[i, :, :, q] = dot(left, GHL[:, q], 0, 0).astype(BF16).reshape(4, 128, 512)
        return 0

    lax.fori_loop(0, 8, grad_up, 0)
    for g in su:
        g.one()

    vec[12:14, :] = jnp.zeros((2, C), F32)

    def second(t, _):
        i, j = t // 4, t % 4
        r = pl.ds(pl.multiple_of(i * 256, 256), 256)
        q = pl.ds(pl.multiple_of(j * 512, 512), 512)
        u = dot(GHL[r], UP[j].reshape(512, 1024), 1, 1)
        n = NB[pl.ds(2 * i, 2), :, q].reshape(256, 512).astype(F32)
        vec[12:13, q] += jnp.sum(u * n, 0, keepdims=True)
        vec[13:14, q] += jnp.sum(u, 0, keepdims=True)
        total = u * vec[4:5, q] + F1[i, :, :, q].reshape(256, 512).astype(F32)
        F1[i, :, :, q] = total.astype(BF16).reshape(2, 128, 512)
        return 0

    lax.fori_loop(0, 16, second, 0)
    tell(3, y_peers)
    for g in (sa, sb, so):
        g.two()
    hear(3, y_peers)
    fq.one()

    def feed(t, _):
        i, j = t // 4, t % 4
        r = pl.ds(pl.multiple_of(i * 512, 512), 512)
        q = pl.ds(pl.multiple_of(j * 512, 512), 512)
        two = pl.ds(2 * i, 2)
        total = dot(ACT[r], DN[:, :, :, q].reshape(1024, 512)) + X[two, :, :, q].reshape(512, 512).astype(F32)
        X[two, :, :, q] = total.astype(BF16).reshape(2, 2, 128, 512)
        return 0

    lax.fori_loop(0, 8, feed, 0)
    for g in down:
        sent(g.all)
    tell(1, xz_peers)
    hear(4, y_peers)
    fp.one()
    for g in su:
        g.mid()

    def grad_down(t, _):
        i, j = t // 2, t % 2
        u = pl.ds(pl.multiple_of(i * 256, 256), 256)
        q = pl.ds(pl.multiple_of(j * 1024, 1024), 1024)
        right = G[:, :, :, q].reshape(1024, 1024)
        GD[i, :, :, q] = dot(ACT[:, u], right, 0, 0).astype(BF16).reshape(4, 64, 1024)
        return 0

    lax.fori_loop(0, 8, grad_down, 0)
    hear(1, xz_peers)
    for g in sd:
        g.one()
    fq.two()
    sent(gs3 + [gf])
    again = [local.start(x_ref, G.at[0, 0]), local.start(g_ref, G.at[0, 1])]

    BQ[...] = jnp.zeros_like(BQ)
    for part in range(3):
        for k in range(2):
            at = part * 256 + k * 128
            BQ[pl.ds(part * 16 + s * 2 + k, 1), :] = gbq[:, at : at + 128]
    for b in range(16):
        at = b * 128
        VT[b, 0:1, :] = gsum[:, at : at + 128]
        VT[b, 1:5, :] = vec[10:14, at : at + 128]
        VT[b, 5:8, :] = BQ[3 * b : 3 * b + 3, :]
    vs = [
        copies.start(VT, v_land.at[k], shifted(y=dy, c=dc)) for k, (dy, dc) in enumerate(SEQ_PEERS)
    ]
    fq.mid()
    fp.two()

    for cp in vs:
        cp.wait_recv()
    for b in range(16):
        total = VT[b]
        for k in range(7):
            total += v_land[k, b]
        CT[b // 4, b % 4, 0:8, :] = total
        CT[b // 4, b % 4, 8:9, :] = gbu[:, b // 2 * 128 : b // 2 * 128 + 128]
        CT[b // 4, b % 4, 9:16, :] = jnp.zeros((7, 128), F32)
    sc.one()

    def store(ref, base=0):
        def put(r, total):
            ref[pl.ds(base + r.start, r.size)] = total.astype(ref.dtype)

        return put

    gu_part = ACT.at[pl.ds(0, 128)]
    gq_part = ACT.at[pl.ds(128, 128), pl.ds(0, 768)]

    def spread(part, out):
        out[s] = part[pl.ds(pl.multiple_of(s * 16, 16), 16)]
        made = []
        for dy, dc in SEQ_PEERS:
            peer = moved(y, dy) * 2 + lax.rem(c + dc, 2)
            made.append(
                copies.start(
                    part.at[pl.ds(pl.multiple_of(peer * 16, 16), 16)], out.at[s], shifted(y=dy, c=dc)
                )
            )
        return made

    sa.three(store(gq_part))
    sb.three(store(gq_part, 48))
    backs = spread(gq_part, gq_all)
    so.three(store(go_part))
    out_back = copies.make(go_part, go_all, source)

    @pl.when(differs)
    def _():
        out_back.start()

    @pl.when(jnp.logical_not(differs))
    def _():
        go_all[...] = go_part[...]

    for g in sd:
        g.mid()
    sc.mid()
    for g in su:
        g.two()
    fp.mid()
    for cp in again:
        cp.wait()

    def grad_in(r, total):
        v = G[0, 0, r].astype(F32)
        v = v - jnp.mean(v, -1, keepdims=True)
        inv = lax.rsqrt(jnp.mean(v * v, -1, keepdims=True) + EPS)
        n = v * inv
        total = total - jnp.mean(total, -1, keepdims=True) - n * jnp.mean(total * n, -1, keepdims=True)
        x_out[r] = (G[0, 1, r].astype(F32) + total * inv).astype(BF16)

    fq.three(grad_in)
    sc.two()
    for k, g in enumerate(su):
        g.three(store(gu_part, 64 * k))
    backs += spread(gu_part, gu_all)
    for g in sd:
        g.two()

    def layer_out(r, total):
        bias = vec[0:1, :] + vec[1:2, :]
        y_out[r] = (G[0, 0, r].astype(F32) + total + bias).astype(BF16)

    fp.three(layer_out)
    sc.three(store(sv))
    for k, g in enumerate(sd):
        g.three(store(gd_out, 32 * k))

    @pl.when(differs)
    def _():
        out_back.wait()

    for cp in backs:
        cp.wait_recv()
    copies.drain()


def layer(x, g, pos, freq, vectors, up, qkv, down, out):
    any_ = pl.BlockSpec(memory_space=pl.ANY)
    vm = pl.BlockSpec(memory_space=pltpu.VMEM)
    n_up, n_qkv = up.shape[-1] // 8, qkv.shape[-1] // 8
    up_all, qk_all = (4, 4, 128, n_up), (4, 4, 128, n_qkv)
    dn_all, wo_all = (4, 4) + down.shape, (4, 4) + out.shape
    blocks, unit = (4, 2, 128, C), (1024, n_up)
    S = pltpu.VMEM
    scratch = [
        (blocks, BF16), (blocks, BF16), ((8, 16, 128), BF16), ((8, 32, 128), F32), ((4, 4, 16, 128), BF16),
        (up_all, BF16), (qk_all, BF16), (dn_all, BF16), (wo_all, BF16),
        (blocks, BF16), ((4, 4, 64, C), BF16), ((8, 128, C), BF16), (unit, BF16), (unit, BF16),
        (qk_all, BF16), (wo_all, BF16), (blocks, BF16), (up_all, BF16), ((8, 128, C), BF16),
        ((1024, HD), F32), ((1024, HD), F32), ((1024, HD), F32), ((1024, HD), F32), ((1024, HD), F32),
        ((48, 128), F32), ((16, 8, 128), F32), ((7, 16, 8, 128), F32), ((4, 4, 16, 128), F32), ((4, 4, 16, 128), F32),
        ((32, C), F32), ((1, C), F32), ((1, n_up), F32), ((1, n_qkv), F32),
        (out.shape, BF16),
    ]
    outs = [
        (x.shape, BF16), (x.shape, BF16), (down.shape, F32),
        ((8, 16, n_up), BF16), ((8, 16, n_qkv), BF16), (out.shape, BF16), ((16, 128), F32),
    ]
    return pl.pallas_call(
        layer_kernel,
        out_shape=[jax.ShapeDtypeStruct(*o) for o in outs],
        in_specs=[any_, any_] + [vm] * 10 + [any_] * 4,
        out_specs=[vm] * 7,
        scratch_shapes=[S(*h) for h in scratch]
        + [pltpu.SemaphoreType.DMA((230,)), pltpu.SemaphoreType.DMA((230,)), pltpu.SemaphoreType.REGULAR((5,)), pltpu.SemaphoreType.DMA((16,))],
        compiler_params=pltpu.CompilerParams(
            collective_id=1, has_side_effects=True, vmem_limit_bytes=64 * 2**20 - 2**16
        ),
    )(x, g, pos, freq, *vectors, up, qkv, down, out)


def finish_kernel(y_in, x_in, gd_in, gu_in, gq_in, go_in, sv,
                  y_out, x_out, gd, gu, gq, go, b_out, b_down, ga, sa, gm, sm, bq, bu):
    s = lax.axis_index("seq")
    b = lax.axis_index("batch")
    y_out[...] = y_in[...]
    x_out[...] = x_in[...]
    gd[...] = gd_in[...]
    go[...] = go_in[...].astype(F32)
    for k in range(8):
        for part in range(3):
            piece = gq_in[k, :, 256 * part : 256 * (part + 1)]
            gq[:, C * part + 256 * k : C * part + 256 * (k + 1)] = piece.astype(F32)
    lane = lax.broadcasted_iota(jnp.int32, (16, 128), 1)
    for j in range(4):
        for p in range(8):
            one = gu_in[2 * j, :, 128 * p : 128 * (p + 1)].astype(F32)
            two = gu_in[2 * j + 1, :, 128 * p : 128 * (p + 1)].astype(F32)
            at = (8 * p + j) * 128
            gu[:, at : at + 128] = jnp.where(lane < 64, one, pltpu.roll(two, 64, 1))
            gu[:, at + 512 : at + 640] = jnp.where(lane < 64, pltpu.roll(one, 64, 1), two)
    mine = pltpu.roll(sv[...], lax.rem(128 - s * 16, 128), 1)
    for k, ref in enumerate((b_out, ga, sa, gm, sm)):
        ref[...] = mine[k : k + 1, 0:16]
    b_down[...] = mine[0:1, 0:16]
    wide = jnp.concatenate([jnp.broadcast_to(sv[k : k + 1, :], (8, 128)) for k in (5, 6, 7)], 1)
    bq[...] = pltpu.roll(wide, lax.rem(384 - s * 48, 384), 1)[0:1, 0:48]
    tail = pltpu.roll(sv[8:16, :], lax.rem(b, 2) * 64, 1)
    bu[...] = tail[0:1, 0:64]


def finish(*parts):
    vm = pl.BlockSpec(memory_space=pltpu.VMEM)
    y, xg, gd, gu, gq, go, _ = parts
    outs = [(y.shape, BF16), (xg.shape, BF16), (gd.shape, F32), ((16, 8 * gu.shape[-1]), F32), ((16, 8 * gq.shape[-1]), F32), (go.shape, F32)]
    outs += [((1, 16), F32)] * 6 + [((1, 48), F32), ((1, 64), F32)]
    return pl.pallas_call(
        finish_kernel,
        out_shape=[jax.ShapeDtypeStruct(*o) for o in outs],
        in_specs=[vm] * 7,
        out_specs=[vm] * len(outs),
    )(*parts)


def shards(
    inputs,
    positions,
    w_qkv,
    b_qkv,
    w_out,
    b_out,
    w_up,
    b_up,
    w_down,
    b_down,
    gain_attn,
    shift_attn,
    gain_mlp,
    shift_mlp,
    grad_out,
):
    half_rot = ROT // 2
    exponent = jnp.arange(half_rot).astype(F32) / half_rot
    frequency = jnp.broadcast_to(jnp.power(10000.0, -exponent)[:, None], (half_rot, 128))
    vectors = [
        v[None] for v in (b_out, b_down, gain_attn, shift_attn, gain_mlp, shift_mlp, b_qkv, b_up)
    ]
    parts = layer(inputs[0], grad_out[0], positions, frequency, vectors, w_up, w_qkv, w_down, w_out)
    layer_out, grad_in, g_down, g_up, g_qkv, g_out, *rest = finish(*parts)
    g_b_out, g_b_down, g_gain_a, g_shift_a, g_gain_m, g_shift_m, g_b_qkv, g_b_up = [v[0] for v in rest]
    return (
        layer_out[None],
        grad_in[None],
        g_qkv,
        g_b_qkv,
        g_out,
        g_b_out,
        g_up,
        g_b_up,
        g_down,
        g_b_down,
        g_gain_a,
        g_shift_a,
        g_gain_m,
        g_shift_m,
    )


def solution(mesh):
    both = ("batch", "seq")
    rows = P("batch", "seq", None)
    matrix = P(both, None)
    vector = P(both)
    return jax.shard_map(
        shards,
        mesh=mesh,
        in_specs=(
            rows,
            P("batch", "seq"),
            matrix,
            vector,
            matrix,
            vector,
            matrix,
            vector,
            matrix,
            vector,
            vector,
            vector,
            vector,
            vector,
            rows,
        ),
        out_specs=(
            rows,
            rows,
            matrix,
            vector,
            matrix,
            vector,
            matrix,
            vector,
            matrix,
            vector,
            vector,
            vector,
            vector,
            vector,
        ),
        check_vma=False,
    )
```
